32 devices in a mesh: parts: 2 (over y), att: 4 (over x, core), ffn: 4 (over z).
Axes of the slice: x: 2, y: 2, z: 4, core: 2. Of those that a mesh axis runs over, the one named last changes fastest.
Arguments:
- incoming: bfloat16 [128, 2, 8192], P('parts', None, 'att'), parts along dimension 0, may hold values from -60 to 60
- queries: bfloat16 [128, 2, 8192], P(('parts', 'att'), None, 'ffn'), parts along dimension 0, may hold values from -19 to 19
- new_kv: bfloat16 [128, 2, 2048], P(('parts', 'att'), None, 'ffn'), parts along dimension 0, may hold values from -6 to 6
- cache: bfloat16 [128, 640, 2048], P(('parts', 'att'), None, 'ffn'), parts along dimension 0, may hold values from -6 to 6
- lengths: int32 [128], P(('parts', 'att')), parts along dimension 0, may hold values from 1 to 640, 20480 in all
- slot_of: int32 [128], P('parts'), parts along dimension 0, may hold values from 0 to 63, each once
- w_out: bfloat16 [8192, 8192], P('ffn', 'att'), may hold values from -0.0625 to 0.0625
- norm_gain: float32 [8192], P('att'), may hold values from 0.5 to 1.5
- w_gate: bfloat16 [8192, 14336], P('att', 'ffn'), may hold values from -0.0625 to 0.0625
- w_up: bfloat16 [8192, 14336], P('att', 'ffn'), may hold values from -0.0625 to 0.0625
- w_down: bfloat16 [14336, 8192], P('ffn', 'att'), may hold values from -0.046875 to 0.046875
Outputs:
- out: bfloat16 [128, 2, 8192], P(('parts', 'ffn'), None, 'att'), parts along dimension 0
The draws below stay inside these ranges and needn't reach their ends.
There are 2 independent parts, one for each index of `parts`. The reference program is written for one: setup_inputs(seed, part) draws one part's arguments, and reference() takes and returns one part's arrays. A program takes and returns all parts, laid end to end along the dimension named above; an argument that names none is the same for every part. Nothing has to cross between parts.
Inputs may be any that keep to these rules, and one draw needn't show every extreme that they name: In each part, the kept lengths of that part's 64 slots sum to 20480. `slot_of`: in each part, every slot holds exactly one request.
All inputs are finite; a program needn't handle non-finite values. No bound on the sum of `lengths` on one device may be relied on, other than what follows from the above.
Results may differ from the reference program's by a relative error of at most 0.0095.
Values may be sent and summed in bfloat16 or wider, within the bound.
No kernel may reach another device: no remote copies, remote signals or barrier semaphores. Data moves between devices by JAX's collectives and lax.ppermute only.
A program may use at most 128 MiB of HBM per device.

```python
import math
import jax
import jax.numpy as jnp
import numpy as np
from jax import lax

D = 8192
FF = 14336
H = 64
KVH = 8
HD = 128
STEPS = 2
CAP = 640
REQ = 64


def draw_incoming(key, part):
    column = jnp.arange(D, dtype=jnp.float32) / D
    background = jnp.clip(jax.random.normal(key, (REQ, STEPS, D), jnp.float32), -6.0, 6.0)
    return (background * 3.0 ** column).astype(jnp.bfloat16)


def draw_queries(key, part):
    return jnp.clip(jax.random.normal(key, (REQ, STEPS, H * HD), jnp.float32), -6.0, 6.0).astype(jnp.bfloat16)


def draw_cache(key, part):
    return jnp.clip(jax.random.normal(key, (REQ, CAP, KVH * 2 * HD), jnp.float32), -6.0, 6.0).astype(jnp.bfloat16)


def steps_of(rng, extent, pieces, least, largest):
    level, own = 1.0, jax.random.fold_in(rng, 6)
    for axis_at, blocks in pieces:
        heights = jnp.exp(jax.random.uniform(jax.random.fold_in(own, axis_at), (blocks,), jnp.float32, least / len(pieces), largest / len(pieces)))
        level = level * jnp.repeat(heights, extent[axis_at] // blocks).reshape([-1 if axis == axis_at else 1 for axis in range(len(extent))])
    return level


def length_profile(number_of, total, reach, skew):
    loads = [(1 << 20) // math.isqrt(grade ** skew) + 1 for grade in range(2, number_of + 1)]
    rest, counts = total - reach - (number_of - 1), [1] * (number_of - 1)
    while rest > 0:
        candidates = [i for i in range(number_of - 1) if counts[i] < reach]
        mass, left = sum([loads[i] for i in candidates]), rest
        for i in candidates:
            addition = min(reach - counts[i], max(1, left * loads[i] // mass), rest)
            counts[i] = counts[i] + addition
            rest = rest - addition
    return np.array([reach] + counts)


def ragged(rng, amount, total, most, slope):
    if amount == 2:
        one = jax.random.randint(rng, (), max(1, total - most), min(most, total - 1) + 1)
        return jnp.stack([one, total - one])
    tallies = jnp.asarray(length_profile(amount, total, most, slope), jnp.int32)
    pairs = (amount - 1) // 2
    source_of, receiver = tallies[1:1 + 2 * pairs:2], tallies[2:2 + 2 * pairs:2]
    margin = jnp.minimum(source_of - 1, most - receiver)
    moved = jax.random.randint(jax.random.fold_in(rng, 1), (pairs,), 0, 1 << 20) % (margin + 1)
    tallies = tallies.at[1:1 + 2 * pairs:2].set(source_of - moved).at[2:2 + 2 * pairs:2].set(receiver + moved)
    return tallies[jax.random.permutation(jax.random.fold_in(rng, 2), amount)]


def scatter_about(stream_key, shape, width, limit, shards=(), kind=jnp.bfloat16):
    values = width * jax.random.normal(stream_key, shape, jnp.float32)
    if shards:
        values = values * steps_of(stream_key, shape, shards, -0.22, 0.18)
    return jnp.clip(values, -limit, limit).astype(kind)


def setup_inputs(seed: int = 0, part: int = 0) -> dict:
    streams_of = jax.random.split(jax.random.key(seed), 12)
    part_keys = jax.random.split(jax.random.fold_in(streams_of[11], part), 12)
    incoming = draw_incoming(jax.random.fold_in(jax.random.fold_in(streams_of[11], part), 71), part)
    queries = draw_queries(jax.random.fold_in(jax.random.fold_in(streams_of[11], part), 71), part)
    new_kv = scatter_about(part_keys[2], (REQ, STEPS, KVH * 2 * HD), 1.0, 6.0, ((0, 4), (2, 4)))
    cache = draw_cache(jax.random.fold_in(jax.random.fold_in(streams_of[11], part), 71), part)
    lengths = ragged(part_keys[4], REQ, REQ * CAP // 2, CAP, 2).astype(jnp.int32)
    slot_of = jax.random.permutation(part_keys[5], REQ).astype(jnp.int32)
    w_out = scatter_about(streams_of[6], (H * HD, D), (H * HD) ** -0.5, 0.0625, ((0, 4), (1, 4)))
    norm_gain = jnp.clip(1.0 + 0.1 * jax.random.normal(streams_of[7], (D,), jnp.float32), 0.5, 1.5)
    w_gate = scatter_about(streams_of[8], (D, FF), D ** -0.5, 0.0625, ((0, 4), (1, 4)))
    w_up = scatter_about(streams_of[9], (D, FF), D ** -0.5, 0.0625, ((0, 4), (1, 4)))
    w_down = scatter_about(streams_of[10], (FF, D), FF ** -0.5, 0.046875, ((0, 4), (1, 4)))
    return {"incoming": incoming, "queries": queries, "new_kv": new_kv, "cache": cache, "lengths": lengths, "slot_of": slot_of, "w_out": w_out, "norm_gain": norm_gain, "w_gate": w_gate, "w_up": w_up, "w_down": w_down}


epsilon = 1e-05

def attend_request(query_rows, fresh_rows, kept_rows, length):
    groups = H // KVH
    score_scale = HD ** (-0.5)
    query_wide = query_rows.astype(jnp.float32).reshape(STEPS, KVH, groups, HD)
    kept_wide = kept_rows.astype(jnp.float32).reshape(CAP, KVH, 2, HD)
    fresh_wide = fresh_rows.astype(jnp.float32).reshape(STEPS, KVH, 2, HD)
    kept_scores = jnp.einsum('skgd,ckd->skgc', query_wide, kept_wide[:, :, 0]) * score_scale
    in_range = jnp.arange(CAP) < length
    kept_scores = jnp.where(in_range, kept_scores, -jnp.inf)
    fresh_scores = jnp.einsum('skgd,tkd->skgt', query_wide, fresh_wide[:, :, 0]) * score_scale
    causal = jnp.arange(STEPS)[None, :] <= jnp.arange(STEPS)[:, None]
    fresh_scores = jnp.where(causal[:, None, None, :], fresh_scores, -jnp.inf)
    top_score = jnp.maximum(lax.optimization_barrier(jnp.max(kept_scores, -1)), lax.optimization_barrier(jnp.max(fresh_scores, -1)))
    kept_exp = jnp.exp(kept_scores - top_score[..., None])
    fresh_exp = jnp.exp(fresh_scores - top_score[..., None])
    denominator = lax.optimization_barrier(jnp.sum(kept_exp, -1)) + lax.optimization_barrier(jnp.sum(fresh_exp, -1))
    kept_prob = (kept_exp / denominator[..., None]).astype(jnp.bfloat16)
    fresh_prob = (fresh_exp / denominator[..., None]).astype(jnp.bfloat16)
    mixture = jnp.einsum('skgc,ckd->skgd', kept_prob.astype(jnp.float32), kept_wide[:, :, 1])
    mixture = mixture + jnp.einsum('skgt,tkd->skgd', fresh_prob.astype(jnp.float32), fresh_wide[:, :, 1])
    return mixture.astype(jnp.bfloat16).reshape(STEPS, H * HD)

def reference(incoming, queries, new_kv, cache, lengths, slot_of, w_out, norm_gain, w_gate, w_up, w_down):

    def attend_one(request):
        slot_index = slot_of[request]
        return attend_request(queries[request], new_kv[request], cache[slot_index], lengths[slot_index])
    attended = lax.map(attend_one, jnp.arange(REQ, dtype=jnp.int32))
    flattened = attended.reshape(REQ * STEPS, H * HD)
    heads_out = jnp.dot(flattened, w_out, preferred_element_type=jnp.float32)
    residual = (incoming.reshape(REQ * STEPS, D).astype(jnp.float32) + heads_out).astype(jnp.bfloat16)
    residual_wide = residual.astype(jnp.float32)
    squares = lax.optimization_barrier(jnp.sum(residual_wide * residual_wide, -1, keepdims=True))
    normed = (residual_wide * lax.rsqrt(squares / D + epsilon) * norm_gain.astype(jnp.float32)).astype(jnp.bfloat16)
    gate = jnp.dot(normed, w_gate, preferred_element_type=jnp.float32)
    upward = jnp.dot(normed, w_up, preferred_element_type=jnp.float32)
    hidden = (jax.nn.silu(gate) * upward).astype(jnp.bfloat16)
    lowered = jnp.dot(hidden, w_down, preferred_element_type=jnp.float32)
    return (residual_wide + lowered).astype(jnp.bfloat16).reshape(REQ, STEPS, D)
```

```python
import functools

import jax
import jax.numpy as jnp
from jax import lax
from jax.experimental import pallas as pl
from jax.experimental.pallas import tpu as pltpu
from jax.sharding import PartitionSpec as P

H = 64
KVH = 8
HD = 128
STEPS = 2
GROUPS = H // KVH
EPSILON = 1e-05
PIECE = 128
FRESH = 16
BLOCK = 256
CHUNKS = 2
F32 = jnp.float32
BF16 = jnp.bfloat16
MIB = 1024 * 1024


def dot(a, b):
    return jnp.dot(a, b, preferred_element_type=F32)


def attend_kernel(lengths, slot_row, qkv, cache, out, kept, qb, mixed, sems):
    slots, cap, width = cache.shape
    kv_local = width // (2 * HD)
    heads = kv_local * GROUPS
    rows = STEPS * heads
    pieces = cap // PIECE
    depth = cap + FRESH

    def piece_copy(i, c):
        part = pl.ds(c * PIECE, PIECE)
        return pltpu.make_async_copy(cache.at[i, part], kept.at[i, part], sems.at[i, c])

    for i in range(slots):
        for c in range(pieces):
            needed = lengths[i] > c * PIECE

            @pl.when(needed)
            def _():
                piece_copy(i, c).start()

            @pl.when(jnp.logical_not(needed))
            def _():
                kept[i, c * PIECE : (c + 1) * PIECE, :] = jnp.zeros((PIECE, width), BF16)

    requests = qkv.shape[0]
    base = lax.axis_index("att") * slots
    wanted = lax.broadcasted_iota(jnp.int32, (slots, requests), 0) + base
    pick = jnp.where(slot_row[...] == wanted, 1.0, 0.0).astype(BF16)
    mine = dot(pick, qkv[...])
    for s in range(STEPS):
        for h in range(heads):
            at = (s * heads + h) * HD
            qb[pl.ds(s * heads + h, slots, stride=rows), :] = mine[:, at : at + HD]
    fresh_at = STEPS * heads * HD
    place = lax.broadcasted_iota(jnp.int32, (FRESH, width), 0)
    for i in range(slots):
        block = jnp.zeros((FRESH, width), F32)
        for t in range(STEPS):
            row = mine[i : i + 1, fresh_at + t * width : fresh_at + (t + 1) * width]
            block = jnp.where(place == t, row, block)
        kept[i, cap:depth, :] = block.astype(BF16)

    key_at = lax.broadcasted_iota(jnp.int32, (rows, depth), 1)
    step_of = lax.broadcasted_iota(jnp.int32, (rows, depth), 0) // heads
    fresh_ok = (key_at >= cap) & (key_at - cap <= step_of)
    group_of = lax.broadcasted_iota(jnp.int32, (rows, HD), 0) % heads // GROUPS
    factor = HD ** (-0.5) * 1.4426950408889634
    together = 4
    for first in range(0, slots, together):
        for i in range(first, first + together):
            for c in range(pieces):

                @pl.when(lengths[i] > c * PIECE)
                def _():
                    piece_copy(i, c).wait()

        for i in range(first, first + together):
            query = qb[i * rows : (i + 1) * rows, :]
            pieces_of_query = []
            for g in range(kv_local):
                pieces_of_query += [jnp.where(group_of == g, query, 0.0), jnp.zeros_like(query)]
            query = jnp.concatenate(pieces_of_query, axis=1).astype(BF16)
            rows_kept = kept[i]
            scores = lax.dot_general(
                query, rows_kept, (((1,), (1,)), ((), ())), preferred_element_type=F32
            )
            scores = jnp.where(fresh_ok | (key_at < lengths[i]), scores, -jnp.inf)
            top = jnp.max(scores, axis=1, keepdims=True)
            weights = jnp.exp2((scores - top) * factor)
            total = jnp.sum(weights, axis=1, keepdims=True)
            values = dot(weights.astype(BF16), rows_kept) / total
            for s in range(STEPS):
                for g in range(kv_local):
                    at = s * heads + g * GROUPS
                    mixed[i * rows + at : i * rows + at + GROUPS, :] = values[
                        at : at + GROUPS, g * 2 * HD + HD : (g + 1) * 2 * HD
                    ]
    for s in range(STEPS):
        for h in range(heads):
            out[s * slots : (s + 1) * slots, h * HD : (h + 1) * HD] = mixed[
                pl.ds(s * heads + h, slots, stride=rows), :
            ].astype(BF16)


def attend(lengths, slot_row, qkv, cache):
    slots, cap, width = cache.shape
    heads = width // (2 * HD) * GROUPS
    rows = STEPS * heads
    vmem = pl.BlockSpec(memory_space=pltpu.VMEM)
    return pl.pallas_call(
        attend_kernel,
        name="attend",
        out_shape=jax.ShapeDtypeStruct((STEPS * slots, heads * HD), BF16),
        in_specs=[
            pl.BlockSpec(memory_space=pltpu.SMEM),
            vmem,
            vmem,
            pl.BlockSpec(memory_space=pl.ANY),
        ],
        out_specs=vmem,
        scratch_shapes=[
            pltpu.VMEM((slots, cap + FRESH, width), BF16),
            pltpu.VMEM((slots * rows, HD), F32),
            pltpu.VMEM((slots * rows, HD), F32),
            pltpu.SemaphoreType.DMA((slots, cap // PIECE)),
        ],
        compiler_params=pltpu.CompilerParams(vmem_limit_bytes=24 * MIB),
        cost_estimate=pl.CostEstimate(
            flops=4 * slots * rows * (cap + FRESH) * width,
            bytes_accessed=slots * cap * width * 2,
            transcendentals=slots * rows * cap,
        ),
    )(lengths, slot_row, qkv, cache)


def project(slot_column, gathered, w, slots):
    rows, depth = gathered.shape
    columns = w.shape[1]
    block = min(512, columns)

    def kernel(slot_column, gathered, w, out, ordered):
        @pl.when(pl.program_id(0) == 0)
        def _():
            wanted = slot_column[...]
            at = lax.broadcasted_iota(jnp.int32, (rows, rows), 1)
            pick = jnp.where(at == wanted, 1.0, 0.0).astype(BF16)
            ordered[...] = dot(pick, gathered[...]).astype(BF16)

        out[...] = dot(ordered[...], w[...]).astype(BF16)

    whole = lambda j: (0, 0)
    return pl.pallas_call(
        kernel,
        name="project",
        grid=(columns // block,),
        out_shape=jax.ShapeDtypeStruct((rows, columns), BF16),
        in_specs=[
            pl.BlockSpec((rows, 1), whole),
            pl.BlockSpec((rows, depth), whole),
            pl.BlockSpec((depth, block), lambda j: (0, j)),
        ],
        out_specs=pl.BlockSpec((rows, block), lambda j: (0, j)),
        scratch_shapes=[pltpu.VMEM((rows, depth), BF16)],
        compiler_params=pltpu.CompilerParams(vmem_limit_bytes=20 * MIB),
        cost_estimate=pl.CostEstimate(
            flops=2 * rows * depth * columns,
            bytes_accessed=2 * depth * columns,
            transcendentals=0,
        ),
    )(slot_column, gathered, w)


def widen(residual, gain, w_gate, w_up, first, count, with_squares):
    rows, depth = residual.shape
    att = lax.axis_size("att")
    chips = att // 2
    share = rows // att
    half = rows // 2
    extra = HD if with_squares else 0
    width = count * 2 * BLOCK + extra

    def kernel(residual, gain, gate, up, keep, send, normed):
        j = pl.program_id(0)

        @pl.when(j == 0)
        def _():
            me = lax.axis_index("att")
            chip, core = me // 2, me % 2
            for side in range(2):
                for d in range(chips):
                    owner = lax.rem(chip + d, chips) * 2 + lax.rem(core + side, 2)
                    part = residual[pl.ds(pl.multiple_of(owner * share, share), share), :].astype(F32)
                    at = side * half + d * share
                    normed[at : at + share, :] = (part * gain[...]).astype(BF16)
                    if with_squares:
                        squares = jnp.sum(part * part, axis=1, keepdims=True)
                        high = squares.astype(BF16).astype(F32)
                        lane = lax.broadcasted_iota(jnp.int32, (share, HD), 1)
                        both = jnp.where(lane == 0, high, squares - high).astype(BF16)
                        target = send if side else keep
                        target[d * share : (d + 1) * share, count * 2 * BLOCK :] = both

        at = pl.multiple_of(j * 2 * BLOCK, 2 * BLOCK)
        for which, w in enumerate((gate, up)):
            product = dot(normed[...], w[...]).astype(BF16)
            here = pl.ds(at + which * BLOCK, BLOCK)
            keep[:, here] = product[:half]
            send[:, here] = product[half:]

    whole = lambda j: (0, 0)
    return pl.pallas_call(
        kernel,
        name="widen",
        grid=(count,),
        out_shape=[jax.ShapeDtypeStruct((half, width), BF16)] * 2,
        in_specs=[
            pl.BlockSpec((rows, depth), whole),
            pl.BlockSpec((1, depth), whole),
            pl.BlockSpec((depth, BLOCK), lambda j: (0, first + j)),
            pl.BlockSpec((depth, BLOCK), lambda j: (0, first + j)),
        ],
        out_specs=[pl.BlockSpec((half, width), whole)] * 2,
        scratch_shapes=[pltpu.VMEM((rows, depth), BF16)],
        compiler_params=pltpu.CompilerParams(vmem_limit_bytes=24 * MIB),
        cost_estimate=pl.CostEstimate(
            flops=4 * rows * depth * count * BLOCK,
            bytes_accessed=4 * depth * count * BLOCK,
            transcendentals=0,
        ),
    )(residual, gain, w_gate, w_up)


def reduce_over_att(keep, send):
    att = lax.axis_size("att")
    chips = att // 2
    share = keep.shape[0] // chips
    arrived = lax.ppermute(send, "att", [(i, i ^ 1) for i in range(att)])
    pair = keep.astype(F32) + arrived.astype(F32)
    total = pair[:share]
    for d in range(1, chips):
        moved = lax.ppermute(
            pair[d * share : (d + 1) * share].astype(BF16),
            "att",
            [(i, (i + 2 * d) % att) for i in range(att)],
        )
        total = total + moved.astype(F32)
    return total


def narrow(hidden, w):
    rows, depth = hidden.shape
    columns = w.shape[1]
    block = min(256, columns)

    def kernel(hidden, w, out):
        out[...] = dot(hidden[...], w[...]).astype(BF16)

    return pl.pallas_call(
        kernel,
        name="narrow",
        grid=(columns // block,),
        out_shape=jax.ShapeDtypeStruct((rows, columns), BF16),
        in_specs=[
            pl.BlockSpec((rows, depth), lambda j: (0, 0)),
            pl.BlockSpec((depth, block), lambda j: (0, j)),
        ],
        out_specs=pl.BlockSpec((rows, block), lambda j: (0, j)),
        compiler_params=pltpu.CompilerParams(vmem_limit_bytes=20 * MIB),
        cost_estimate=pl.CostEstimate(
            flops=2 * rows * depth * columns,
            bytes_accessed=2 * depth * columns,
            transcendentals=0,
        ),
    )(hidden, w)


def sum_rows_over_ffn(partial):
    ffn = lax.axis_size("ffn")
    rows, columns = partial.shape
    pieces = partial.reshape(ffn, rows // ffn, columns)
    pieces = lax.all_to_all(pieces, "ffn", split_axis=0, concat_axis=0, tiled=True)
    return jnp.sum(pieces.astype(F32), axis=0)


def local(
    incoming, queries, new_kv, cache, lengths, slot_of, w_out, norm_gain, w_gate, w_up, w_down
):
    ffn = lax.axis_size("ffn")
    ffn_index = lax.axis_index("ffn")
    att = lax.axis_size("att")
    requests = slot_of.shape[0]
    slots = cache.shape[0]
    model = w_out.shape[1]
    width = w_gate.shape[1]
    owned = requests // ffn

    qkv = jnp.concatenate([queries.reshape(slots, -1), new_kv.reshape(slots, -1)], axis=1)
    qkv = lax.all_gather(qkv, "att", axis=0, tiled=True)
    attended = attend(lengths, slot_of.reshape(1, requests), qkv, cache)
    attended = lax.all_gather(attended, "att", axis=0, tiled=True)

    at_step = (slot_of // slots * (STEPS * slots) + slot_of % slots).reshape(ffn, 1, owned)
    source = at_step + (jnp.arange(STEPS, dtype=jnp.int32) * slots)[None, :, None]
    heads_out = project(source.reshape(STEPS * requests, 1), attended, w_out, slots)
    heads_sum = sum_rows_over_ffn(heads_out)

    own = lax.dynamic_slice_in_dim(incoming, ffn_index * owned, owned, 0)
    own = jnp.swapaxes(own, 0, 1).reshape(STEPS * owned, model)
    residual_own = (own.astype(F32) + heads_sum).astype(BF16)
    residual = lax.all_gather(residual_own, "ffn", axis=0, tiled=True)

    gain = norm_gain.reshape(1, model)
    blocks = width // BLOCK
    edges = [blocks * k // CHUNKS for k in range(CHUNKS + 1)]
    hidden = []
    scale = None
    for first, last in zip(edges[:-1], edges[1:]):
        count = last - first
        keep, send = widen(residual, gain, w_gate, w_up, first, count, first == 0)
        total = reduce_over_att(keep, send)
        if first == 0:
            at = count * 2 * BLOCK
            squares = total[:, at : at + 1] + total[:, at + 1 : at + 2]
            scale = lax.rsqrt(squares / (model * att) + EPSILON)
            total = total[:, :at]
        pairs = (total * scale).reshape(-1, count, 2, BLOCK)
        gated = jax.nn.silu(pairs[:, :, 0]) * pairs[:, :, 1]
        hidden.append(gated.reshape(-1, count * BLOCK).astype(BF16))
    hidden = jnp.concatenate(hidden, axis=1)
    hidden = lax.all_gather(hidden, "att", axis=0, tiled=True)
    lowered = sum_rows_over_ffn(narrow(hidden, w_down))
    out = (residual_own.astype(F32) + lowered).astype(BF16)
    return jnp.swapaxes(out.reshape(STEPS, owned, model), 0, 1)


def solution(mesh):
    return jax.shard_map(
        local,
        mesh=mesh,
        in_specs=(
            P("parts", None, "att"),
            P(("parts", "att"), None, "ffn"),
            P(("parts", "att"), None, "ffn"),
            P(("parts", "att"), None, "ffn"),
            P(("parts", "att")),
            P("parts"),
            P("ffn", "att"),
            P("att"),
            P("att", "ffn"),
            P("att", "ffn"),
            P("ffn", "att"),
        ),
        out_specs=P(("parts", "ffn"), None, "att"),
        check_vma=False,
    )
```

```python
import functools

import jax
import jax.numpy as jnp
from jax import lax
from jax.experimental import pallas as pl
from jax.experimental.pallas import tpu as pltpu
from jax.sharding import PartitionSpec as P

H = 64
KVH = 8
HD = 128
STEPS = 2
GROUPS = H // KVH
EPSILON = 1e-05
BLOCK = 256
CHUNKS = 2
F32 = jnp.float32
BF16 = jnp.bfloat16
MIB = 1024 * 1024


def dot(a, b):
    return jnp.dot(a, b, preferred_element_type=F32)

VMEM = pl.BlockSpec(memory_space=pltpu.VMEM)
ANY = pl.BlockSpec(memory_space=pl.ANY)
SMEM = pl.BlockSpec(memory_space=pltpu.SMEM)
TOKEN = jax.ShapeDtypeStruct((8, HD), F32)


def shift(x, axis, d):
    n = lax.axis_size(axis)
    return lax.ppermute(x, axis, [(i, (i + d) % n) for i in range(n)])


def swap_cores(x):
    return lax.ppermute(x, "att", [(i, i ^ 1) for i in range(lax.axis_size("att"))])


def gather_att(x):
    blocks = [x, swap_cores(x)]
    for d in range(1, lax.axis_size("att") // 2):
        moved = shift(x, "att", 2 * d)
        blocks += [moved, swap_cores(moved)]
    return blocks


def att_source(entry):
    me, chips = lax.axis_index("att"), lax.axis_size("att") // 2
    chip = lax.rem(me // 2 + chips - entry // 2, chips)
    return chip * 2 + lax.rem(me + entry, 2)


def place_blocks(blocks, whole, columns=slice(None)):
    for entry, block in enumerate(blocks):
        rows = block.shape[0]
        at = pl.multiple_of(att_source(entry) * rows, rows)
        whole[pl.ds(at, rows), columns] = block[...]


def load(arrays, after, name):
    count = len(arrays)

    def kernel(*refs):
        sources, targets = refs[:count], refs[count + 1 : 2 * count + 1]
        token, sems = refs[-2:]
        copies = []
        for k in range(count):
            lead = sources[k].shape[0]
            parts = min(8, lead)
            for p in range(parts):
                part = pl.ds(lead * p // parts, lead // parts)
                copies.append(
                    pltpu.make_async_copy(
                        sources[k].at[part], targets[k].at[part], sems.at[k, p]
                    )
                )
        for copy in copies:
            copy.start()
        token[...] = jnp.zeros_like(token)
        for copy in copies:
            copy.wait()

    return pl.pallas_call(
        kernel,
        name=name,
        out_shape=[pltpu.VMEM(x.shape, x.dtype) for x in arrays] + [TOKEN],
        in_specs=[ANY] * count + [VMEM],
        out_specs=[VMEM] * (count + 1),
        scratch_shapes=[pltpu.SemaphoreType.DMA((count, 8))],
        compiler_params=pltpu.CompilerParams(vmem_limit_bytes=MIB),
        cost_estimate=pl.CostEstimate(
            flops=0,
            bytes_accessed=sum(2 * x.size * x.dtype.itemsize for x in arrays),
            transcendentals=0,
        ),
    )(*[pltpu.with_memory_space_constraint(x, pltpu.HBM) for x in arrays], after)


def attend(lengths, slot_row, blocks, cache):
    slots, cap, width = cache.shape
    kv_local = width // (2 * HD)
    heads = kv_local * GROUPS
    rows = STEPS * heads
    requests = slot_row.shape[1]
    count = len(blocks)
    fresh_at = STEPS * heads * HD
    columns = fresh_at + STEPS * width
    factor = HD ** (-0.5) * 1.4426950408889634

    def kernel(lengths, slot_row, *refs):
        blocks, cache, out = refs[:count], refs[count], refs[count + 1]
        qkv, qs, fresh, wide, scores, fresh_scores, mixed = refs[count + 2 :]
        place_blocks(blocks, qkv)
        base = lax.axis_index("att") * slots
        wanted = lax.broadcasted_iota(jnp.int32, (slots, requests), 0) + base
        pick = jnp.where(slot_row[...] == wanted, 1.0, 0.0).astype(BF16)
        mine = dot(pick, qkv[...])
        for s in range(STEPS):
            for h in range(heads):
                at = (s * heads + h) * HD
                qs[pl.ds(s * heads + h, slots, stride=rows), :] = mine[:, at : at + HD]
            fresh[s * slots : (s + 1) * slots, :] = mine[
                :, fresh_at + s * width : fresh_at + (s + 1) * width
            ].astype(BF16)
        group_of = lax.broadcasted_iota(jnp.int32, (slots * rows, HD), 0) % heads // GROUPS
        for g in range(kv_local):
            own = jnp.where(group_of == g, qs[...], 0.0)
            wide[:, g * 2 * HD : g * 2 * HD + HD] = own.astype(BF16)
            wide[:, g * 2 * HD + HD : (g + 1) * 2 * HD] = jnp.zeros((slots * rows, HD), BF16)

        across = (((1,), (1,)), ((), ()))
        fresh_scores[...] = lax.dot_general(
            wide[...], fresh[...], across, preferred_element_type=F32
        )
        for i in range(slots):
            here = slice(i * rows, (i + 1) * rows)
            scores[here, :] = lax.dot_general(
                wide[here, :], cache[i], across, preferred_element_type=F32
            )
        key_at = lax.broadcasted_iota(jnp.int32, (rows, cap), 1)
        fresh_step = lax.broadcasted_iota(jnp.int32, (rows, STEPS * slots), 1)
        row_step = lax.broadcasted_iota(jnp.int32, (rows, STEPS * slots), 0) // heads
        for i in range(slots):
            here = slice(i * rows, (i + 1) * rows)
            kept = jnp.where(key_at < lengths[i], scores[here, :], -jnp.inf)
            own = (fresh_step % slots == i) & (fresh_step // slots <= row_step)
            new = jnp.where(own, fresh_scores[here, :], -jnp.inf)
            top = jnp.maximum(
                jnp.max(kept, axis=1, keepdims=True), jnp.max(new, axis=1, keepdims=True)
            )
            kept = jnp.exp2((kept - top) * factor)
            new = jnp.exp2((new - top) * factor)
            total = jnp.sum(kept, axis=1, keepdims=True) + jnp.sum(new, axis=1, keepdims=True)
            values = dot(kept.astype(BF16), cache[i]) + dot(new.astype(BF16), fresh[...])
            values = values / total
            for s in range(STEPS):
                for g in range(kv_local):
                    at = s * heads + g * GROUPS
                    mixed[i * rows + at : i * rows + at + GROUPS, :] = values[
                        at : at + GROUPS, g * 2 * HD + HD : (g + 1) * 2 * HD
                    ]
        for s in range(STEPS):
            for h in range(heads):
                out[s * slots : (s + 1) * slots, h * HD : (h + 1) * HD] = mixed[
                    pl.ds(s * heads + h, slots, stride=rows), :
                ].astype(BF16)

    return pl.pallas_call(
        kernel,
        name="attend",
        out_shape=jax.ShapeDtypeStruct((STEPS * slots, heads * HD), BF16),
        in_specs=[SMEM, VMEM] + [VMEM] * count + [VMEM],
        out_specs=VMEM,
        scratch_shapes=[
            pltpu.VMEM((requests, columns), BF16),
            pltpu.VMEM((slots * rows, HD), F32),
            pltpu.VMEM((STEPS * slots, width), BF16),
            pltpu.VMEM((slots * rows, width), BF16),
            pltpu.VMEM((slots * rows, cap), F32),
            pltpu.VMEM((slots * rows, STEPS * slots), F32),
            pltpu.VMEM((slots * rows, HD), F32),
        ],
        compiler_params=pltpu.CompilerParams(vmem_limit_bytes=12 * MIB),
        cost_estimate=pl.CostEstimate(
            flops=4 * slots * rows * cap * width,
            bytes_accessed=slots * cap * width * 2,
            transcendentals=slots * rows * cap,
        ),
    )(lengths, slot_row, *blocks, cache)


def matmul_cost(rows, depth, columns):
    return pl.CostEstimate(
        flops=2 * rows * depth * columns,
        bytes_accessed=2 * (rows * depth + depth * columns + rows * columns),
        transcendentals=0,
    )


def shares(rows, columns):
    others = lax.axis_size("ffn") - 1
    share = rows // (others + 1)
    return [jax.ShapeDtypeStruct((share, columns), F32)] + [
        jax.ShapeDtypeStruct((share, columns), BF16)
    ] * others


def store_shares(product, outs, here):
    share = product.shape[0] // len(outs)
    for d, out in enumerate(outs):
        out[:, here] = product[d * share : (d + 1) * share].astype(out.dtype)


def project(source, blocks, w):
    count = len(blocks)
    rows = source.shape[0]
    depth, columns = w.shape
    block = min(512, columns)
    others = lax.axis_size("ffn") - 1
    share = rows // (others + 1)

    def kernel(source, *refs):
        blocks, w, outs = refs[:count], refs[count], refs[count + 1 : count + 2 + others]
        gathered, ordered = refs[-2:]
        place_blocks(blocks, gathered)
        for d in range(others + 1):
            owner = lax.rem(lax.axis_index("ffn") + d, others + 1)
            wanted = source[pl.ds(pl.multiple_of(owner * share, share), share), :]
            at = lax.broadcasted_iota(jnp.int32, (share, rows), 1)
            pick = jnp.where(at == wanted, 1.0, 0.0).astype(BF16)
            ordered[d * share : (d + 1) * share, :] = dot(pick, gathered[...]).astype(BF16)
        for j in range(columns // block):
            here = slice(j * block, (j + 1) * block)
            store_shares(dot(ordered[...], w[:, here]), outs, here)

    return pl.pallas_call(
        kernel,
        name="project",
        out_shape=shares(rows, columns),
        in_specs=[VMEM] * (count + 2),
        out_specs=[VMEM] * (others + 1),
        scratch_shapes=[pltpu.VMEM((rows, depth), BF16)] * 2,
        compiler_params=pltpu.CompilerParams(vmem_limit_bytes=8 * MIB),
        cost_estimate=matmul_cost(rows, depth, columns),
    )(source, *blocks, w)


def sum_over_ffn(parts):
    total = parts[0]
    for d in range(1, len(parts)):
        total = total + shift(parts[d], "ffn", d).astype(F32)
    return total


def widen(blocks, gain, w_gate, w_up, first, count, with_squares):
    parts = len(blocks)
    depth = blocks[0].shape[1]
    rows = sum(block.shape[0] for block in blocks)
    att = lax.axis_size("att")
    chips = att // 2
    share = rows // att
    half = rows // 2
    extra = HD if with_squares else 0
    width = count * 2 * BLOCK + extra

    def kernel(*refs):
        blocks, (gain, gate, up, keep, send) = refs[:parts], refs[parts : parts + 5]
        residual, normed = refs[-2:]
        at = 0
        for block in blocks:
            residual[at : at + block.shape[0], :] = block[...]
            at += block.shape[0]
        me = lax.axis_index("att")
        chip, core = me // 2, lax.rem(me, 2)
        for side in range(2):
            for d in range(chips):
                owner = lax.rem(chip + d, chips) * 2 + lax.rem(core + side, 2)
                part = residual[pl.ds(pl.multiple_of(owner * share, share), share), :].astype(F32)
                at = side * half + d * share
                normed[at : at + share, :] = (part * gain[...]).astype(BF16)
                if with_squares:
                    squares = jnp.sum(part * part, axis=1, keepdims=True)
                    high = squares.astype(BF16).astype(F32)
                    lane = lax.broadcasted_iota(jnp.int32, (share, HD), 1)
                    both = jnp.where(lane == 0, high, squares - high).astype(BF16)
                    target = send if side else keep
                    target[d * share : (d + 1) * share, count * 2 * BLOCK :] = both
        for j in range(count):
            for which, w in enumerate((gate, up)):
                product = dot(normed[...], w[:, (first + j) * BLOCK : (first + j + 1) * BLOCK])
                here = slice((2 * j + which) * BLOCK, (2 * j + which + 1) * BLOCK)
                keep[:, here] = product[:half].astype(BF16)
                send[:, here] = product[half:].astype(BF16)

    return pl.pallas_call(
        kernel,
        name="widen",
        out_shape=[jax.ShapeDtypeStruct((half, width), BF16)] * 2,
        in_specs=[VMEM] * (parts + 3),
        out_specs=[VMEM] * 2,
        scratch_shapes=[pltpu.VMEM((rows, depth), BF16)] * 2,
        compiler_params=pltpu.CompilerParams(vmem_limit_bytes=8 * MIB),
        cost_estimate=matmul_cost(rows, depth, count * 2 * BLOCK),
    )(*blocks, gain, w_gate, w_up)


def add_pair(keep, arrived):
    chips = lax.axis_size("att") // 2
    half, width = keep.shape
    share = half // chips

    def kernel(keep, arrived, *outs):
        for d, out in enumerate(outs):
            here = slice(d * share, (d + 1) * share)
            out[...] = (keep[here, :].astype(F32) + arrived[here, :].astype(F32)).astype(out.dtype)

    return pl.pallas_call(
        kernel,
        name="add_pair",
        out_shape=[jax.ShapeDtypeStruct((share, width), F32)]
        + [jax.ShapeDtypeStruct((share, width), BF16)] * (chips - 1),
        in_specs=[VMEM] * 2,
        out_specs=[VMEM] * chips,
        compiler_params=pltpu.CompilerParams(vmem_limit_bytes=8 * MIB),
    )(keep, arrived)


def gate_rows(own, moved, scale, model):
    share, width = own.shape
    count = width // (2 * BLOCK)
    first = scale is None
    others = len(moved)

    def kernel(*refs):
        own, moved, rest = refs[0], refs[1 : 1 + others], refs[1 + others :]

        def total(here):
            value = own[:, here]
            for part in moved:
                value = value + part[:, here].astype(F32)
            return value

        if first:
            out, scale = rest
            tail = total(slice(count * 2 * BLOCK, count * 2 * BLOCK + HD))
            squares = tail[:, 0:1] + tail[:, 1:2]
            factor = lax.rsqrt(squares / model + EPSILON)
            scale[...] = jnp.broadcast_to(factor, scale.shape)
        else:
            scale, out = rest
            factor = scale[:, 0:1]
        for j in range(count):
            gate = total(slice(2 * j * BLOCK, (2 * j + 1) * BLOCK)) * factor
            up = total(slice((2 * j + 1) * BLOCK, (2 * j + 2) * BLOCK)) * factor
            out[:, j * BLOCK : (j + 1) * BLOCK] = (gate / (1.0 + jnp.exp(-gate)) * up).astype(BF16)

    hidden = jax.ShapeDtypeStruct((share, count * BLOCK), BF16)
    kept = jax.ShapeDtypeStruct((share, HD), F32)
    return pl.pallas_call(
        kernel,
        name="gate",
        out_shape=[hidden, kept] if first else hidden,
        in_specs=[VMEM] * (1 + others + (0 if first else 1)),
        out_specs=[VMEM] * 2 if first else VMEM,
        compiler_params=pltpu.CompilerParams(vmem_limit_bytes=8 * MIB),
    )(own, *moved, *([] if first else [scale]))


def narrow(chunks, w):
    depth, columns = w.shape
    count = len(chunks[0])
    sizes = [chunk[0].shape[1] for chunk in chunks]
    rows = count * chunks[0][0].shape[0]
    others = lax.axis_size("ffn") - 1
    block = min(512, columns)
    flat = [block for chunk in chunks for block in chunk]

    def kernel(*refs):
        w, outs, hidden = refs[len(flat)], refs[len(flat) + 1 : -1], refs[-1]
        at = 0
        for k, size in enumerate(sizes):
            place_blocks(refs[k * count : (k + 1) * count], hidden, slice(at, at + size))
            at += size
        for j in range(columns // block):
            here = slice(j * block, (j + 1) * block)
            store_shares(dot(hidden[...], w[:, here]), outs, here)

    return pl.pallas_call(
        kernel,
        name="narrow",
        out_shape=shares(rows, columns),
        in_specs=[VMEM] * (len(flat) + 1),
        out_specs=[VMEM] * (others + 1),
        scratch_shapes=[pltpu.VMEM((rows, depth), BF16)],
        compiler_params=pltpu.CompilerParams(vmem_limit_bytes=8 * MIB),
        cost_estimate=matmul_cost(rows, depth, columns),
    )(*flat, w)


def local(
    incoming, queries, new_kv, cache, lengths, slot_of, w_out, norm_gain, w_gate, w_up, w_down
):
    ffn = lax.axis_size("ffn")
    att = lax.axis_size("att")
    requests = slot_of.shape[0]
    slots = cache.shape[0]
    model = w_out.shape[1]
    width = w_gate.shape[1]
    owned = requests // ffn

    qkv = jnp.concatenate([queries.reshape(slots, -1), new_kv.reshape(slots, -1)], axis=1)
    blocks = [qkv, swap_cores(qkv)]
    moved = [shift(qkv, "att", 2 * d) for d in range(1, att // 2)]
    cache, token = load([cache], slot_of.reshape(1, requests), "load_cache")
    moved, token = lax.optimization_barrier((moved, token))
    for block in moved:
        blocks += [block, swap_cores(block)]
    w_out, token = load([w_out], token, "load_out")
    attended = attend(lengths, slot_of.reshape(1, requests), blocks, cache)

    at_step = (slot_of // slots * (STEPS * slots) + slot_of % slots).reshape(ffn, 1, owned)
    source = at_step + (jnp.arange(STEPS, dtype=jnp.int32) * slots)[None, :, None]
    parts = project(source.reshape(STEPS * requests, 1), gather_att(attended), w_out)
    w_gate, w_up, token = load([w_gate, w_up], parts[1][:8, :HD], "load_wide")
    own = lax.dynamic_slice_in_dim(incoming, lax.axis_index("ffn") * owned, owned, 0)
    own = jnp.swapaxes(own, 0, 1).reshape(STEPS * owned, model)
    residual = (own.astype(F32) + sum_over_ffn(parts)).astype(BF16)
    w_down, token = load([w_down], residual[:8, :HD], "load_narrow")

    blocks = [residual] + [shift(residual, "ffn", -d) for d in range(1, ffn)]
    gain = norm_gain.reshape(1, model)
    edges = [width // BLOCK * k // CHUNKS for k in range(CHUNKS + 1)]
    chunks = []
    scale = None
    for first, last in zip(edges[:-1], edges[1:]):
        keep, send = widen(blocks, gain, w_gate, w_up, first, last - first, first == 0)
        total, *out = add_pair(keep, swap_cores(send))
        moved = [shift(part, "att", 2 * (d + 1)) for d, part in enumerate(out)]
        if first == 0:
            hidden, scale = gate_rows(total, moved, None, model * att)
        else:
            hidden = gate_rows(total, moved, scale, model * att)
        chunks.append(gather_att(hidden))
    lowered = sum_over_ffn(narrow(chunks, w_down))
    out = (residual.astype(F32) + lowered).astype(BF16)
    return jnp.swapaxes(out.reshape(STEPS, owned, model), 0, 1)


def solution(mesh):
    return jax.shard_map(
        local,
        mesh=mesh,
        in_specs=(
            P("parts", None, "att"),
            P(("parts", "att"), None, "ffn"),
            P(("parts", "att"), None, "ffn"),
            P(("parts", "att"), None, "ffn"),
            P(("parts", "att")),
            P("parts"),
            P("ffn", "att"),
            P("att"),
            P("att", "ffn"),
            P("att", "ffn"),
            P("ffn", "att"),
        ),
        out_specs=P(("parts", "ffn"), None, "att"),
        check_vma=False,
    )
```

```python
import functools

import jax
import jax.numpy as jnp
from jax import lax
from jax.experimental import pallas as pl
from jax.experimental.pallas import tpu as pltpu
from jax.sharding import PartitionSpec as P

H = 64
KVH = 8
HD = 128
STEPS = 2
GROUPS = H // KVH
EPSILON = 1e-05
BLOCK = 256
F32 = jnp.float32
BF16 = jnp.bfloat16
MIB = 1024 * 1024


def dot(a, b):
    return jnp.dot(a, b, preferred_element_type=F32)

VMEM = pl.BlockSpec(memory_space=pltpu.VMEM)
ANY = pl.BlockSpec(memory_space=pl.ANY)
TOKEN = jax.ShapeDtypeStruct((8, HD), F32)


def shift(x, axis, d):
    n = lax.axis_size(axis)
    return lax.ppermute(x, axis, [(i, (i + d) % n) for i in range(n)])


def exchange(x, axis, bit):
    return lax.ppermute(x, axis, [(i, i ^ bit) for i in range(lax.axis_size(axis))])


def limit(mib):
    return pltpu.CompilerParams(vmem_limit_bytes=mib * MIB)


def join(blocks, after=()):
    count = len(blocks)
    rows = [block.shape[0] for block in blocks]

    def kernel(*refs):
        out, at = refs[-1], 0
        for ref, size in zip(refs[:count], rows):
            out[at : at + size, :] = ref[...]
            at += size

    return pl.pallas_call(
        kernel,
        name="join",
        out_shape=jax.ShapeDtypeStruct((sum(rows), blocks[0].shape[1]), blocks[0].dtype),
        in_specs=[VMEM] * (count + len(after)),
        out_specs=VMEM,
        compiler_params=limit(4),
    )(*blocks, *after)


def gather_att(x, token=()):
    chips = lax.axis_size("att") // 2
    same = join([x] + [shift(x, "att", 2 * d) for d in range(1, chips)], token)
    return same, exchange(same, "att", 1)


def place_gathered(same, other, whole):
    me, chips = lax.axis_index("att"), lax.axis_size("att") // 2
    rows = same.shape[0] // chips
    for d in range(chips):
        chip = lax.rem(me // 2 + chips - d, chips)
        for side, ref in enumerate((same, other)):
            source = chip * 2 + lax.rem(me + side, 2)
            at = pl.multiple_of(source * rows, rows)
            whole[pl.ds(at, rows), :] = ref[d * rows : (d + 1) * rows, :]


def reduce_ffn(keep, send):
    arrived, bit = exchange(send, "ffn", 1), 2
    while bit < lax.axis_size("ffn"):
        keep, send = add_parts(keep, arrived, 2)
        arrived, bit = exchange(send, "ffn", bit), 2 * bit
    return keep, arrived


def gather_ffn(x):
    bit = lax.axis_size("ffn") // 2
    while bit > 1:
        x, bit = join([x, exchange(x, "ffn", bit)]), bit // 2
    return x, exchange(x, "ffn", 1)


def ffn_order(n):
    order, bit = [0], n // 2
    while bit:
        order, bit = order + [r ^ bit for r in order], bit // 2
    return order


def hbm(x):
    return pltpu.with_memory_space_constraint(x, pltpu.HBM)


class Copies:
    def __init__(self, entries):
        self.entries = entries
        self.sources = [hbm(x) for x, _, _ in entries]
        self.shapes = [pltpu.VMEM(x.shape[:-1] + (n,), x.dtype) for x, _, n in entries]
        self.scratch = pltpu.SemaphoreType.DMA((len(entries), 8))
        self.bytes = sum(2 * x.size // x.shape[-1] * n * x.dtype.itemsize for x, _, n in entries)

    def started(self, sources, targets, sems):
        copies = []
        for k, (x, first, columns) in enumerate(self.entries):
            parts = 8 if x.shape[0] % 8 == 0 else 1
            size = x.shape[0] // parts
            for p in range(parts):
                rows = pl.ds(p * size, size)
                source = sources[k].at[rows]
                if columns != x.shape[-1]:
                    source = sources[k].at[rows, pl.ds(first, columns)]
                copies.append(
                    pltpu.make_async_copy(source, targets[k].at[rows], sems.at[k, p])
                )
        for copy in copies:
            copy.start()
        return copies


def load(entries, after, name):
    work = Copies(entries)
    count = len(entries)

    def kernel(*refs):
        targets, token, sems = refs[count + 1 : 2 * count + 1], refs[-2], refs[-1]
        copies = work.started(refs[:count], targets, sems)
        token[...] = jnp.zeros_like(token)
        for copy in copies:
            copy.wait()

    return pl.pallas_call(
        kernel,
        name=name,
        out_shape=work.shapes + [jax.ShapeDtypeStruct((8, HD), F32)],
        in_specs=[ANY] * count + [VMEM],
        out_specs=[VMEM] * (count + 1),
        scratch_shapes=[work.scratch],
        compiler_params=limit(1),
        cost_estimate=pl.CostEstimate(flops=0, bytes_accessed=work.bytes, transcendentals=0),
    )(*work.sources, after)


def attend(lengths, slot_row, same, other, cache, entries):
    work = Copies(entries)
    riders = len(entries)
    slots, cap, width = cache.shape
    kv_local = width // (2 * HD)
    heads = kv_local * GROUPS
    rows = STEPS * heads
    requests = slot_row.shape[1]
    fresh_at = STEPS * heads * HD
    columns = fresh_at + STEPS * width
    factor = HD ** (-0.5) * 1.4426950408889634

    def kernel(lengths, slot_row, same, other, cache, *refs):
        sources, out, targets = refs[:riders], refs[riders], refs[riders + 1 : 2 * riders + 1]
        qkv, qs, fresh, wide, scores, fresh_scores, mixed, sems = refs[2 * riders + 1 :]
        copies = work.started(sources, targets, sems)
        place_gathered(same, other, qkv)
        base = lax.axis_index("att") * slots
        wanted = lax.broadcasted_iota(jnp.int32, (slots, requests), 0) + base
        pick = jnp.where(slot_row[...] == wanted, 1.0, 0.0).astype(BF16)
        mine = dot(pick, qkv[...])
        for s in range(STEPS):
            for h in range(heads):
                at = (s * heads + h) * HD
                qs[pl.ds(s * heads + h, slots, stride=rows), :] = mine[:, at : at + HD]
            fresh[s * slots : (s + 1) * slots, :] = mine[
                :, fresh_at + s * width : fresh_at + (s + 1) * width
            ].astype(BF16)
        group_of = lax.broadcasted_iota(jnp.int32, (slots * rows, HD), 0) % heads // GROUPS
        for g in range(kv_local):
            own = jnp.where(group_of == g, qs[...], 0.0)
            wide[:, g * 2 * HD : g * 2 * HD + HD] = own.astype(BF16)
            wide[:, g * 2 * HD + HD : (g + 1) * 2 * HD] = jnp.zeros((slots * rows, HD), BF16)

        across = (((1,), (1,)), ((), ()))
        fresh_scores[...] = lax.dot_general(
            wide[...], fresh[...], across, preferred_element_type=F32
        )
        for i in range(slots):
            here = slice(i * rows, (i + 1) * rows)
            scores[here, :] = lax.dot_general(
                wide[here, :], cache[i], across, preferred_element_type=F32
            )
        key_at = lax.broadcasted_iota(jnp.int32, (rows, cap), 1)
        fresh_step = lax.broadcasted_iota(jnp.int32, (rows, STEPS * slots), 1)
        row_step = lax.broadcasted_iota(jnp.int32, (rows, STEPS * slots), 0) // heads
        for i in range(slots):
            here = slice(i * rows, (i + 1) * rows)
            kept = jnp.where(key_at < lengths[:, i : i + 1], scores[here, :], -jnp.inf)
            own = (fresh_step % slots == i) & (fresh_step // slots <= row_step)
            new = jnp.where(own, fresh_scores[here, :], -jnp.inf)
            top = jnp.maximum(
                jnp.max(kept, axis=1, keepdims=True), jnp.max(new, axis=1, keepdims=True)
            )
            kept = jnp.exp2((kept - top) * factor)
            new = jnp.exp2((new - top) * factor)
            total = jnp.sum(kept, axis=1, keepdims=True) + jnp.sum(new, axis=1, keepdims=True)
            values = dot(kept.astype(BF16), cache[i]) + dot(new.astype(BF16), fresh[...])
            values = values / total
            for s in range(STEPS):
                for g in range(kv_local):
                    at = s * heads + g * GROUPS
                    mixed[i * rows + at : i * rows + at + GROUPS, :] = values[
                        at : at + GROUPS, g * 2 * HD + HD : (g + 1) * 2 * HD
                    ]
        for s in range(STEPS):
            for h in range(heads):
                out[s * slots : (s + 1) * slots, h * HD : (h + 1) * HD] = mixed[
                    pl.ds(s * heads + h, slots, stride=rows), :
                ].astype(BF16)
        for copy in copies:
            copy.wait()

    return pl.pallas_call(
        kernel,
        name="attend",
        out_shape=[jax.ShapeDtypeStruct((STEPS * slots, heads * HD), BF16)] + work.shapes,
        in_specs=[VMEM] * 5 + [ANY] * riders,
        out_specs=[VMEM] * (riders + 1),
        scratch_shapes=[
            pltpu.VMEM((requests, columns), BF16),
            pltpu.VMEM((slots * rows, HD), F32),
            pltpu.VMEM((STEPS * slots, width), BF16),
            pltpu.VMEM((slots * rows, width), BF16),
            pltpu.VMEM((slots * rows, cap), F32),
            pltpu.VMEM((slots * rows, STEPS * slots), F32),
            pltpu.VMEM((slots * rows, HD), F32),
            work.scratch,
        ],
        compiler_params=limit(6),
        cost_estimate=pl.CostEstimate(
            flops=4 * slots * rows * cap * width,
            bytes_accessed=slots * cap * width * 2 + work.bytes,
            transcendentals=slots * rows * cap,
        ),
    )(lengths, slot_row, same, other, cache, *work.sources)


def matmul_cost(rows, depth, columns):
    return pl.CostEstimate(
        flops=2 * rows * depth * columns,
        bytes_accessed=2 * (rows * depth + depth * columns + rows * columns),
        transcendentals=0,
    )


def halves(rows, columns):
    return [
        jax.ShapeDtypeStruct((rows // 2, columns), F32),
        jax.ShapeDtypeStruct((rows // 2, columns), BF16),
    ]


def multiply_halves(rows, w, keep, send):
    half = rows.shape[0] // 2
    columns = w.shape[1]
    block = min(512, columns)
    for j in range(columns // block):
        here = slice(j * block, (j + 1) * block)
        product = dot(rows[...], w[:, here])
        keep[:, here] = product[:half]
        send[:, here] = product[half:].astype(BF16)


def project(source, step, same, other, w):
    rows = source.shape[0]
    held = STEPS * rows
    before = step * (rows // lax.axis_size("att"))
    depth, columns = w.shape
    ffn = lax.axis_size("ffn")
    share = rows // ffn

    def kernel(source, same, other, w, keep, send, gathered, ordered):
        place_gathered(same, other, gathered)
        me = lax.axis_index("ffn")
        for k, r in enumerate(ffn_order(ffn)):
            owner = jnp.bitwise_xor(me, r)
            wanted = source[pl.ds(pl.multiple_of(owner * share, share), share), :]
            at = lax.broadcasted_iota(jnp.int32, (share, held), 1)
            pick = jnp.where(at == wanted + before, 1.0, 0.0).astype(BF16)
            ordered[k * share : (k + 1) * share, :] = dot(pick, gathered[...]).astype(BF16)
        multiply_halves(ordered, w, keep, send)

    return pl.pallas_call(
        kernel,
        name="project",
        out_shape=halves(rows, columns),
        in_specs=[VMEM] * 4,
        out_specs=[VMEM] * 2,
        scratch_shapes=[pltpu.VMEM((held, depth), BF16), pltpu.VMEM((rows, depth), BF16)],
        compiler_params=limit(4),
        cost_estimate=matmul_cost(rows, depth, columns),
    )(source, same, other, w)


def add_parts(keep, arrived, parts):
    rows, width = keep.shape
    share = rows // parts

    def kernel(keep, arrived, *outs):
        for d, out in enumerate(outs):
            here = slice(d * share, (d + 1) * share)
            out[...] = (keep[here, :].astype(F32) + arrived[here, :].astype(F32)).astype(out.dtype)

    return pl.pallas_call(
        kernel,
        name="add_parts",
        out_shape=[jax.ShapeDtypeStruct((share, width), F32)]
        + [jax.ShapeDtypeStruct((share, width), BF16)] * (parts - 1),
        in_specs=[VMEM] * 2,
        out_specs=[VMEM] * parts,
        compiler_params=limit(4),
    )(keep, arrived)


def add_residual(own, step, terms, after):
    rows, columns = terms[0].shape

    def kernel(own, keep, arrived, after, out):
        total = keep[...] + arrived[...].astype(F32)
        out[...] = (own[step * rows : (step + 1) * rows, :].astype(F32) + total).astype(BF16)

    return pl.pallas_call(
        kernel,
        name="add_residual",
        out_shape=jax.ShapeDtypeStruct((rows, columns), BF16),
        in_specs=[VMEM] * 4,
        out_specs=VMEM,
        compiler_params=limit(4),
    )(own, *terms, after)


def widen(blocks, gain, weights):
    parts = len(blocks)
    depth = blocks[0].shape[1]
    rows = sum(block.shape[0] for block in blocks)
    att = lax.axis_size("att")
    chips = att // 2
    share = rows // att
    half = rows // 2
    pieces = [(k, at) for k, w in enumerate(weights) for at in range(0, w.shape[1], BLOCK)]
    count = len(pieces) // 2
    width = count * 2 * BLOCK + HD

    def kernel(*refs):
        blocks, gain = refs[:parts], refs[parts]
        weights, (keep, send, residual, normed) = refs[parts + 1 : -4], refs[-4:]
        at = 0
        for block in blocks:
            residual[at : at + block.shape[0], :] = block[...]
            at += block.shape[0]
        me = lax.axis_index("att")
        chip, core = me // 2, lax.rem(me, 2)
        for side in range(2):
            for d in range(chips):
                owner = lax.rem(chip + d, chips) * 2 + lax.rem(core + side, 2)
                part = residual[pl.ds(pl.multiple_of(owner * share, share), share), :].astype(F32)
                at = side * half + d * share
                normed[at : at + share, :] = (part * gain[...]).astype(BF16)
                squares = jnp.sum(part * part, axis=1, keepdims=True)
                high = squares.astype(BF16).astype(F32)
                lane = lax.broadcasted_iota(jnp.int32, (share, HD), 1)
                both = jnp.where(lane == 0, high, squares - high).astype(BF16)
                target = send if side else keep
                target[d * share : (d + 1) * share, count * 2 * BLOCK :] = both
        for j in range(count):
            for which in range(2):
                k, at = pieces[which * count + j]
                product = dot(normed[...], weights[k][:, at : at + BLOCK])
                here = slice((2 * j + which) * BLOCK, (2 * j + which + 1) * BLOCK)
                keep[:, here] = product[:half].astype(BF16)
                send[:, here] = product[half:].astype(BF16)

    return pl.pallas_call(
        kernel,
        name="widen",
        out_shape=[jax.ShapeDtypeStruct((half, width), BF16)] * 2,
        in_specs=[VMEM] * (parts + 1 + len(weights)),
        out_specs=[VMEM] * 2,
        scratch_shapes=[pltpu.VMEM((rows, depth), BF16)] * 2,
        compiler_params=limit(4),
        cost_estimate=matmul_cost(rows, depth, count * 2 * BLOCK),
    )(*blocks, gain, *weights)


def gate_rows(own, moved, model, after):
    share, width = own.shape
    count = width // (2 * BLOCK)
    others = len(moved)

    def kernel(*refs):
        own, moved, out = refs[0], refs[1 : 1 + others], refs[-1]

        def total(here):
            value = own[:, here]
            for part in moved:
                value = value + part[:, here].astype(F32)
            return value

        tail = total(slice(count * 2 * BLOCK, count * 2 * BLOCK + HD))
        factor = lax.rsqrt((tail[:, 0:1] + tail[:, 1:2]) / model + EPSILON)
        for j in range(count):
            gate = total(slice(2 * j * BLOCK, (2 * j + 1) * BLOCK)) * factor
            up = total(slice((2 * j + 1) * BLOCK, (2 * j + 2) * BLOCK)) * factor
            out[:, j * BLOCK : (j + 1) * BLOCK] = (gate / (1.0 + jnp.exp(-gate)) * up).astype(BF16)

    return pl.pallas_call(
        kernel,
        name="gate",
        out_shape=jax.ShapeDtypeStruct((share, count * BLOCK), BF16),
        in_specs=[VMEM] * (2 + others),
        out_specs=VMEM,
        compiler_params=limit(4),
    )(own, *moved, after)


def narrow(same, other, w):
    depth, columns = w.shape
    rows = 2 * same.shape[0]

    def kernel(same, other, w, keep, send, hidden):
        place_gathered(same, other, hidden)
        multiply_halves(hidden, w, keep, send)

    return pl.pallas_call(
        kernel,
        name="narrow",
        out_shape=halves(rows, columns),
        in_specs=[VMEM] * 3,
        out_specs=[VMEM] * 2,
        scratch_shapes=[pltpu.VMEM((rows, depth), BF16)],
        compiler_params=limit(4),
        cost_estimate=matmul_cost(rows, depth, columns),
    )(same, other, w)


def local(
    incoming, queries, new_kv, cache, lengths, slot_of, w_out, norm_gain, w_gate, w_up, w_down
):
    ffn = lax.axis_size("ffn")
    att = lax.axis_size("att")
    requests = slot_of.shape[0]
    slots = cache.shape[0]
    model = w_out.shape[1]
    width = w_gate.shape[1]
    owned = requests // ffn

    whole = lambda x: (x, 0, x.shape[-1])
    corner = lambda x: x[:8, :HD]

    qkv = jnp.concatenate([queries.reshape(slots, -1), new_kv.reshape(slots, -1)], axis=1)
    small = [slot_of.reshape(1, requests), lengths.reshape(1, slots)]
    entries = [whole(x) for x in [cache] + small]
    cache, slot_row, lengths, token = load(entries, corner(qkv), "load_cache")
    same, other = gather_att(qkv, [token])
    cut = width // BLOCK // 2 * BLOCK
    attended, w_out, up_ahead = attend(
        lengths, slot_row, same, other, cache, [whole(w_out), (w_up, 0, cut)]
    )

    w_gate, token = load([whole(w_gate)], corner(attended), "load_gate")
    same, other = gather_att(attended, [token])
    source = (slot_of // slots * (STEPS * slots) + slot_of % slots).reshape(requests, 1)
    products = [project(source, step, same, other, w_out) for step in range(STEPS)]
    up_behind, token = load([(w_up, cut, width - cut)], corner(products[-1][1]), "load_up")
    own = lax.dynamic_slice_in_dim(incoming, lax.axis_index("ffn") * owned, owned, 0)
    own = jnp.swapaxes(own, 0, 1).reshape(STEPS * owned, model)
    residual = [add_residual(own, k, reduce_ffn(*products[k]), token) for k in range(STEPS)]

    gain = norm_gain.reshape(1, model)
    weights = [w_gate, up_ahead, up_behind]
    sums = [widen(gather_ffn(residual[k]), gain, weights) for k in range(STEPS)]
    w_down, token = load([whole(w_down)], corner(sums[-1][0]), "load_down")
    outs = []
    for step, (keep, send) in enumerate(sums):
        total, *away = add_parts(keep, exchange(send, "att", 1), att // 2)
        moved = [shift(part, "att", 2 * (d + 1)) for d, part in enumerate(away)]
        hidden = gate_rows(total, moved, model * att, token)
        keep, arrived = reduce_ffn(*narrow(*gather_att(hidden), w_down))
        outs.append((residual[step].astype(F32) + (keep + arrived.astype(F32))).astype(BF16))
    return jnp.stack(outs, axis=1)


def solution(mesh):
    return jax.shard_map(
        local,
        mesh=mesh,
        in_specs=(
            P("parts", None, "att"),
            P(("parts", "att"), None, "ffn"),
            P(("parts", "att"), None, "ffn"),
            P(("parts", "att"), None, "ffn"),
            P(("parts", "att")),
            P("parts"),
            P("ffn", "att"),
            P("att"),
            P("att", "ffn"),
            P("att", "ffn"),
            P("ffn", "att"),
        ),
        out_specs=P(("parts", "ffn"), None, "att"),
        check_vma=False,
    )
```

```python
import functools

import jax
import jax.numpy as jnp
from jax import lax
from jax.experimental import pallas as pl
from jax.experimental.pallas import tpu as pltpu
from jax.sharding import PartitionSpec as P

H = 64
KVH = 8
HD = 128
STEPS = 2
GROUPS = H // KVH
EPSILON = 1e-05
BLOCK = 256
CHUNKS = 3
F32 = jnp.float32
BF16 = jnp.bfloat16
MIB = 1024 * 1024


def dot(a, b):
    return jnp.dot(a, b, preferred_element_type=F32)

VMEM = pl.BlockSpec(memory_space=pltpu.VMEM)
ANY = pl.BlockSpec(memory_space=pl.ANY)


def shift(x, axis, d):
    n = lax.axis_size(axis)
    return lax.ppermute(x, axis, [(i, (i + d) % n) for i in range(n)])


def exchange(x, axis, bit):
    return lax.ppermute(x, axis, [(i, i ^ bit) for i in range(lax.axis_size(axis))])


def limit(mib):
    return pltpu.CompilerParams(vmem_limit_bytes=mib * MIB)


def join(blocks, after=()):
    count = len(blocks)
    rows = [block.shape[0] for block in blocks]

    def kernel(*refs):
        out, at = refs[-1], 0
        for ref, size in zip(refs[:count], rows):
            out[at : at + size, :] = ref[...]
            at += size

    return pl.pallas_call(
        kernel,
        name="join",
        out_shape=jax.ShapeDtypeStruct((sum(rows), blocks[0].shape[1]), blocks[0].dtype),
        in_specs=[VMEM] * (count + len(after)),
        out_specs=VMEM,
        compiler_params=limit(4),
    )(*blocks, *after)


def gather_att(x, token=()):
    chips = lax.axis_size("att") // 2
    same = join([x] + [shift(x, "att", 2 * d) for d in range(1, chips)], token)
    return same, exchange(same, "att", 1)


def place_gathered(same, other, whole, columns=slice(None)):
    me, chips = lax.axis_index("att"), lax.axis_size("att") // 2
    rows = same.shape[0] // chips
    for d in range(chips):
        chip = lax.rem(me // 2 + chips - d, chips)
        for side, ref in enumerate((same, other)):
            source = chip * 2 + lax.rem(me + side, 2)
            at = pl.multiple_of(source * rows, rows)
            whole[pl.ds(at, rows), columns] = ref[d * rows : (d + 1) * rows, :]


def reduce_ffn(own, near, keep, far):
    terms = [own, exchange(near, "ffn", 1)]
    ffn = lax.axis_size("ffn")
    if ffn > 2:
        sums = add_parts(keep, exchange(far, "ffn", 1), ffn // 2 - 1)
        terms += [exchange(part, "ffn", 2 * (k + 1)) for k, part in enumerate(sums)]
    return terms


def gather_ffn(x, token=()):
    across = [exchange(x, "ffn", m) for m in range(2, lax.axis_size("ffn"), 2)]
    across = [join([block], token) for block in across]
    blocks = [x, exchange(x, "ffn", 1)]
    for block in across:
        blocks += [block, exchange(block, "ffn", 1)]
    return blocks


def take_own(x, count):
    def kernel(x, out, sem):
        rows = pl.ds(lax.axis_index("ffn") * count, count)
        copy = pltpu.make_async_copy(x.at[rows], out, sem)
        copy.start()
        copy.wait()

    return pl.pallas_call(
        kernel,
        name="take_own",
        out_shape=jax.ShapeDtypeStruct((count,) + x.shape[1:], x.dtype),
        in_specs=[ANY],
        out_specs=VMEM,
        scratch_shapes=[pltpu.SemaphoreType.DMA(())],
        compiler_params=limit(4),
    )(hbm(x))


def hbm(x):
    return pltpu.with_memory_space_constraint(x, pltpu.HBM)


class Copies:
    def __init__(self, entries):
        self.entries = entries
        self.sources = [hbm(x) for x, _, _ in entries]
        self.shapes = [pltpu.VMEM(x.shape[:-1] + (n,), x.dtype) for x, _, n in entries]
        self.scratch = pltpu.SemaphoreType.DMA((len(entries), 8))
        self.bytes = sum(2 * x.size // x.shape[-1] * n * x.dtype.itemsize for x, _, n in entries)

    def started(self, sources, targets, sems):
        copies = []
        for k, (x, first, columns) in enumerate(self.entries):
            parts = 8 if x.shape[0] % 8 == 0 else 1
            size = x.shape[0] // parts
            for p in range(parts):
                rows = pl.ds(p * size, size)
                source = sources[k].at[rows]
                if columns != x.shape[-1]:
                    source = sources[k].at[rows, pl.ds(first, columns)]
                copies.append(
                    pltpu.make_async_copy(source, targets[k].at[rows], sems.at[k, p])
                )
        for copy in copies:
            copy.start()
        return copies


def load(entries, after, name):
    work = Copies(entries)
    count = len(entries)

    def kernel(*refs):
        targets, token, sems = refs[count + 1 : 2 * count + 1], refs[-2], refs[-1]
        copies = work.started(refs[:count], targets, sems)
        token[...] = jnp.zeros_like(token)
        for copy in copies:
            copy.wait()

    return pl.pallas_call(
        kernel,
        name=name,
        out_shape=work.shapes + [jax.ShapeDtypeStruct((8, HD), F32)],
        in_specs=[ANY] * count + [VMEM],
        out_specs=[VMEM] * (count + 1),
        scratch_shapes=[work.scratch],
        compiler_params=limit(1),
        cost_estimate=pl.CostEstimate(flops=0, bytes_accessed=work.bytes, transcendentals=0),
    )(*work.sources, after)


def attend(lengths, slot_row, same, other, cache):
    slots, cap, width = cache.shape
    kv_local = width // (2 * HD)
    heads = kv_local * GROUPS
    rows = STEPS * heads
    requests = slot_row.shape[1]
    fresh_at = STEPS * heads * HD
    columns = fresh_at + STEPS * width
    factor = HD ** (-0.5) * 1.4426950408889634

    def kernel(lengths, slot_row, same, other, cache, out, *scratch):
        qkv, qs, fresh, wide, scores, fresh_scores, mixed = scratch
        place_gathered(same, other, qkv)
        base = lax.axis_index("att") * slots
        wanted = lax.broadcasted_iota(jnp.int32, (slots, requests), 0) + base
        pick = jnp.where(slot_row[...] == wanted, 1.0, 0.0).astype(BF16)
        mine = dot(pick, qkv[...])
        for s in range(STEPS):
            for h in range(heads):
                at = (s * heads + h) * HD
                qs[pl.ds(s * heads + h, slots, stride=rows), :] = mine[:, at : at + HD]
            fresh[s * slots : (s + 1) * slots, :] = mine[
                :, fresh_at + s * width : fresh_at + (s + 1) * width
            ].astype(BF16)
        group_of = lax.broadcasted_iota(jnp.int32, (slots * rows, HD), 0) % heads // GROUPS
        for g in range(kv_local):
            own = jnp.where(group_of == g, qs[...], 0.0)
            wide[:, g * 2 * HD : g * 2 * HD + HD] = own.astype(BF16)
            wide[:, g * 2 * HD + HD : (g + 1) * 2 * HD] = jnp.zeros((slots * rows, HD), BF16)

        across = (((1,), (1,)), ((), ()))
        fresh_scores[...] = lax.dot_general(
            wide[...], fresh[...], across, preferred_element_type=F32
        )
        for i in range(slots):
            here = slice(i * rows, (i + 1) * rows)
            scores[here, :] = lax.dot_general(
                wide[here, :], cache[i], across, preferred_element_type=F32
            )
        key_at = lax.broadcasted_iota(jnp.int32, (rows, cap), 1)
        fresh_step = lax.broadcasted_iota(jnp.int32, (rows, STEPS * slots), 1)
        row_step = lax.broadcasted_iota(jnp.int32, (rows, STEPS * slots), 0) // heads
        for i in range(slots):
            here = slice(i * rows, (i + 1) * rows)
            kept = jnp.where(key_at < lengths[:, i : i + 1], scores[here, :], -jnp.inf)
            own = (fresh_step % slots == i) & (fresh_step // slots <= row_step)
            new = jnp.where(own, fresh_scores[here, :], -jnp.inf)
            top = jnp.maximum(
                jnp.max(kept, axis=1, keepdims=True), jnp.max(new, axis=1, keepdims=True)
            )
            kept = jnp.exp2((kept - top) * factor)
            new = jnp.exp2((new - top) * factor)
            total = jnp.sum(kept, axis=1, keepdims=True) + jnp.sum(new, axis=1, keepdims=True)
            values = dot(kept.astype(BF16), cache[i]) + dot(new.astype(BF16), fresh[...])
            values = values / total
            for s in range(STEPS):
                for g in range(kv_local):
                    at = s * heads + g * GROUPS
                    mixed[i * rows + at : i * rows + at + GROUPS, :] = values[
                        at : at + GROUPS, g * 2 * HD + HD : (g + 1) * 2 * HD
                    ]
        for s in range(STEPS):
            for h in range(heads):
                out[s * slots : (s + 1) * slots, h * HD : (h + 1) * HD] = mixed[
                    pl.ds(s * heads + h, slots, stride=rows), :
                ].astype(BF16)
    return pl.pallas_call(
        kernel,
        name="attend",
        out_shape=jax.ShapeDtypeStruct((STEPS * slots, heads * HD), BF16),
        in_specs=[VMEM] * 5,
        out_specs=VMEM,
        scratch_shapes=[
            pltpu.VMEM((requests, columns), BF16),
            pltpu.VMEM((slots * rows, HD), F32),
            pltpu.VMEM((STEPS * slots, width), BF16),
            pltpu.VMEM((slots * rows, width), BF16),
            pltpu.VMEM((slots * rows, cap), F32),
            pltpu.VMEM((slots * rows, STEPS * slots), F32),
            pltpu.VMEM((slots * rows, HD), F32),
        ],
        compiler_params=limit(6),
        cost_estimate=pl.CostEstimate(
            flops=4 * slots * rows * cap * width,
            bytes_accessed=slots * cap * width * 2,
            transcendentals=slots * rows * cap,
        ),
    )(lengths, slot_row, same, other, cache)


def matmul_cost(rows, depth, columns):
    return pl.CostEstimate(
        flops=2 * rows * depth * columns,
        bytes_accessed=2 * (rows * depth + depth * columns + rows * columns),
        transcendentals=0,
    )


def order_rows(source, same, other):
    requests = source.shape[0]
    rows = STEPS * requests
    depth = same.shape[1]
    slots = requests // lax.axis_size("att")
    ffn = lax.axis_size("ffn")
    owned = requests // ffn

    def kernel(source, same, other, out, gathered):
        place_gathered(same, other, gathered)
        me = lax.axis_index("ffn")
        for r in range(ffn):
            owner = jnp.bitwise_xor(me, r)
            first = source[pl.ds(pl.multiple_of(owner * owned, owned), owned), :]
            wanted = jnp.concatenate([first + step * slots for step in range(STEPS)], axis=0)
            at = lax.broadcasted_iota(jnp.int32, (STEPS * owned, rows), 1)
            pick = jnp.where(at == wanted, 1.0, 0.0).astype(BF16)
            here = slice(r * STEPS * owned, (r + 1) * STEPS * owned)
            out[here, :] = dot(pick, gathered[...]).astype(BF16)

    return pl.pallas_call(
        kernel,
        name="order_rows",
        out_shape=jax.ShapeDtypeStruct((rows, depth), BF16),
        in_specs=[VMEM] * 3,
        out_specs=VMEM,
        scratch_shapes=[pltpu.VMEM((rows, depth), BF16)],
        compiler_params=limit(4),
    )(source, same, other)


def multiply(rows, w, name):
    columns = w.shape[1]
    count, depth = rows.shape
    ffn = lax.axis_size("ffn")
    share = count // ffn
    rest = (ffn // 2 - 1) * share
    block = min(512, columns)

    def kernel(rows, w, own, near, keep, far):
        for j in range(columns // block):
            here = slice(j * block, (j + 1) * block)
            product = dot(rows[...], w[:, here])
            for r in range(ffn):
                part = product[r * share : (r + 1) * share]
                at = slice((r // 2 - 1) * share, r // 2 * share)
                if r == 0:
                    own[:, here] = part
                elif r == 1:
                    near[:, here] = part.astype(BF16)
                elif r % 2 == 0:
                    keep[at, here] = part
                else:
                    far[at, here] = part.astype(BF16)

    return pl.pallas_call(
        kernel,
        name=name,
        out_shape=[
            jax.ShapeDtypeStruct((share, columns), F32),
            jax.ShapeDtypeStruct((share, columns), BF16),
            jax.ShapeDtypeStruct((rest, columns), F32),
            jax.ShapeDtypeStruct((rest, columns), BF16),
        ],
        in_specs=[VMEM] * 2,
        out_specs=[VMEM] * 4,
        compiler_params=limit(4),
        cost_estimate=matmul_cost(count, depth, columns),
    )(rows, w)


def add_parts(keep, arrived, parts, first=BF16):
    rows, width = keep.shape
    share = rows // parts
    types = [first] + [BF16] * (parts - 1)

    def kernel(keep, arrived, *outs):
        for d, out in enumerate(outs):
            here = slice(d * share, (d + 1) * share)
            out[...] = (keep[here, :].astype(F32) + arrived[here, :].astype(F32)).astype(out.dtype)

    return pl.pallas_call(
        kernel,
        name="add_parts",
        out_shape=[jax.ShapeDtypeStruct((share, width), kind) for kind in types],
        in_specs=[VMEM] * 2,
        out_specs=[VMEM] * parts,
        compiler_params=limit(4),
    )(keep, arrived)


def add_residual(own, terms, after):
    rows, columns = terms[0].shape
    owned = rows // STEPS
    count = len(terms)

    def kernel(own, *refs):
        terms, out = refs[:count], refs[-1]
        total = terms[0][...]
        for term in terms[1:]:
            total = total + term[...].astype(F32)
        for step in range(STEPS):
            here = slice(step * owned, (step + 1) * owned)
            at = step * columns
            out[here, :] = (own[:, at : at + columns].astype(F32) + total[here]).astype(BF16)

    return pl.pallas_call(
        kernel,
        name="add_residual",
        out_shape=jax.ShapeDtypeStruct((rows, columns), BF16),
        in_specs=[VMEM] * (1 + count + len(after)),
        out_specs=VMEM,
        compiler_params=limit(4),
    )(own, *terms, *after)


def norm_rows(blocks, gain):
    count = len(blocks)
    size, depth = blocks[0].shape
    rows = size * count
    att = lax.axis_size("att")
    chips = att // 2
    share = rows // att

    def kernel(*refs):
        blocks, (gain, normed, tail, residual) = refs[:count], refs[count:]
        for r, block in enumerate(blocks):
            residual[r * size : (r + 1) * size, :] = block[...]
        me = lax.axis_index("att")
        chip, core = me // 2, lax.rem(me, 2)
        for side in range(2):
            for d in range(chips):
                owner = lax.rem(chip + d, chips) * 2 + lax.rem(core + side, 2)
                part = residual[pl.ds(pl.multiple_of(owner * share, share), share), :].astype(F32)
                here = slice((side * chips + d) * share, (side * chips + d + 1) * share)
                normed[here, :] = (part * gain[...]).astype(BF16)
                squares = jnp.sum(part * part, axis=1, keepdims=True)
                high = squares.astype(BF16).astype(F32)
                lane = lax.broadcasted_iota(jnp.int32, (share, HD), 1)
                tail[here, :] = jnp.where(lane == 0, high, squares - high).astype(BF16)

    return pl.pallas_call(
        kernel,
        name="norm_rows",
        out_shape=[
            jax.ShapeDtypeStruct((rows, depth), BF16),
            jax.ShapeDtypeStruct((rows, HD), BF16),
        ],
        in_specs=[VMEM] * (count + 1),
        out_specs=[VMEM] * 2,
        scratch_shapes=[pltpu.VMEM((rows, depth), BF16)],
        compiler_params=limit(4),
    )(*blocks, gain)


def widen(normed, tail, w_gate, w_up, first, count, after):
    rows, depth = normed.shape
    half = rows // 2
    extra = [] if tail is None else [tail]
    width = count * 2 * BLOCK + HD * len(extra)

    def kernel(normed, gate, up, *refs):
        keep, send = refs[-2:]
        for tail in refs[: len(extra)]:
            keep[:, count * 2 * BLOCK :] = tail[:half, :]
            send[:, count * 2 * BLOCK :] = tail[half:, :]
        for j in range(count):
            for which, w in enumerate((gate, up)):
                at = (first + j) * BLOCK
                product = dot(normed[...], w[:, at : at + BLOCK])
                here = slice((2 * j + which) * BLOCK, (2 * j + which + 1) * BLOCK)
                keep[:, here] = product[:half].astype(BF16)
                send[:, here] = product[half:].astype(BF16)

    return pl.pallas_call(
        kernel,
        name="widen",
        out_shape=[jax.ShapeDtypeStruct((half, width), BF16)] * 2,
        in_specs=[VMEM] * (3 + len(extra) + len(after)),
        out_specs=[VMEM] * 2,
        compiler_params=limit(4),
        cost_estimate=matmul_cost(rows, depth, count * 2 * BLOCK),
    )(normed, w_gate, w_up, *extra, *after)


def gate_rows(own, moved, scale, model, after=()):
    share, width = own.shape
    count = width // (2 * BLOCK)
    first = scale is None
    others = len(moved)

    def kernel(*refs):
        own, moved, rest = refs[0], refs[1 : 1 + others], refs[1 + others + len(after) :]

        def total(here):
            value = own[:, here]
            for part in moved:
                value = value + part[:, here].astype(F32)
            return value

        if first:
            out, scale = rest
            tail = total(slice(count * 2 * BLOCK, count * 2 * BLOCK + HD))
            factor = lax.rsqrt((tail[:, 0:1] + tail[:, 1:2]) / model + EPSILON)
            scale[...] = jnp.broadcast_to(factor, scale.shape)
        else:
            scale, out = rest
            factor = scale[:, 0:1]
        for j in range(count):
            gate = total(slice(2 * j * BLOCK, (2 * j + 1) * BLOCK)) * factor
            up = total(slice((2 * j + 1) * BLOCK, (2 * j + 2) * BLOCK)) * factor
            out[:, j * BLOCK : (j + 1) * BLOCK] = (gate / (1.0 + jnp.exp(-gate)) * up).astype(BF16)

    hidden = jax.ShapeDtypeStruct((share, count * BLOCK), BF16)
    kept = jax.ShapeDtypeStruct((share, HD), F32)
    return pl.pallas_call(
        kernel,
        name="gate",
        out_shape=[hidden, kept] if first else hidden,
        in_specs=[VMEM] * (1 + others + len(after) + (0 if first else 1)),
        out_specs=[VMEM] * 2 if first else VMEM,
        compiler_params=limit(4),
    )(own, *moved, *after, *([] if first else [scale]))


def place_rows(chunks):
    sizes = [same.shape[1] for same, _ in chunks]
    rows = 2 * chunks[0][0].shape[0]

    def kernel(*refs):
        out, at = refs[-1], 0
        for k, size in enumerate(sizes):
            place_gathered(refs[2 * k], refs[2 * k + 1], out, slice(at, at + size))
            at += size

    return pl.pallas_call(
        kernel,
        name="place_rows",
        out_shape=jax.ShapeDtypeStruct((rows, sum(sizes)), BF16),
        in_specs=[VMEM] * (2 * len(sizes)),
        out_specs=VMEM,
        compiler_params=limit(4),
    )(*[x for pair in chunks for x in pair])


def finish(residual, terms):
    def kernel(residual, *refs):
        terms, out = refs[:-1], refs[-1]
        total = terms[0][...]
        for term in terms[1:]:
            total = total + term[...].astype(F32)
        out[...] = (residual[...].astype(F32) + total).astype(BF16)

    return pl.pallas_call(
        kernel,
        name="finish",
        out_shape=jax.ShapeDtypeStruct(residual.shape, BF16),
        in_specs=[VMEM] * (1 + len(terms)),
        out_specs=VMEM,
        compiler_params=limit(4),
    )(residual, *terms)


def local(
    incoming, queries, new_kv, cache, lengths, slot_of, w_out, norm_gain, w_gate, w_up, w_down
):
    ffn = lax.axis_size("ffn")
    att = lax.axis_size("att")
    requests = slot_of.shape[0]
    slots = cache.shape[0]
    model = w_out.shape[1]
    width = w_gate.shape[1]
    owned = requests // ffn

    whole = lambda x: (x, 0, x.shape[-1])
    corner = lambda x: x[:8, :HD]

    qkv = jnp.concatenate([queries.reshape(slots, -1), new_kv.reshape(slots, -1)], axis=1)
    small = [slot_of.reshape(1, requests), lengths.reshape(1, slots)]
    cache, slot_row, lengths, token = load(
        [whole(x) for x in [cache] + small], corner(qkv), "load_cache"
    )
    same, other = gather_att(qkv, [token])
    attended = attend(lengths, slot_row, same, other, cache)
    w_out, token = load([whole(w_out)], corner(attended), "load_out")
    source = (slot_of // slots * (STEPS * slots) + slot_of % slots).reshape(requests, 1)
    rows = order_rows(source, *gather_att(attended, [token]))

    own = take_own(incoming, owned).reshape(owned, STEPS * model)
    product = multiply(rows, w_out, "project")
    w_gate, token = load([whole(w_gate)], corner(product[-1]), "load_gate")
    residual = add_residual(own, reduce_ffn(*product), [token])

    w_up, token = load([whole(w_up)], corner(residual), "load_up")
    normed, tail = norm_rows(gather_ffn(residual, [token]), norm_gain.reshape(1, model))
    edges = [width // BLOCK * k // CHUNKS for k in range(CHUNKS + 1)]
    pairs = []
    for k, (first, last) in enumerate(zip(edges[:-1], edges[1:])):
        after = [corner(keep)] if k == 1 else [corner(pairs[k - 2][1])] if k else []
        ends = tail if k == 0 else None
        keep, send = widen(normed, ends, w_gate, w_up, first, last - first, after)
        pairs.append(add_parts(keep, exchange(send, "att", 1), att // 2, F32))
    w_down, token = load([whole(w_down)], corner(keep), "load_down")
    chunks = []
    scale = None
    for k, (total, *away) in enumerate(pairs):
        moved = [shift(part, "att", 2 * (d + 1)) for d, part in enumerate(away)]
        if k == 0:
            hidden, scale = gate_rows(total, moved, None, model * att, [token])
        else:
            hidden = gate_rows(total, moved, scale, model * att)
        chunks.append(gather_att(hidden))
    hidden = place_rows(chunks)
    out = finish(residual, reduce_ffn(*multiply(hidden, w_down, "narrow")))
    return jnp.swapaxes(out.reshape(STEPS, owned, model), 0, 1)


def solution(mesh):
    return jax.shard_map(
        local,
        mesh=mesh,
        in_specs=(
            P("parts", None, "att"),
            P(("parts", "att"), None, "ffn"),
            P(("parts", "att"), None, "ffn"),
            P(("parts", "att"), None, "ffn"),
            P(("parts", "att")),
            P("parts"),
            P("ffn", "att"),
            P("att"),
            P("att", "ffn"),
            P("att", "ffn"),
            P("ffn", "att"),
        ),
        out_specs=P(("parts", "ffn"), None, "att"),
        check_vma=False,
    )
```

```python
import functools

import jax
import jax.numpy as jnp
from jax import lax
from jax.experimental import pallas as pl
from jax.experimental.pallas import tpu as pltpu
from jax.sharding import PartitionSpec as P

H = 64
KVH = 8
HD = 128
STEPS = 2
GROUPS = H // KVH
EPSILON = 1e-05
BLOCK = 256
CHUNKS = 3
F32 = jnp.float32
BF16 = jnp.bfloat16
MIB = 1024 * 1024


def dot(a, b):
    return jnp.dot(a, b, preferred_element_type=F32)

VMEM = pl.BlockSpec(memory_space=pltpu.VMEM)
ANY = pl.BlockSpec(memory_space=pl.ANY)


def shift(x, axis, d):
    n = lax.axis_size(axis)
    return lax.ppermute(x, axis, [(i, (i + d) % n) for i in range(n)])


def exchange(x, axis, bit):
    return lax.ppermute(x, axis, [(i, i ^ bit) for i in range(lax.axis_size(axis))])


def corner(x):
    return x[:8, :HD]


def limit(mib):
    return pltpu.CompilerParams(vmem_limit_bytes=mib * MIB)


def join(blocks, after=()):
    count = len(blocks)
    rows = [block.shape[0] for block in blocks]

    def kernel(*refs):
        out, at = refs[-1], 0
        for ref, size in zip(refs[:count], rows):
            out[at : at + size, :] = ref[...]
            at += size

    return pl.pallas_call(
        kernel,
        name="join",
        out_shape=jax.ShapeDtypeStruct((sum(rows), blocks[0].shape[1]), blocks[0].dtype),
        in_specs=[VMEM] * (count + len(after)),
        out_specs=VMEM,
        compiler_params=limit(4),
    )(*blocks, *after)


def gather_att(x, token=()):
    chips = lax.axis_size("att") // 2
    same = join([x] + [shift(x, "att", 2 * d) for d in range(1, chips)], token)
    return same, exchange(same, "att", 1)


def place_gathered(same, other, whole, columns=slice(None)):
    me, chips = lax.axis_index("att"), lax.axis_size("att") // 2
    rows = same.shape[0] // chips
    for d in range(chips):
        chip = lax.rem(me // 2 + chips - d, chips)
        for side, ref in enumerate((same, other)):
            source = chip * 2 + lax.rem(me + side, 2)
            at = pl.multiple_of(source * rows, rows)
            whole[pl.ds(at, rows), columns] = ref[d * rows : (d + 1) * rows, :]


def reduce_ffn(own, near, keep, far):
    sums = add_parts(keep, exchange(far, "ffn", 1), lax.axis_size("ffn") // 2 - 1)
    across = [exchange(part, "ffn", 2 * (k + 1)) for k, part in enumerate(sums)]
    return [own] + across + [exchange(join([near], [corner(sums[0])]), "ffn", 1)]


def gather_ffn(x, token=()):
    across = [exchange(x, "ffn", m) for m in range(2, lax.axis_size("ffn"), 2)]
    across = [join([block], token) for block in across]
    blocks = [x, exchange(x, "ffn", 1)]
    for block in across:
        blocks += [block, exchange(block, "ffn", 1)]
    return blocks


def hbm(x):
    return pltpu.with_memory_space_constraint(x, pltpu.HBM)


class Copies:
    def __init__(self, entries):
        self.entries = entries
        self.sources = [hbm(x) for x, _ in entries]
        self.shapes = [pltpu.VMEM((n,) + x.shape[1:], x.dtype) for x, n in entries]
        self.scratch = pltpu.SemaphoreType.DMA((len(entries), 8))
        self.bytes = sum(2 * x.size // x.shape[0] * n * x.dtype.itemsize for x, n in entries)

    def started(self, sources, targets, sems):
        copies = []
        for k, (x, rows) in enumerate(self.entries):
            parts = 8 if rows % 8 == 0 else 1
            size = rows // parts
            begin = 0 if rows == x.shape[0] else lax.axis_index("ffn") * rows
            for p in range(parts):
                copies.append(
                    pltpu.make_async_copy(
                        sources[k].at[pl.ds(begin + p * size, size)],
                        targets[k].at[pl.ds(p * size, size)],
                        sems.at[k, p],
                    )
                )
        for copy in copies:
            copy.start()
        return copies


def load(entries, name, after=()):
    work = Copies(entries)
    count = len(entries)

    def kernel(*refs):
        targets, token, sems = refs[-2 - count : -2], refs[-2], refs[-1]
        copies = work.started(refs[:count], targets, sems)
        token[...] = jnp.zeros_like(token)
        for copy in copies:
            copy.wait()

    return pl.pallas_call(
        kernel,
        name=name,
        out_shape=work.shapes + [jax.ShapeDtypeStruct((8, HD), F32)],
        in_specs=[ANY] * count + [VMEM] * len(after),
        out_specs=[VMEM] * (count + 1),
        scratch_shapes=[work.scratch],
        compiler_params=limit(1),
        cost_estimate=pl.CostEstimate(flops=0, bytes_accessed=work.bytes, transcendentals=0),
    )(*work.sources, *after)


def attend(lengths, slot_row, same, other, cache):
    slots, cap, width = cache.shape
    kv_local = width // (2 * HD)
    heads = kv_local * GROUPS
    rows = STEPS * heads
    requests = slot_row.shape[1]
    fresh_at = STEPS * heads * HD
    columns = fresh_at + STEPS * width
    factor = HD ** (-0.5) * 1.4426950408889634

    def kernel(lengths, slot_row, same, other, cache, out, *scratch):
        qkv, qs, fresh, wide, scores, fresh_scores, mixed = scratch
        place_gathered(same, other, qkv)
        base = lax.axis_index("att") * slots
        wanted = lax.broadcasted_iota(jnp.int32, (slots, requests), 0) + base
        pick = jnp.where(slot_row[...] == wanted, 1.0, 0.0).astype(BF16)
        mine = dot(pick, qkv[...])
        for s in range(STEPS):
            for h in range(heads):
                at = (s * heads + h) * HD
                qs[pl.ds(s * heads + h, slots, stride=rows), :] = mine[:, at : at + HD]
            fresh[s * slots : (s + 1) * slots, :] = mine[
                :, fresh_at + s * width : fresh_at + (s + 1) * width
            ].astype(BF16)
        group_of = lax.broadcasted_iota(jnp.int32, (slots * rows, HD), 0) % heads // GROUPS
        for g in range(kv_local):
            own = jnp.where(group_of == g, qs[...], 0.0)
            wide[:, g * 2 * HD : g * 2 * HD + HD] = own.astype(BF16)
            wide[:, g * 2 * HD + HD : (g + 1) * 2 * HD] = jnp.zeros((slots * rows, HD), BF16)

        across = (((1,), (1,)), ((), ()))
        fresh_scores[...] = lax.dot_general(
            wide[...], fresh[...], across, preferred_element_type=F32
        )
        for i in range(slots):
            here = slice(i * rows, (i + 1) * rows)
            scores[here, :] = lax.dot_general(
                wide[here, :], cache[i], across, preferred_element_type=F32
            )
        key_at = lax.broadcasted_iota(jnp.int32, (rows, cap), 1)
        fresh_step = lax.broadcasted_iota(jnp.int32, (rows, STEPS * slots), 1)
        row_step = lax.broadcasted_iota(jnp.int32, (rows, STEPS * slots), 0) // heads
        for i in range(slots):
            here = slice(i * rows, (i + 1) * rows)
            kept = jnp.where(key_at < lengths[:, i : i + 1], scores[here, :], -jnp.inf)
            own = (fresh_step % slots == i) & (fresh_step // slots <= row_step)
            new = jnp.where(own, fresh_scores[here, :], -jnp.inf)
            top = jnp.maximum(
                jnp.max(kept, axis=1, keepdims=True), jnp.max(new, axis=1, keepdims=True)
            )
            kept = jnp.exp2((kept - top) * factor)
            new = jnp.exp2((new - top) * factor)
            total = jnp.sum(kept, axis=1, keepdims=True) + jnp.sum(new, axis=1, keepdims=True)
            values = dot(kept.astype(BF16), cache[i]) + dot(new.astype(BF16), fresh[...])
            values = values / total
            for s in range(STEPS):
                for g in range(kv_local):
                    at = s * heads + g * GROUPS
                    mixed[i * rows + at : i * rows + at + GROUPS, :] = values[
                        at : at + GROUPS, g * 2 * HD + HD : (g + 1) * 2 * HD
                    ]
        for s in range(STEPS):
            for h in range(heads):
                out[s * slots : (s + 1) * slots, h * HD : (h + 1) * HD] = mixed[
                    pl.ds(s * heads + h, slots, stride=rows), :
                ].astype(BF16)
    return pl.pallas_call(
        kernel,
        name="attend",
        out_shape=jax.ShapeDtypeStruct((STEPS * slots, heads * HD), BF16),
        in_specs=[VMEM] * 5,
        out_specs=VMEM,
        scratch_shapes=[
            pltpu.VMEM((requests, columns), BF16),
            pltpu.VMEM((slots * rows, HD), F32),
            pltpu.VMEM((STEPS * slots, width), BF16),
            pltpu.VMEM((slots * rows, width), BF16),
            pltpu.VMEM((slots * rows, cap), F32),
            pltpu.VMEM((slots * rows, STEPS * slots), F32),
            pltpu.VMEM((slots * rows, HD), F32),
        ],
        compiler_params=limit(6),
        cost_estimate=pl.CostEstimate(
            flops=4 * slots * rows * cap * width,
            bytes_accessed=slots * cap * width * 2,
            transcendentals=slots * rows * cap,
        ),
    )(lengths, slot_row, same, other, cache)


def matmul_cost(rows, depth, columns):
    return pl.CostEstimate(
        flops=2 * rows * depth * columns,
        bytes_accessed=2 * (rows * depth + depth * columns + rows * columns),
        transcendentals=0,
    )


def order_rows(slot_row, same, other):
    requests = slot_row.shape[1]
    rows = STEPS * requests
    depth = same.shape[1]
    slots = requests // lax.axis_size("att")
    ffn = lax.axis_size("ffn")
    owned = requests // ffn

    def kernel(slot_row, same, other, out, gathered, natural):
        place_gathered(same, other, gathered)
        slot = slot_row[...]
        first = lax.div(slot, slots) * (STEPS * slots) + lax.rem(slot, slots)
        at = lax.broadcasted_iota(jnp.int32, (rows, requests), 0)
        me = lax.axis_index("ffn")
        for step in range(STEPS):
            pick = jnp.where(at == first + step * slots, 1.0, 0.0).astype(BF16)
            picked = lax.dot_general(
                pick, gathered[...], (((0,), (0,)), ((), ())), preferred_element_type=F32
            )
            natural[...] = picked.astype(BF16)
            for r in range(ffn):
                owner = jnp.bitwise_xor(me, r)
                here = slice((r * STEPS + step) * owned, (r * STEPS + step + 1) * owned)
                out[here, :] = natural[pl.ds(pl.multiple_of(owner * owned, owned), owned), :]

    return pl.pallas_call(
        kernel,
        name="order_rows",
        out_shape=jax.ShapeDtypeStruct((rows, depth), BF16),
        in_specs=[VMEM] * 3,
        out_specs=VMEM,
        scratch_shapes=[pltpu.VMEM((rows, depth), BF16), pltpu.VMEM((requests, depth), BF16)],
        compiler_params=limit(4),
    )(slot_row, same, other)


def multiply(rows, w, name):
    columns = w.shape[1]
    count, depth = rows.shape
    ffn = lax.axis_size("ffn")
    share = count // ffn
    rest = (ffn // 2 - 1) * share
    block = min(512, columns)

    def kernel(rows, w, own, near, keep, far):
        for j in range(columns // block):
            here = slice(j * block, (j + 1) * block)
            product = dot(rows[...], w[:, here])
            for r in range(ffn):
                part = product[r * share : (r + 1) * share]
                at = slice((r // 2 - 1) * share, r // 2 * share)
                if r == 0:
                    own[:, here] = part
                elif r == 1:
                    near[:, here] = part.astype(BF16)
                elif r % 2 == 0:
                    keep[at, here] = part
                else:
                    far[at, here] = part.astype(BF16)

    return pl.pallas_call(
        kernel,
        name=name,
        out_shape=[
            jax.ShapeDtypeStruct((share, columns), F32),
            jax.ShapeDtypeStruct((share, columns), BF16),
            jax.ShapeDtypeStruct((rest, columns), F32),
            jax.ShapeDtypeStruct((rest, columns), BF16),
        ],
        in_specs=[VMEM] * 2,
        out_specs=[VMEM] * 4,
        compiler_params=limit(4),
        cost_estimate=matmul_cost(count, depth, columns),
    )(rows, w)


def add_parts(keep, arrived, parts, first=BF16):
    rows, width = keep.shape
    share = rows // parts
    types = [first] + [BF16] * (parts - 1)

    def kernel(keep, arrived, *outs):
        for d, out in enumerate(outs):
            here = slice(d * share, (d + 1) * share)
            out[...] = (keep[here, :].astype(F32) + arrived[here, :].astype(F32)).astype(out.dtype)

    return pl.pallas_call(
        kernel,
        name="add_parts",
        out_shape=[jax.ShapeDtypeStruct((share, width), kind) for kind in types],
        in_specs=[VMEM] * 2,
        out_specs=[VMEM] * parts,
        compiler_params=limit(4),
    )(keep, arrived)


def add_residual(own, terms, after):
    rows, columns = terms[0].shape
    owned = rows // STEPS
    count = len(terms)

    def kernel(own, *refs):
        terms, out = refs[:count], refs[-1]
        total = terms[0][...]
        for term in terms[1:]:
            total = total + term[...].astype(F32)
        for step in range(STEPS):
            here = slice(step * owned, (step + 1) * owned)
            at = step * columns
            out[here, :] = (own[:, at : at + columns].astype(F32) + total[here]).astype(BF16)

    return pl.pallas_call(
        kernel,
        name="add_residual",
        out_shape=jax.ShapeDtypeStruct((rows, columns), BF16),
        in_specs=[VMEM] * (1 + count + len(after)),
        out_specs=VMEM,
        compiler_params=limit(4),
    )(own, *terms, *after)


def norm_rows(blocks, gain):
    count = len(blocks)
    size, depth = blocks[0].shape
    rows = size * count
    att = lax.axis_size("att")
    chips = att // 2
    share = rows // att

    def kernel(*refs):
        blocks, (gain, normed, tail, residual) = refs[:count], refs[count:]
        for r, block in enumerate(blocks):
            residual[r * size : (r + 1) * size, :] = block[...]
        me = lax.axis_index("att")
        chip, core = me // 2, lax.rem(me, 2)
        for side in range(2):
            for d in range(chips):
                owner = lax.rem(chip + d, chips) * 2 + lax.rem(core + side, 2)
                part = residual[pl.ds(pl.multiple_of(owner * share, share), share), :].astype(F32)
                here = slice((side * chips + d) * share, (side * chips + d + 1) * share)
                normed[here, :] = (part * gain[...]).astype(BF16)
                squares = jnp.sum(part * part, axis=1, keepdims=True)
                high = squares.astype(BF16).astype(F32)
                lane = lax.broadcasted_iota(jnp.int32, (share, HD), 1)
                tail[here, :] = jnp.where(lane == 0, high, squares - high).astype(BF16)

    return pl.pallas_call(
        kernel,
        name="norm_rows",
        out_shape=[
            jax.ShapeDtypeStruct((rows, depth), BF16),
            jax.ShapeDtypeStruct((rows, HD), BF16),
        ],
        in_specs=[VMEM] * (count + 1),
        out_specs=[VMEM] * 2,
        scratch_shapes=[pltpu.VMEM((rows, depth), BF16)],
        compiler_params=limit(4),
    )(*blocks, gain)


def widen(normed, tail, w_gate, w_up, first, count, after):
    rows, depth = normed.shape
    half = rows // 2
    width = count * 2 * BLOCK + HD

    def kernel(normed, tail, gate, up, *refs):
        keep, send = refs[-2:]
        keep[:, count * 2 * BLOCK :] = tail[:half, :]
        send[:, count * 2 * BLOCK :] = tail[half:, :]
        for j in range(count):
            for which, w in enumerate((gate, up)):
                at = (first + j) * BLOCK
                product = dot(normed[...], w[:, at : at + BLOCK])
                here = slice((2 * j + which) * BLOCK, (2 * j + which + 1) * BLOCK)
                keep[:, here] = product[:half].astype(BF16)
                send[:, here] = product[half:].astype(BF16)

    return pl.pallas_call(
        kernel,
        name="widen",
        out_shape=[jax.ShapeDtypeStruct((half, width), BF16)] * 2,
        in_specs=[VMEM] * (4 + len(after)),
        out_specs=[VMEM] * 2,
        compiler_params=limit(4),
        cost_estimate=matmul_cost(rows, depth, count * 2 * BLOCK),
    )(normed, tail, w_gate, w_up, *after)


def gate_rows(own, moved, model, after=()):
    share, width = own.shape
    count = width // (2 * BLOCK)
    others = len(moved)

    def kernel(*refs):
        own, moved, out = refs[0], refs[1 : 1 + others], refs[-1]

        def total(here):
            value = own[:, here]
            for part in moved:
                value = value + part[:, here].astype(F32)
            return value

        tail = total(slice(count * 2 * BLOCK, count * 2 * BLOCK + HD))
        factor = lax.rsqrt((tail[:, 0:1] + tail[:, 1:2]) / model + EPSILON)
        for j in range(count):
            gate = total(slice(2 * j * BLOCK, (2 * j + 1) * BLOCK)) * factor
            up = total(slice((2 * j + 1) * BLOCK, (2 * j + 2) * BLOCK)) * factor
            out[:, j * BLOCK : (j + 1) * BLOCK] = (gate / (1.0 + jnp.exp(-gate)) * up).astype(BF16)

    return pl.pallas_call(
        kernel,
        name="gate",
        out_shape=jax.ShapeDtypeStruct((share, count * BLOCK), BF16),
        in_specs=[VMEM] * (1 + others + len(after)),
        out_specs=VMEM,
        compiler_params=limit(4),
    )(own, *moved, *after)


def place_rows(chunks):
    sizes = [same.shape[1] for same, _ in chunks]
    rows = 2 * chunks[0][0].shape[0]

    def kernel(*refs):
        out, at = refs[-1], 0
        for k, size in enumerate(sizes):
            place_gathered(refs[2 * k], refs[2 * k + 1], out, slice(at, at + size))
            at += size

    return pl.pallas_call(
        kernel,
        name="place_rows",
        out_shape=jax.ShapeDtypeStruct((rows, sum(sizes)), BF16),
        in_specs=[VMEM] * (2 * len(sizes)),
        out_specs=VMEM,
        compiler_params=limit(4),
    )(*[x for pair in chunks for x in pair])


def finish(residual, terms):
    def kernel(residual, *refs):
        terms, out = refs[:-1], refs[-1]
        total = terms[0][...]
        for term in terms[1:]:
            total = total + term[...].astype(F32)
        out[...] = (residual[...].astype(F32) + total).astype(BF16)

    return pl.pallas_call(
        kernel,
        name="finish",
        out_shape=jax.ShapeDtypeStruct(residual.shape, BF16),
        in_specs=[VMEM] * (1 + len(terms)),
        out_specs=VMEM,
        compiler_params=limit(4),
    )(residual, *terms)


def local(
    incoming, queries, new_kv, cache, lengths, slot_of, w_out, norm_gain, w_gate, w_up, w_down
):
    ffn = lax.axis_size("ffn")
    att = lax.axis_size("att")
    requests = slot_of.shape[0]
    slots = cache.shape[0]
    model = w_out.shape[1]
    width = w_gate.shape[1]
    owned = requests // ffn

    whole = lambda x: (x, x.shape[0])
    queries, new_kv, token = load([whole(queries), whole(new_kv)], "load_new")
    qkv = jnp.concatenate([queries.reshape(slots, -1), new_kv.reshape(slots, -1)], axis=1)
    small = [whole(slot_of.reshape(1, requests)), whole(lengths.reshape(1, slots))]
    cache, slot_row, lengths, own, token = load(
        [whole(cache)] + small + [(incoming, owned)], "load_cache", [corner(qkv)]
    )
    own = own.reshape(owned, STEPS * model)
    same, other = gather_att(qkv, [token])
    attended = attend(lengths, slot_row, same, other, cache)
    w_out, token = load([whole(w_out)], "load_out", [corner(attended)])
    rows = order_rows(slot_row, *gather_att(attended, [token]))
    product = multiply(rows, w_out, "project")
    w_gate, token = load([whole(w_gate)], "load_gate", [corner(product[-1])])
    residual = add_residual(own, reduce_ffn(*product), [token])

    w_up, token = load([whole(w_up)], "load_up", [corner(residual)])
    normed, tail = norm_rows(gather_ffn(residual, [token]), norm_gain.reshape(1, model))
    edges = [-(-(width // BLOCK) * k // CHUNKS) for k in range(CHUNKS + 1)]
    pairs = []
    for k, (first, last) in enumerate(zip(edges[:-1], edges[1:])):
        after = [corner(keep)] if k == 1 else [corner(pairs[k - 2][1])] if k else []
        keep, send = widen(normed, tail, w_gate, w_up, first, last - first, after)
        pairs.append(add_parts(keep, exchange(send, "att", 1), att // 2, F32))
    moved = [
        [shift(part, "att", 2 * (d + 1)) for d, part in enumerate(away)] for _, *away in pairs
    ]
    w_down, token = load([whole(w_down)], "load_down", [corner(moved[0][0])])
    chunks = [
        gather_att(gate_rows(pair[0], parts, model * att, [token]))
        for pair, parts in zip(pairs, moved)
    ]
    hidden = place_rows(chunks)
    out = finish(residual, reduce_ffn(*multiply(hidden, w_down, "narrow")))
    return jnp.swapaxes(out.reshape(STEPS, owned, model), 0, 1)


def solution(mesh):
    return jax.shard_map(
        local,
        mesh=mesh,
        in_specs=(
            P("parts", None, "att"),
            P(("parts", "att"), None, "ffn"),
            P(("parts", "att"), None, "ffn"),
            P(("parts", "att"), None, "ffn"),
            P(("parts", "att")),
            P("parts"),
            P("ffn", "att"),
            P("att"),
            P("att", "ffn"),
            P("att", "ffn"),
            P("ffn", "att"),
        ),
        out_specs=P(("parts", "ffn"), None, "att"),
        check_vma=False,
    )
```

```python
import functools

import jax
import jax.numpy as jnp
from jax import lax
from jax.experimental import pallas as pl
from jax.experimental.pallas import tpu as pltpu
from jax.sharding import PartitionSpec as P

H = 64
KVH = 8
HD = 128
STEPS = 2
GROUPS = H // KVH
EPSILON = 1e-05
BLOCK = 256
CHUNKS = 2
F32 = jnp.float32
BF16 = jnp.bfloat16
MIB = 1024 * 1024


def dot(a, b):
    return jnp.dot(a, b, preferred_element_type=F32)

VMEM = pl.BlockSpec(memory_space=pltpu.VMEM)
ANY = pl.BlockSpec(memory_space=pl.ANY)


def shift(x, axis, d):
    n = lax.axis_size(axis)
    return lax.ppermute(x, axis, [(i, (i + d) % n) for i in range(n)])


def exchange(x, axis, bit):
    return lax.ppermute(x, axis, [(i, i ^ bit) for i in range(lax.axis_size(axis))])


def corner(x):
    return x[:8, :HD]


def limit(mib):
    return pltpu.CompilerParams(vmem_limit_bytes=mib * MIB)


def join(blocks, after=()):
    count = len(blocks)
    rows = [block.shape[0] for block in blocks]

    def kernel(*refs):
        out, at = refs[-1], 0
        for ref, size in zip(refs[:count], rows):
            out[at : at + size, :] = ref[...]
            at += size

    return pl.pallas_call(
        kernel,
        name="join",
        out_shape=jax.ShapeDtypeStruct((sum(rows), blocks[0].shape[1]), blocks[0].dtype),
        in_specs=[VMEM] * (count + len(after)),
        out_specs=VMEM,
        compiler_params=limit(4),
    )(*blocks, *after)


def gather_att(x, token=()):
    chips = lax.axis_size("att") // 2
    same = join([x] + [shift(x, "att", 2 * d) for d in range(1, chips)], token)
    return same, exchange(same, "att", 1)


def place_gathered(same, other, whole, columns=slice(None)):
    me, chips = lax.axis_index("att"), lax.axis_size("att") // 2
    rows = same.shape[0] // chips
    for d in range(chips):
        chip = lax.rem(me // 2 + chips - d, chips)
        for side, ref in enumerate((same, other)):
            source = chip * 2 + lax.rem(me + side, 2)
            at = pl.multiple_of(source * rows, rows)
            whole[pl.ds(at, rows), columns] = ref[d * rows : (d + 1) * rows, :]


def reduce_ffn(own, *others):
    masks = range(len(others), 0, -1)
    return [own] + [exchange(others[mask - 1], "ffn", mask) for mask in masks]


def gather_ffn(x, token):
    across = [exchange(x, "ffn", m) for m in range(2, lax.axis_size("ffn"), 2)]
    across = [join([block], [token]) for block in across]
    blocks = [x, exchange(x, "ffn", 1)]
    for block in across:
        blocks += [block, exchange(block, "ffn", 1)]
    return blocks


def hbm(x):
    return pltpu.with_memory_space_constraint(x, pltpu.HBM)


class Copies:
    def __init__(self, entries):
        self.entries = entries
        self.sources = [hbm(x) for x, _ in entries]
        self.shapes = [pltpu.VMEM((n,) + x.shape[1:], x.dtype) for x, n in entries]
        self.scratch = pltpu.SemaphoreType.DMA((len(entries), 8))
        self.bytes = sum(2 * x.size // x.shape[0] * n * x.dtype.itemsize for x, n in entries)

    def started(self, sources, targets, sems):
        copies = []
        for k, (x, rows) in enumerate(self.entries):
            parts = 8 if rows % 8 == 0 else 1
            size = rows // parts
            begin = 0 if rows == x.shape[0] else lax.axis_index("ffn") * rows
            for p in range(parts):
                copies.append(
                    pltpu.make_async_copy(
                        sources[k].at[pl.ds(begin + p * size, size)],
                        targets[k].at[pl.ds(p * size, size)],
                        sems.at[k, p],
                    )
                )
        for copy in copies:
            copy.start()
        return copies


def load(entries, name, after=()):
    work = Copies(entries)
    count = len(entries)

    def kernel(*refs):
        targets, token, sems = refs[-2 - count : -2], refs[-2], refs[-1]
        copies = work.started(refs[:count], targets, sems)
        token[...] = jnp.zeros_like(token)
        for copy in copies:
            copy.wait()

    return pl.pallas_call(
        kernel,
        name=name,
        out_shape=work.shapes + [jax.ShapeDtypeStruct((8, HD), F32)],
        in_specs=[ANY] * count + [VMEM] * len(after),
        out_specs=[VMEM] * (count + 1),
        scratch_shapes=[work.scratch],
        compiler_params=limit(1),
        cost_estimate=pl.CostEstimate(flops=0, bytes_accessed=work.bytes, transcendentals=0),
    )(*work.sources, *after)


def attend(lengths, slot_row, same, other, cache):
    slots, cap, width = cache.shape
    kv_local = width // (2 * HD)
    heads = kv_local * GROUPS
    rows = STEPS * heads
    requests = slot_row.shape[1]
    fresh_at = STEPS * heads * HD
    columns = fresh_at + STEPS * width
    factor = HD ** (-0.5) * 1.4426950408889634

    def kernel(lengths, slot_row, same, other, cache, out, *scratch):
        qkv, qs, fresh, wide, scores, fresh_scores, mixed = scratch
        place_gathered(same, other, qkv)
        base = lax.axis_index("att") * slots
        wanted = lax.broadcasted_iota(jnp.int32, (slots, requests), 0) + base
        pick = jnp.where(slot_row[...] == wanted, 1.0, 0.0).astype(BF16)
        mine = dot(pick, qkv[...])
        for s in range(STEPS):
            for h in range(heads):
                at = (s * heads + h) * HD
                qs[pl.ds(s * heads + h, slots, stride=rows), :] = mine[:, at : at + HD]
            fresh[s * slots : (s + 1) * slots, :] = mine[
                :, fresh_at + s * width : fresh_at + (s + 1) * width
            ].astype(BF16)
        group_of = lax.broadcasted_iota(jnp.int32, (slots * rows, HD), 0) % heads // GROUPS
        for g in range(kv_local):
            own = jnp.where(group_of == g, qs[...], 0.0)
            wide[:, g * 2 * HD : g * 2 * HD + HD] = own.astype(BF16)
            wide[:, g * 2 * HD + HD : (g + 1) * 2 * HD] = jnp.zeros((slots * rows, HD), BF16)

        across = (((1,), (1,)), ((), ()))
        fresh_scores[...] = lax.dot_general(
            wide[...], fresh[...], across, preferred_element_type=F32
        )
        for i in range(slots):
            here = slice(i * rows, (i + 1) * rows)
            scores[here, :] = lax.dot_general(
                wide[here, :], cache[i], across, preferred_element_type=F32
            )
        key_at = lax.broadcasted_iota(jnp.int32, (rows, cap), 1)
        fresh_step = lax.broadcasted_iota(jnp.int32, (rows, STEPS * slots), 1)
        row_step = lax.broadcasted_iota(jnp.int32, (rows, STEPS * slots), 0) // heads
        for i in range(slots):
            here = slice(i * rows, (i + 1) * rows)
            kept = jnp.where(key_at < lengths[:, i : i + 1], scores[here, :], -jnp.inf)
            own = (fresh_step % slots == i) & (fresh_step // slots <= row_step)
            new = jnp.where(own, fresh_scores[here, :], -jnp.inf)
            top = jnp.maximum(
                jnp.max(kept, axis=1, keepdims=True), jnp.max(new, axis=1, keepdims=True)
            )
            kept = jnp.exp2((kept - top) * factor)
            new = jnp.exp2((new - top) * factor)
            total = jnp.sum(kept, axis=1, keepdims=True) + jnp.sum(new, axis=1, keepdims=True)
            values = dot(kept.astype(BF16), cache[i]) + dot(new.astype(BF16), fresh[...])
            values = values / total
            for s in range(STEPS):
                for g in range(kv_local):
                    at = s * heads + g * GROUPS
                    mixed[i * rows + at : i * rows + at + GROUPS, :] = values[
                        at : at + GROUPS, g * 2 * HD + HD : (g + 1) * 2 * HD
                    ]
        for s in range(STEPS):
            for h in range(heads):
                out[s * slots : (s + 1) * slots, h * HD : (h + 1) * HD] = mixed[
                    pl.ds(s * heads + h, slots, stride=rows), :
                ].astype(BF16)
    return pl.pallas_call(
        kernel,
        name="attend",
        out_shape=jax.ShapeDtypeStruct((STEPS * slots, heads * HD), BF16),
        in_specs=[VMEM] * 5,
        out_specs=VMEM,
        scratch_shapes=[
            pltpu.VMEM((requests, columns), BF16),
            pltpu.VMEM((slots * rows, HD), F32),
            pltpu.VMEM((STEPS * slots, width), BF16),
            pltpu.VMEM((slots * rows, width), BF16),
            pltpu.VMEM((slots * rows, cap), F32),
            pltpu.VMEM((slots * rows, STEPS * slots), F32),
            pltpu.VMEM((slots * rows, HD), F32),
        ],
        compiler_params=limit(6),
        cost_estimate=pl.CostEstimate(
            flops=4 * slots * rows * cap * width,
            bytes_accessed=slots * cap * width * 2,
            transcendentals=slots * rows * cap,
        ),
    )(lengths, slot_row, same, other, cache)


def matmul_cost(rows, depth, columns):
    return pl.CostEstimate(
        flops=2 * rows * depth * columns,
        bytes_accessed=2 * (rows * depth + depth * columns + rows * columns),
        transcendentals=0,
    )


def order_rows(slot_row, same, other):
    requests = slot_row.shape[1]
    rows = STEPS * requests
    depth = same.shape[1]
    slots = requests // lax.axis_size("att")
    ffn = lax.axis_size("ffn")
    owned = requests // ffn

    def kernel(slot_row, same, other, out, gathered, natural):
        place_gathered(same, other, gathered)
        slot = slot_row[...]
        first = lax.div(slot, slots) * (STEPS * slots) + lax.rem(slot, slots)
        at = lax.broadcasted_iota(jnp.int32, (rows, requests), 0)
        me = lax.axis_index("ffn")
        for step in range(STEPS):
            pick = jnp.where(at == first + step * slots, 1.0, 0.0).astype(BF16)
            picked = lax.dot_general(
                pick, gathered[...], (((0,), (0,)), ((), ())), preferred_element_type=F32
            )
            natural[...] = picked.astype(BF16)
            for r in range(ffn):
                owner = jnp.bitwise_xor(me, r)
                here = slice((r * STEPS + step) * owned, (r * STEPS + step + 1) * owned)
                out[here, :] = natural[pl.ds(pl.multiple_of(owner * owned, owned), owned), :]

    return pl.pallas_call(
        kernel,
        name="order_rows",
        out_shape=jax.ShapeDtypeStruct((rows, depth), BF16),
        in_specs=[VMEM] * 3,
        out_specs=VMEM,
        scratch_shapes=[pltpu.VMEM((rows, depth), BF16), pltpu.VMEM((requests, depth), BF16)],
        compiler_params=limit(4),
    )(slot_row, same, other)


def multiply(rows, w, name):
    columns = w.shape[1]
    count, depth = rows.shape
    ffn = lax.axis_size("ffn")
    share = count // ffn
    block = min(512, columns)

    def kernel(rows, w, *outs):
        for j in range(columns // block):
            here = slice(j * block, (j + 1) * block)
            product = dot(rows[...], w[:, here])
            for r, out in enumerate(outs):
                out[:, here] = product[r * share : (r + 1) * share].astype(out.dtype)

    return pl.pallas_call(
        kernel,
        name=name,
        out_shape=[
            jax.ShapeDtypeStruct((share, columns), BF16 if r else F32) for r in range(ffn)
        ],
        in_specs=[VMEM] * 2,
        out_specs=[VMEM] * ffn,
        compiler_params=limit(4),
        cost_estimate=matmul_cost(count, depth, columns),
    )(rows, w)


def add_parts(keep, arrived, parts, first=BF16):
    rows, width = keep.shape
    share = rows // parts
    types = [first] + [BF16] * (parts - 1)

    def kernel(keep, arrived, *outs):
        for d, out in enumerate(outs):
            here = slice(d * share, (d + 1) * share)
            out[...] = (keep[here, :].astype(F32) + arrived[here, :].astype(F32)).astype(out.dtype)

    return pl.pallas_call(
        kernel,
        name="add_parts",
        out_shape=[jax.ShapeDtypeStruct((share, width), kind) for kind in types],
        in_specs=[VMEM] * 2,
        out_specs=[VMEM] * parts,
        compiler_params=limit(4),
    )(keep, arrived)


def add_residual(own, terms, after):
    rows, columns = terms[0].shape
    owned = rows // STEPS
    count = len(terms)

    def kernel(own, *refs):
        terms, out = refs[:count], refs[-1]
        total = terms[0][...]
        for term in terms[1:]:
            total = total + term[...].astype(F32)
        for step in range(STEPS):
            here = slice(step * owned, (step + 1) * owned)
            at = step * columns
            out[here, :] = (own[:, at : at + columns].astype(F32) + total[here]).astype(BF16)

    return pl.pallas_call(
        kernel,
        name="add_residual",
        out_shape=jax.ShapeDtypeStruct((rows, columns), BF16),
        in_specs=[VMEM] * (1 + count + len(after)),
        out_specs=VMEM,
        compiler_params=limit(4),
    )(own, *terms, *after)


def norm_rows(blocks, gain):
    count = len(blocks)
    size, depth = blocks[0].shape
    rows = size * count
    att = lax.axis_size("att")
    chips = att // 2
    share = rows // att

    def kernel(*refs):
        blocks, (gain, normed, tail, residual) = refs[:count], refs[count:]
        for r, block in enumerate(blocks):
            residual[r * size : (r + 1) * size, :] = block[...]
        me = lax.axis_index("att")
        chip, core = me // 2, lax.rem(me, 2)
        for side in range(2):
            for d in range(chips):
                owner = lax.rem(chip + d, chips) * 2 + lax.rem(core + side, 2)
                part = residual[pl.ds(pl.multiple_of(owner * share, share), share), :].astype(F32)
                here = slice((side * chips + d) * share, (side * chips + d + 1) * share)
                normed[here, :] = (part * gain[...]).astype(BF16)
                squares = jnp.sum(part * part, axis=1, keepdims=True)
                high = squares.astype(BF16).astype(F32)
                lane = lax.broadcasted_iota(jnp.int32, (share, HD), 1)
                tail[here, :] = jnp.where(lane == 0, high, squares - high).astype(BF16)

    return pl.pallas_call(
        kernel,
        name="norm_rows",
        out_shape=[
            jax.ShapeDtypeStruct((rows, depth), BF16),
            jax.ShapeDtypeStruct((rows, HD), BF16),
        ],
        in_specs=[VMEM] * (count + 1),
        out_specs=[VMEM] * 2,
        scratch_shapes=[pltpu.VMEM((rows, depth), BF16)],
        compiler_params=limit(4),
    )(*blocks, gain)


def widen(normed, tail, w_gate, w_up, first, count, after):
    rows, depth = normed.shape
    half = rows // 2
    width = count * 2 * BLOCK + HD

    def kernel(normed, tail, gate, up, *refs):
        keep, send = refs[-2:]
        keep[:, count * 2 * BLOCK :] = tail[:half, :]
        send[:, count * 2 * BLOCK :] = tail[half:, :]
        for j in range(count):
            for which, w in enumerate((gate, up)):
                at = (first + j) * BLOCK
                product = dot(normed[...], w[:, at : at + BLOCK])
                here = slice((2 * j + which) * BLOCK, (2 * j + which + 1) * BLOCK)
                keep[:, here] = product[:half].astype(BF16)
                send[:, here] = product[half:].astype(BF16)

    return pl.pallas_call(
        kernel,
        name="widen",
        out_shape=[jax.ShapeDtypeStruct((half, width), BF16)] * 2,
        in_specs=[VMEM] * (4 + len(after)),
        out_specs=[VMEM] * 2,
        compiler_params=limit(4),
    )(normed, tail, w_gate, w_up, *after)


def gate_rows(own, moved, model, after):
    share, width = own.shape
    count = width // (2 * BLOCK)
    others = len(moved)

    def kernel(*refs):
        own, moved, out = refs[0], refs[1 : 1 + others], refs[-1]

        def total(here):
            value = own[:, here]
            for part in moved:
                value = value + part[:, here].astype(F32)
            return value

        tail = total(slice(count * 2 * BLOCK, count * 2 * BLOCK + HD))
        factor = lax.rsqrt((tail[:, 0:1] + tail[:, 1:2]) / model + EPSILON)
        for j in range(count):
            gate = total(slice(2 * j * BLOCK, (2 * j + 1) * BLOCK)) * factor
            up = total(slice((2 * j + 1) * BLOCK, (2 * j + 2) * BLOCK)) * factor
            out[:, j * BLOCK : (j + 1) * BLOCK] = (gate / (1.0 + jnp.exp(-gate)) * up).astype(BF16)

    return pl.pallas_call(
        kernel,
        name="gate",
        out_shape=jax.ShapeDtypeStruct((share, count * BLOCK), BF16),
        in_specs=[VMEM] * (2 + others),
        out_specs=VMEM,
        compiler_params=limit(4),
    )(own, *moved, after)


def place_rows(chunks):
    sizes = [same.shape[1] for same, _ in chunks]
    rows = 2 * chunks[0][0].shape[0]

    def kernel(*refs):
        out, at = refs[-1], 0
        for k, size in enumerate(sizes):
            place_gathered(refs[2 * k], refs[2 * k + 1], out, slice(at, at + size))
            at += size

    return pl.pallas_call(
        kernel,
        name="place_rows",
        out_shape=jax.ShapeDtypeStruct((rows, sum(sizes)), BF16),
        in_specs=[VMEM] * (2 * len(sizes)),
        out_specs=VMEM,
        compiler_params=limit(4),
    )(*[x for pair in chunks for x in pair])


def finish(residual, terms):
    def kernel(residual, *refs):
        terms, out = refs[:-1], refs[-1]
        total = terms[0][...]
        for term in terms[1:]:
            total = total + term[...].astype(F32)
        out[...] = (residual[...].astype(F32) + total).astype(BF16)

    return pl.pallas_call(
        kernel,
        name="finish",
        out_shape=jax.ShapeDtypeStruct(residual.shape, BF16),
        in_specs=[VMEM] * (1 + len(terms)),
        out_specs=VMEM,
        compiler_params=limit(4),
    )(residual, *terms)


def local(
    incoming, queries, new_kv, cache, lengths, slot_of, w_out, norm_gain, w_gate, w_up, w_down
):
    ffn = lax.axis_size("ffn")
    att = lax.axis_size("att")
    requests = slot_of.shape[0]
    slots = cache.shape[0]
    model = w_out.shape[1]
    width = w_gate.shape[1]
    owned = requests // ffn

    whole = lambda x: (x, x.shape[0])
    queries, new_kv, token = load([whole(queries), whole(new_kv)], "load_new")
    qkv = jnp.concatenate([queries.reshape(slots, -1), new_kv.reshape(slots, -1)], axis=1)
    small = [whole(slot_of.reshape(1, requests)), whole(lengths.reshape(1, slots))]
    cache, slot_row, lengths, own, token = load(
        [whole(cache)] + small + [(incoming, owned)], "load_cache", [corner(qkv)]
    )
    own = own.reshape(owned, STEPS * model)
    same, other = gather_att(qkv, [token])
    attended = attend(lengths, slot_row, same, other, cache)
    w_out, token = load([whole(w_out)], "load_out", [corner(attended)])
    rows = order_rows(slot_row, *gather_att(attended, [token]))
    product = multiply(rows, w_out, "project")
    w_gate, token = load([whole(w_gate)], "load_gate", [corner(product[-1])])
    residual = add_residual(own, reduce_ffn(*product), [token])

    w_up, token = load([whole(w_up)], "load_up", [corner(residual)])
    normed, tail = norm_rows(gather_ffn(residual, token), norm_gain.reshape(1, model))
    edges = [-(-(width // BLOCK) * k // CHUNKS) for k in range(CHUNKS + 1)]
    pairs = []
    for k, (first, last) in enumerate(zip(edges[:-1], edges[1:])):
        after = [corner(keep)] if k == 1 else [corner(pairs[k - 2][1])] if k else []
        keep, send = widen(normed, tail, w_gate, w_up, first, last - first, after)
        pairs.append(add_parts(keep, exchange(send, "att", 1), att // 2, F32))
    moved = [
        [shift(part, "att", 2 * (d + 1)) for d, part in enumerate(away)] for _, *away in pairs
    ]
    w_down, token = load([whole(w_down)], "load_down", [corner(pairs[-1][1])])
    chunks = [
        gather_att(gate_rows(pair[0], parts, model * att, token))
        for pair, parts in zip(pairs, moved)
    ]
    hidden = place_rows(chunks)
    out = finish(residual, reduce_ffn(*multiply(hidden, w_down, "narrow")))
    return jnp.swapaxes(out.reshape(STEPS, owned, model), 0, 1)


def solution(mesh):
    return jax.shard_map(
        local,
        mesh=mesh,
        in_specs=(
            P("parts", None, "att"),
            P(("parts", "att"), None, "ffn"),
            P(("parts", "att"), None, "ffn"),
            P(("parts", "att"), None, "ffn"),
            P(("parts", "att")),
            P("parts"),
            P("ffn", "att"),
            P("att"),
            P("att", "ffn"),
            P("att", "ffn"),
            P("ffn", "att"),
        ),
        out_specs=P(("parts", "ffn"), None, "att"),
        check_vma=False,
    )
```

```python
import functools

import jax
import jax.numpy as jnp
from jax import lax
from jax.experimental import pallas as pl
from jax.experimental.pallas import tpu as pltpu
from jax.sharding import PartitionSpec as P

H = 64
KVH = 8
HD = 128
STEPS = 2
GROUPS = H // KVH
EPSILON = 1e-05
BLOCK = 256
CHUNKS = 2
PARTS = 2
F32 = jnp.float32
BF16 = jnp.bfloat16
MIB = 1024 * 1024


def dot(a, b):
    return jnp.dot(a, b, preferred_element_type=F32)

VMEM = pl.BlockSpec(memory_space=pltpu.VMEM)
ANY = pl.BlockSpec(memory_space=pl.ANY)


def shift(x, axis, d):
    n = lax.axis_size(axis)
    return lax.ppermute(x, axis, [(i, (i + d) % n) for i in range(n)])


def exchange(x, axis, bit):
    return lax.ppermute(x, axis, [(i, i ^ bit) for i in range(lax.axis_size(axis))])


def corner(x):
    return x[:8, :HD]


def limit(mib):
    return pltpu.CompilerParams(vmem_limit_bytes=mib * MIB)


def join(blocks, after=()):
    count = len(blocks)
    rows = [block.shape[0] for block in blocks]

    def kernel(*refs):
        out, at = refs[-1], 0
        for ref, size in zip(refs[:count], rows):
            out[at : at + size, :] = ref[...]
            at += size

    return pl.pallas_call(
        kernel,
        name="join",
        out_shape=jax.ShapeDtypeStruct((sum(rows), blocks[0].shape[1]), blocks[0].dtype),
        in_specs=[VMEM] * (count + len(after)),
        out_specs=VMEM,
        compiler_params=limit(4),
    )(*blocks, *after)


def gather_att(x, token=()):
    chips = lax.axis_size("att") // 2
    same = join([x] + [shift(x, "att", 2 * d) for d in range(1, chips)], token)
    return same, exchange(same, "att", 1)


def place_gathered(same, other, whole, columns=slice(None)):
    me, chips = lax.axis_index("att"), lax.axis_size("att") // 2
    rows = same.shape[0] // chips
    for d in range(chips):
        chip = lax.rem(me // 2 + chips - d, chips)
        for side, ref in enumerate((same, other)):
            source = chip * 2 + lax.rem(me + side, 2)
            at = pl.multiple_of(source * rows, rows)
            whole[pl.ds(at, rows), columns] = ref[d * rows : (d + 1) * rows, :]


def reduce_ffn(own, *others):
    masks = range(len(others), 0, -1)
    return [own] + [exchange(others[mask - 1], "ffn", mask) for mask in masks]


def gather_ffn(x):
    across = [exchange(x, "ffn", m) for m in range(2, lax.axis_size("ffn"), 2)]
    blocks = [x, exchange(x, "ffn", 1)]
    for block in across:
        blocks += [block, exchange(block, "ffn", 1)]
    return blocks


def vmem(x):
    return pltpu.with_memory_space_constraint(x, pltpu.VMEM)


def hbm(x):
    return pltpu.with_memory_space_constraint(x, pltpu.HBM)


class Copies:
    def __init__(self, entries):
        self.entries = entries
        self.sources = [hbm(x) for x, _ in entries]
        self.shapes = [pltpu.VMEM((n,) + x.shape[1:], x.dtype) for x, n in entries]
        self.scratch = pltpu.SemaphoreType.DMA((len(entries), 8))
        self.bytes = sum(2 * x.size // x.shape[0] * n * x.dtype.itemsize for x, n in entries)

    def started(self, sources, targets, sems):
        copies = []
        for k, (x, rows) in enumerate(self.entries):
            parts = 8 if rows % 8 == 0 else 1
            size = rows // parts
            begin = 0 if rows == x.shape[0] else lax.axis_index("ffn") * rows
            for p in range(parts):
                copies.append(
                    pltpu.make_async_copy(
                        sources[k].at[pl.ds(begin + p * size, size)],
                        targets[k].at[pl.ds(p * size, size)],
                        sems.at[k, p],
                    )
                )
        for copy in copies:
            copy.start()
        return copies


def load(entries, name, after=()):
    work = Copies(entries)
    count = len(entries)

    def kernel(*refs):
        targets, token, sems = refs[-2 - count : -2], refs[-2], refs[-1]
        copies = work.started(refs[:count], targets, sems)
        token[...] = jnp.zeros_like(token)
        for copy in copies:
            copy.wait()

    return pl.pallas_call(
        kernel,
        name=name,
        out_shape=work.shapes + [jax.ShapeDtypeStruct((8, HD), F32)],
        in_specs=[ANY] * count + [VMEM] * len(after),
        out_specs=[VMEM] * (count + 1),
        scratch_shapes=[work.scratch],
        compiler_params=limit(1),
        cost_estimate=pl.CostEstimate(flops=0, bytes_accessed=work.bytes, transcendentals=0),
    )(*work.sources, *after)


def attend(lengths, slot_row, same, other, cache):
    slots, cap, width = cache.shape
    kv_local = width // (2 * HD)
    heads = kv_local * GROUPS
    rows = STEPS * heads
    requests = slot_row.shape[1]
    fresh_at = STEPS * heads * HD
    columns = fresh_at + STEPS * width
    factor = HD ** (-0.5) * 1.4426950408889634

    def kernel(lengths, slot_row, same, other, cache, out, *scratch):
        qkv, qs, fresh, wide, scores, fresh_scores, mixed = scratch
        place_gathered(same, other, qkv)
        base = lax.axis_index("att") * slots
        wanted = lax.broadcasted_iota(jnp.int32, (slots, requests), 0) + base
        pick = jnp.where(slot_row[...] == wanted, 1.0, 0.0).astype(BF16)
        mine = dot(pick, qkv[...])
        for s in range(STEPS):
            for h in range(heads):
                at = (s * heads + h) * HD
                qs[pl.ds(s * heads + h, slots, stride=rows), :] = mine[:, at : at + HD]
            fresh[s * slots : (s + 1) * slots, :] = mine[
                :, fresh_at + s * width : fresh_at + (s + 1) * width
            ].astype(BF16)
        group_of = lax.broadcasted_iota(jnp.int32, (slots * rows, HD), 0) % heads // GROUPS
        for g in range(kv_local):
            own = jnp.where(group_of == g, qs[...], 0.0)
            wide[:, g * 2 * HD : g * 2 * HD + HD] = own.astype(BF16)
            wide[:, g * 2 * HD + HD : (g + 1) * 2 * HD] = jnp.zeros((slots * rows, HD), BF16)

        across = (((1,), (1,)), ((), ()))
        fresh_scores[...] = lax.dot_general(
            wide[...], fresh[...], across, preferred_element_type=F32
        )
        for i in range(slots):
            here = slice(i * rows, (i + 1) * rows)
            scores[here, :] = lax.dot_general(
                wide[here, :], cache[i], across, preferred_element_type=F32
            )
        key_at = lax.broadcasted_iota(jnp.int32, (rows, cap), 1)
        fresh_step = lax.broadcasted_iota(jnp.int32, (rows, STEPS * slots), 1)
        row_step = lax.broadcasted_iota(jnp.int32, (rows, STEPS * slots), 0) // heads
        for i in range(slots):
            here = slice(i * rows, (i + 1) * rows)
            kept = jnp.where(key_at < lengths[:, i : i + 1], scores[here, :], -jnp.inf)
            own = (fresh_step % slots == i) & (fresh_step // slots <= row_step)
            new = jnp.where(own, fresh_scores[here, :], -jnp.inf)
            top = jnp.maximum(
                jnp.max(kept, axis=1, keepdims=True), jnp.max(new, axis=1, keepdims=True)
            )
            kept = jnp.exp2((kept - top) * factor)
            new = jnp.exp2((new - top) * factor)
            total = jnp.sum(kept, axis=1, keepdims=True) + jnp.sum(new, axis=1, keepdims=True)
            values = dot(kept.astype(BF16), cache[i]) + dot(new.astype(BF16), fresh[...])
            values = values / total
            for s in range(STEPS):
                for g in range(kv_local):
                    at = s * heads + g * GROUPS
                    mixed[i * rows + at : i * rows + at + GROUPS, :] = values[
                        at : at + GROUPS, g * 2 * HD + HD : (g + 1) * 2 * HD
                    ]
        for s in range(STEPS):
            for h in range(heads):
                out[s * slots : (s + 1) * slots, h * HD : (h + 1) * HD] = mixed[
                    pl.ds(s * heads + h, slots, stride=rows), :
                ].astype(BF16)
    return pl.pallas_call(
        kernel,
        name="attend",
        out_shape=jax.ShapeDtypeStruct((STEPS * slots, heads * HD), BF16),
        in_specs=[VMEM] * 5,
        out_specs=VMEM,
        scratch_shapes=[
            pltpu.VMEM((requests, columns), BF16),
            pltpu.VMEM((slots * rows, HD), F32),
            pltpu.VMEM((STEPS * slots, width), BF16),
            pltpu.VMEM((slots * rows, width), BF16),
            pltpu.VMEM((slots * rows, cap), F32),
            pltpu.VMEM((slots * rows, STEPS * slots), F32),
            pltpu.VMEM((slots * rows, HD), F32),
        ],
        compiler_params=limit(6),
        cost_estimate=pl.CostEstimate(
            flops=4 * slots * rows * cap * width,
            bytes_accessed=slots * cap * width * 2,
            transcendentals=slots * rows * cap,
        ),
    )(lengths, slot_row, same, other, cache)


def matmul_cost(rows, depth, columns):
    return pl.CostEstimate(
        flops=2 * rows * depth * columns,
        bytes_accessed=2 * (rows * depth + depth * columns + rows * columns),
        transcendentals=0,
    )


def order_rows(slot_row, same, other):
    requests = slot_row.shape[1]
    rows = STEPS * requests
    depth = same.shape[1]
    slots = requests // lax.axis_size("att")
    ffn = lax.axis_size("ffn")
    owned = requests // ffn

    def kernel(slot_row, same, other, out, gathered, natural):
        place_gathered(same, other, gathered)
        slot = slot_row[...]
        first = lax.div(slot, slots) * (STEPS * slots) + lax.rem(slot, slots)
        at = lax.broadcasted_iota(jnp.int32, (rows, requests), 0)
        me = lax.axis_index("ffn")
        for step in range(STEPS):
            pick = jnp.where(at == first + step * slots, 1.0, 0.0).astype(BF16)
            picked = lax.dot_general(
                pick, gathered[...], (((0,), (0,)), ((), ())), preferred_element_type=F32
            )
            natural[...] = picked.astype(BF16)
            for r in range(ffn):
                owner = jnp.bitwise_xor(me, r)
                here = slice((r * STEPS + step) * owned, (r * STEPS + step + 1) * owned)
                out[here, :] = natural[pl.ds(pl.multiple_of(owner * owned, owned), owned), :]

    return pl.pallas_call(
        kernel,
        name="order_rows",
        out_shape=jax.ShapeDtypeStruct((rows, depth), BF16),
        in_specs=[VMEM] * 3,
        out_specs=VMEM,
        scratch_shapes=[pltpu.VMEM((rows, depth), BF16), pltpu.VMEM((requests, depth), BF16)],
        compiler_params=limit(4),
    )(slot_row, same, other)


def multiply(rows, w, part, name):
    columns = w.shape[1] // PARTS
    first = part * columns
    count, depth = rows.shape
    ffn = lax.axis_size("ffn")
    share = count // ffn
    block = min(512, columns)

    def kernel(rows, w, *outs):
        for j in range(columns // block):
            here = slice(j * block, (j + 1) * block)
            at = first + j * block
            product = dot(rows[...], w[:, at : at + block])
            for r, out in enumerate(outs):
                out[:, here] = product[r * share : (r + 1) * share].astype(out.dtype)

    return pl.pallas_call(
        kernel,
        name=name,
        out_shape=[
            jax.ShapeDtypeStruct((share, columns), BF16 if r else F32) for r in range(ffn)
        ],
        in_specs=[VMEM] * 2,
        out_specs=[VMEM] * ffn,
        compiler_params=limit(4),
        cost_estimate=matmul_cost(count, depth, columns),
    )(rows, w)


def add_parts(keep, arrived, parts, first=BF16):
    rows, width = keep.shape
    share = rows // parts
    types = [first] + [BF16] * (parts - 1)

    def kernel(keep, arrived, *outs):
        for d, out in enumerate(outs):
            here = slice(d * share, (d + 1) * share)
            out[...] = (keep[here, :].astype(F32) + arrived[here, :].astype(F32)).astype(out.dtype)

    return pl.pallas_call(
        kernel,
        name="add_parts",
        out_shape=[jax.ShapeDtypeStruct((share, width), kind) for kind in types],
        in_specs=[VMEM] * 2,
        out_specs=[VMEM] * parts,
        compiler_params=limit(4),
    )(keep, arrived)


def add_residual(own, part, terms):
    rows, columns = terms[0].shape
    model = columns * PARTS
    owned = rows // STEPS
    count = len(terms)

    def kernel(own, *refs):
        terms, out = refs[:count], refs[-1]
        total = terms[0][...]
        for term in terms[1:]:
            total = total + term[...].astype(F32)
        for step in range(STEPS):
            here = slice(step * owned, (step + 1) * owned)
            at = step * model + part * columns
            out[here, :] = (own[:, at : at + columns].astype(F32) + total[here]).astype(BF16)

    return pl.pallas_call(
        kernel,
        name="add_residual",
        out_shape=jax.ShapeDtypeStruct((rows, columns), BF16),
        in_specs=[VMEM] * (1 + count),
        out_specs=VMEM,
        compiler_params=limit(4),
    )(own, *terms)


def norm_rows(halves, gain):
    count = len(halves[0])
    flat = [block for blocks in halves for block in blocks]
    size, columns = flat[0].shape
    rows, depth = size * count, columns * len(halves)
    att = lax.axis_size("att")
    chips = att // 2
    share = rows // att

    def kernel(*refs):
        blocks, (gain, normed, tail, residual) = refs[: len(flat)], refs[len(flat) :]
        for k, block in enumerate(blocks):
            part, r = k // count, k % count
            residual[r * size : (r + 1) * size, part * columns : (part + 1) * columns] = block[...]
        me = lax.axis_index("att")
        chip, core = me // 2, lax.rem(me, 2)
        for side in range(2):
            for d in range(chips):
                owner = lax.rem(chip + d, chips) * 2 + lax.rem(core + side, 2)
                part = residual[pl.ds(pl.multiple_of(owner * share, share), share), :].astype(F32)
                here = slice((side * chips + d) * share, (side * chips + d + 1) * share)
                normed[here, :] = (part * gain[...]).astype(BF16)
                squares = jnp.sum(part * part, axis=1, keepdims=True)
                high = squares.astype(BF16).astype(F32)
                lane = lax.broadcasted_iota(jnp.int32, (share, HD), 1)
                tail[here, :] = jnp.where(lane == 0, high, squares - high).astype(BF16)

    return pl.pallas_call(
        kernel,
        name="norm_rows",
        out_shape=[
            jax.ShapeDtypeStruct((rows, depth), BF16),
            jax.ShapeDtypeStruct((rows, HD), BF16),
        ],
        in_specs=[VMEM] * (len(flat) + 1),
        out_specs=[VMEM] * 2,
        scratch_shapes=[pltpu.VMEM((rows, depth), BF16)],
        compiler_params=limit(4),
    )(*flat, gain)


def widen(normed, tail, w_gate, w_up, first, count, after):
    rows, depth = normed.shape
    half = rows // 2
    width = count * 2 * BLOCK + HD

    def kernel(normed, tail, gate, up, *refs):
        keep, send = refs[-2:]
        keep[:, count * 2 * BLOCK :] = tail[:half, :]
        send[:, count * 2 * BLOCK :] = tail[half:, :]
        for j in range(count):
            for which, w in enumerate((gate, up)):
                at = (first + j) * BLOCK
                product = dot(normed[...], w[:, at : at + BLOCK])
                here = slice((2 * j + which) * BLOCK, (2 * j + which + 1) * BLOCK)
                keep[:, here] = product[:half].astype(BF16)
                send[:, here] = product[half:].astype(BF16)

    return pl.pallas_call(
        kernel,
        name="widen",
        out_shape=[jax.ShapeDtypeStruct((half, width), BF16)] * 2,
        in_specs=[VMEM] * (4 + len(after)),
        out_specs=[VMEM] * 2,
        compiler_params=limit(4),
    )(normed, tail, vmem(w_gate), vmem(w_up), *after)


def gate_rows(own, moved, model, after):
    share, width = own.shape
    count = width // (2 * BLOCK)
    others = len(moved)

    def kernel(*refs):
        own, moved, out = refs[0], refs[1 : 1 + others], refs[-1]

        def total(here):
            value = own[:, here]
            for part in moved:
                value = value + part[:, here].astype(F32)
            return value

        tail = total(slice(count * 2 * BLOCK, count * 2 * BLOCK + HD))
        factor = lax.rsqrt((tail[:, 0:1] + tail[:, 1:2]) / model + EPSILON)
        for j in range(count):
            gate = total(slice(2 * j * BLOCK, (2 * j + 1) * BLOCK)) * factor
            up = total(slice((2 * j + 1) * BLOCK, (2 * j + 2) * BLOCK)) * factor
            out[:, j * BLOCK : (j + 1) * BLOCK] = (gate / (1.0 + jnp.exp(-gate)) * up).astype(BF16)

    return pl.pallas_call(
        kernel,
        name="gate",
        out_shape=jax.ShapeDtypeStruct((share, count * BLOCK), BF16),
        in_specs=[VMEM] * (2 + others),
        out_specs=VMEM,
        compiler_params=limit(4),
    )(own, *moved, after)


def place_rows(chunks):
    sizes = [same.shape[1] for same, _ in chunks]
    rows = 2 * chunks[0][0].shape[0]

    def kernel(*refs):
        out, at = refs[-1], 0
        for k, size in enumerate(sizes):
            place_gathered(refs[2 * k], refs[2 * k + 1], out, slice(at, at + size))
            at += size

    return pl.pallas_call(
        kernel,
        name="place_rows",
        out_shape=jax.ShapeDtypeStruct((rows, sum(sizes)), BF16),
        in_specs=[VMEM] * (2 * len(sizes)),
        out_specs=VMEM,
        compiler_params=limit(4),
    )(*[x for pair in chunks for x in pair])


def finish(residual, terms):
    count = len(terms[0])
    rows, columns = residual[0].shape

    def kernel(*refs):
        out = refs[-1]
        for part in range(PARTS):
            total = refs[PARTS + part * count][...]
            for term in refs[PARTS + part * count + 1 : PARTS + (part + 1) * count]:
                total = total + term[...].astype(F32)
            here = slice(part * columns, (part + 1) * columns)
            out[:, here] = (refs[part][...].astype(F32) + total).astype(BF16)

    return pl.pallas_call(
        kernel,
        name="finish",
        out_shape=jax.ShapeDtypeStruct((rows, PARTS * columns), BF16),
        in_specs=[VMEM] * (PARTS + PARTS * count),
        out_specs=VMEM,
        compiler_params=limit(4),
    )(*residual, *[term for group in terms for term in group])


def local(
    incoming, queries, new_kv, cache, lengths, slot_of, w_out, norm_gain, w_gate, w_up, w_down
):
    ffn = lax.axis_size("ffn")
    att = lax.axis_size("att")
    requests = slot_of.shape[0]
    slots = cache.shape[0]
    model = w_out.shape[1]
    width = w_gate.shape[1]
    owned = requests // ffn

    whole = lambda x: (x, x.shape[0])
    queries, new_kv, token = load([whole(queries), whole(new_kv)], "load_new")
    qkv = jnp.concatenate([queries.reshape(slots, -1), new_kv.reshape(slots, -1)], axis=1)
    small = [whole(slot_of.reshape(1, requests)), whole(lengths.reshape(1, slots))]
    cache, slot_row, lengths, own, token = load(
        [whole(cache)] + small + [(incoming, owned)], "load_cache", [corner(qkv)]
    )
    own = own.reshape(owned, STEPS * model)
    same, other = gather_att(qkv, [token])
    attended = attend(lengths, slot_row, same, other, cache)
    w_out, token = load([whole(w_out)], "load_out", [corner(attended)])
    rows = order_rows(slot_row, *gather_att(attended, [token]))
    products = [multiply(rows, w_out, part, "project") for part in range(PARTS)]
    residual = [add_residual(own, k, reduce_ffn(*products[k])) for k in range(PARTS)]

    halves = [gather_ffn(x) for x in residual]
    normed, tail = norm_rows(halves, norm_gain.reshape(1, model))
    edges = [-(-(width // BLOCK) * k // CHUNKS) for k in range(CHUNKS + 1)]
    pairs = []
    for k, (first, last) in enumerate(zip(edges[:-1], edges[1:])):
        after = [corner(keep)] if k == 1 else [corner(pairs[k - 2][1])] if k else []
        keep, send = widen(normed, tail, w_gate, w_up, first, last - first, after)
        pairs.append(add_parts(keep, exchange(send, "att", 1), att // 2, F32))
    moved = [
        [shift(part, "att", 2 * (d + 1)) for d, part in enumerate(away)] for _, *away in pairs
    ]
    w_down, token = load([whole(w_down)], "load_down", [corner(pairs[-1][1])])
    chunks = [
        gather_att(gate_rows(pair[0], parts, model * att, token))
        for pair, parts in zip(pairs, moved)
    ]
    hidden = place_rows(chunks)
    sums = [reduce_ffn(*multiply(hidden, w_down, part, "narrow")) for part in range(PARTS)]
    out = finish(residual, sums)
    return jnp.swapaxes(out.reshape(STEPS, owned, model), 0, 1)


def solution(mesh):
    return jax.shard_map(
        local,
        mesh=mesh,
        in_specs=(
            P("parts", None, "att"),
            P(("parts", "att"), None, "ffn"),
            P(("parts", "att"), None, "ffn"),
            P(("parts", "att"), None, "ffn"),
            P(("parts", "att")),
            P("parts"),
            P("ffn", "att"),
            P("att"),
            P("att", "ffn"),
            P("att", "ffn"),
            P("ffn", "att"),
        ),
        out_specs=P(("parts", "ffn"), None, "att"),
        check_vma=False,
    )
```

```python
import functools

import jax
import jax.numpy as jnp
from jax import lax
from jax.experimental import pallas as pl
from jax.experimental.pallas import tpu as pltpu
from jax.sharding import PartitionSpec as P

H = 64
KVH = 8
HD = 128
STEPS = 2
GROUPS = H // KVH
EPSILON = 1e-05
BLOCK = 256
CHUNKS = (2, 3, 2)
PARTS = 2
WAIT = 30000
F32 = jnp.float32
BF16 = jnp.bfloat16
MIB = 1024 * 1024


def dot(a, b):
    return jnp.dot(a, b, preferred_element_type=F32)

VMEM = pl.BlockSpec(memory_space=pltpu.VMEM)
ANY = pl.BlockSpec(memory_space=pl.ANY)


def shift(x, axis, d):
    n = lax.axis_size(axis)
    return lax.ppermute(x, axis, [(i, (i + d) % n) for i in range(n)])


def exchange(x, axis, bit):
    return lax.ppermute(x, axis, [(i, i ^ bit) for i in range(lax.axis_size(axis))])


def corner(x):
    return x[:8, :HD]


def limit(mib):
    return pltpu.CompilerParams(vmem_limit_bytes=mib * MIB)


def join(blocks, after=()):
    count = len(blocks)
    rows = [block.shape[0] for block in blocks]

    def kernel(*refs):
        out, at = refs[-1], 0
        for ref, size in zip(refs[:count], rows):
            out[at : at + size, :] = ref[...]
            at += size

    return pl.pallas_call(
        kernel,
        name="join",
        out_shape=jax.ShapeDtypeStruct((sum(rows), blocks[0].shape[1]), blocks[0].dtype),
        in_specs=[VMEM] * (count + len(after)),
        out_specs=VMEM,
        compiler_params=limit(4),
    )(*blocks, *after)


def gather_att(x, token=()):
    chips = lax.axis_size("att") // 2
    same = join([x] + [shift(x, "att", 2 * d) for d in range(1, chips)], token)
    return same, exchange(same, "att", 1)


def place_gathered(same, other, whole, columns=slice(None)):
    me, chips = lax.axis_index("att"), lax.axis_size("att") // 2
    rows = same.shape[0] // chips
    for d in range(chips):
        chip = lax.rem(me // 2 + chips - d, chips)
        for side, ref in enumerate((same, other)):
            source = chip * 2 + lax.rem(me + side, 2)
            at = pl.multiple_of(source * rows, rows)
            whole[pl.ds(at, rows), columns] = ref[d * rows : (d + 1) * rows, :]


def reduce_ffn(own, *others):
    return [own] + [exchange(rows, "ffn", k + 1) for k, rows in enumerate(others)]


def gather_ffn(x):
    across = [exchange(x, "ffn", m) for m in range(2, lax.axis_size("ffn"), 2)]
    blocks = [x, exchange(x, "ffn", 1)]
    for block in across:
        blocks += [block, exchange(block, "ffn", 1)]
    return blocks


def vmem(x):
    return pltpu.with_memory_space_constraint(x, pltpu.VMEM)


def hbm(x):
    return pltpu.with_memory_space_constraint(x, pltpu.HBM)


class Copies:
    def __init__(self, entries):
        self.entries = entries
        self.sources = [hbm(x) for x, _ in entries]
        self.shapes = [pltpu.VMEM((n,) + x.shape[1:], x.dtype) for x, n in entries]
        self.scratch = pltpu.SemaphoreType.DMA((len(entries), 8))
        self.bytes = sum(2 * x.size // x.shape[0] * n * x.dtype.itemsize for x, n in entries)

    def started(self, sources, targets, sems):
        copies = []
        for k, (x, rows) in enumerate(self.entries):
            parts = 8 if rows % 8 == 0 else 1
            size = rows // parts
            begin = 0 if rows == x.shape[0] else lax.axis_index("ffn") * rows
            for p in range(parts):
                copies.append(
                    pltpu.make_async_copy(
                        sources[k].at[pl.ds(begin + p * size, size)],
                        targets[k].at[pl.ds(p * size, size)],
                        sems.at[k, p],
                    )
                )
        for copy in copies:
            copy.start()
        return copies


def load(entries, name, after=(), cover=True):
    work = Copies(entries)
    count = len(entries)

    def kernel(*refs):
        targets, token, sems = refs[-2 - count : -2], refs[-2], refs[-1]
        copies = work.started(refs[:count], targets, sems)
        token[...] = jnp.zeros_like(token)
        for copy in copies:
            copy.wait()

    return pl.pallas_call(
        kernel,
        name=name,
        out_shape=work.shapes + [jax.ShapeDtypeStruct((8, HD), F32)],
        in_specs=[ANY] * count + [VMEM] * len(after),
        out_specs=[VMEM] * (count + 1),
        scratch_shapes=[work.scratch],
        compiler_params=limit(1),
        cost_estimate=pl.CostEstimate(
            flops=0, bytes_accessed=work.bytes if cover else 0, transcendentals=0
        ),
    )(*work.sources, *after)


def attend(lengths, slot_row, same, other, cache):
    slots, cap, width = cache.shape
    kv_local = width // (2 * HD)
    heads = kv_local * GROUPS
    rows = STEPS * heads
    requests = slot_row.shape[1]
    fresh_at = STEPS * heads * HD
    columns = fresh_at + STEPS * width
    factor = HD ** (-0.5) * 1.4426950408889634

    def kernel(lengths, slot_row, same, other, cache, out, *scratch):
        qkv, qs, fresh, wide, scores, fresh_scores, mixed = scratch
        place_gathered(same, other, qkv)
        base = lax.axis_index("att") * slots
        wanted = lax.broadcasted_iota(jnp.int32, (slots, requests), 0) + base
        pick = jnp.where(slot_row[...] == wanted, 1.0, 0.0).astype(BF16)
        mine = dot(pick, qkv[...])
        for s in range(STEPS):
            for h in range(heads):
                at = (s * heads + h) * HD
                qs[pl.ds(s * heads + h, slots, stride=rows), :] = mine[:, at : at + HD]
            fresh[s * slots : (s + 1) * slots, :] = mine[
                :, fresh_at + s * width : fresh_at + (s + 1) * width
            ].astype(BF16)
        group_of = lax.broadcasted_iota(jnp.int32, (slots * rows, HD), 0) % heads // GROUPS
        for g in range(kv_local):
            own = jnp.where(group_of == g, qs[...], 0.0)
            wide[:, g * HD : (g + 1) * HD] = own.astype(BF16)

        def of_groups(rows_kept, which):
            at = [g * 2 * HD + which * HD for g in range(kv_local)]
            return jnp.concatenate([rows_kept[:, first : first + HD] for first in at], axis=1)

        across = (((1,), (1,)), ((), ()))
        fresh_scores[...] = lax.dot_general(
            wide[...], of_groups(fresh, 0), across, preferred_element_type=F32
        )
        for i in range(slots):
            here = slice(i * rows, (i + 1) * rows)
            scores[here, :] = lax.dot_general(
                wide[here, :], of_groups(cache.at[i], 0), across, preferred_element_type=F32
            )
        key_at = lax.broadcasted_iota(jnp.int32, (rows, cap), 1)
        fresh_step = lax.broadcasted_iota(jnp.int32, (rows, STEPS * slots), 1)
        row_step = lax.broadcasted_iota(jnp.int32, (rows, STEPS * slots), 0) // heads
        for i in range(slots):
            here = slice(i * rows, (i + 1) * rows)
            kept = jnp.where(key_at < lengths[:, i : i + 1], scores[here, :], -jnp.inf)
            own = (fresh_step % slots == i) & (fresh_step // slots <= row_step)
            new = jnp.where(own, fresh_scores[here, :], -jnp.inf)
            top = jnp.maximum(
                jnp.max(kept, axis=1, keepdims=True), jnp.max(new, axis=1, keepdims=True)
            )
            kept = jnp.exp2((kept - top) * factor)
            new = jnp.exp2((new - top) * factor)
            total = jnp.sum(kept, axis=1, keepdims=True) + jnp.sum(new, axis=1, keepdims=True)
            values = dot(kept.astype(BF16), of_groups(cache.at[i], 1))
            values = values + dot(new.astype(BF16), of_groups(fresh, 1))
            values = values / total
            for s in range(STEPS):
                for g in range(kv_local):
                    at = s * heads + g * GROUPS
                    mixed[i * rows + at : i * rows + at + GROUPS, :] = values[
                        at : at + GROUPS, g * HD : (g + 1) * HD
                    ]
        for s in range(STEPS):
            for h in range(heads):
                out[s * slots : (s + 1) * slots, h * HD : (h + 1) * HD] = mixed[
                    pl.ds(s * heads + h, slots, stride=rows), :
                ].astype(BF16)
    return pl.pallas_call(
        kernel,
        name="attend",
        out_shape=jax.ShapeDtypeStruct((STEPS * slots, heads * HD), BF16),
        in_specs=[VMEM] * 5,
        out_specs=VMEM,
        scratch_shapes=[
            pltpu.VMEM((requests, columns), BF16),
            pltpu.VMEM((slots * rows, HD), F32),
            pltpu.VMEM((STEPS * slots, width), BF16),
            pltpu.VMEM((slots * rows, kv_local * HD), BF16),
            pltpu.VMEM((slots * rows, cap), F32),
            pltpu.VMEM((slots * rows, STEPS * slots), F32),
            pltpu.VMEM((slots * rows, HD), F32),
        ],
        compiler_params=limit(6),
        cost_estimate=pl.CostEstimate(
            flops=4 * slots * rows * cap * width,
            bytes_accessed=slots * cap * width * 2,
            transcendentals=slots * rows * cap,
        ),
    )(lengths, slot_row, same, other, cache)


def matmul_cost(rows, depth, columns):
    return pl.CostEstimate(
        flops=2 * rows * depth * columns,
        bytes_accessed=2 * (rows * depth + depth * columns + rows * columns),
        transcendentals=0,
    )


def order_rows(slot_row, same, other):
    requests = slot_row.shape[1]
    rows = STEPS * requests
    depth = same.shape[1]
    slots = requests // lax.axis_size("att")
    ffn = lax.axis_size("ffn")
    owned = requests // ffn

    def kernel(slot_row, same, other, out, gathered, natural):
        place_gathered(same, other, gathered)
        slot = slot_row[...]
        first = lax.div(slot, slots) * (STEPS * slots) + lax.rem(slot, slots)
        at = lax.broadcasted_iota(jnp.int32, (rows, requests), 0)
        me = lax.axis_index("ffn")
        for step in range(STEPS):
            pick = jnp.where(at == first + step * slots, 1.0, 0.0).astype(BF16)
            picked = lax.dot_general(
                pick, gathered[...], (((0,), (0,)), ((), ())), preferred_element_type=F32
            )
            natural[...] = picked.astype(BF16)
            for r in range(ffn):
                owner = jnp.bitwise_xor(me, r)
                here = slice((r * STEPS + step) * owned, (r * STEPS + step + 1) * owned)
                out[here, :] = natural[pl.ds(pl.multiple_of(owner * owned, owned), owned), :]

    return pl.pallas_call(
        kernel,
        name="order_rows",
        out_shape=jax.ShapeDtypeStruct((rows, depth), BF16),
        in_specs=[VMEM] * 3,
        out_specs=VMEM,
        scratch_shapes=[pltpu.VMEM((rows, depth), BF16), pltpu.VMEM((requests, depth), BF16)],
        compiler_params=limit(4),
    )(slot_row, same, other)


def multiply(rows, w, part, name):
    columns = w.shape[1] // PARTS
    first = part * columns
    count, depth = rows.shape
    ffn = lax.axis_size("ffn")
    share = count // ffn
    block = min(512, columns)

    def kernel(rows, w, *outs):
        for j in range(columns // block):
            here = slice(j * block, (j + 1) * block)
            at = first + j * block
            product = dot(rows[...], w[:, at : at + block])
            for r, out in enumerate(outs):
                out[:, here] = product[r * share : (r + 1) * share].astype(out.dtype)

    return pl.pallas_call(
        kernel,
        name=name,
        out_shape=[
            jax.ShapeDtypeStruct((share, columns), BF16 if r else F32) for r in range(ffn)
        ],
        in_specs=[VMEM] * 2,
        out_specs=[VMEM] * ffn,
        compiler_params=limit(4),
        cost_estimate=matmul_cost(count, depth, columns),
    )(rows, vmem(w))


def add_parts(keep, arrived, parts, first=BF16):
    rows, width = keep.shape
    share = rows // parts
    types = [first] + [BF16] * (parts - 1)

    def kernel(keep, arrived, *outs):
        for d, out in enumerate(outs):
            here = slice(d * share, (d + 1) * share)
            out[...] = (keep[here, :].astype(F32) + arrived[here, :].astype(F32)).astype(out.dtype)

    return pl.pallas_call(
        kernel,
        name="add_parts",
        out_shape=[jax.ShapeDtypeStruct((share, width), kind) for kind in types],
        in_specs=[VMEM] * 2,
        out_specs=[VMEM] * parts,
        compiler_params=limit(4),
    )(keep, arrived)


def add_residual(own, part, terms, after):
    rows, columns = terms[0].shape
    model = columns * PARTS
    owned = rows // STEPS
    count = len(terms)

    def kernel(own, *refs):
        terms, out = refs[:count], refs[-1]
        total = terms[0][...]
        for term in terms[1:]:
            total = total + term[...].astype(F32)
        for step in range(STEPS):
            here = slice(step * owned, (step + 1) * owned)
            at = step * model + part * columns
            out[here, :] = (own[:, at : at + columns].astype(F32) + total[here]).astype(BF16)

    return pl.pallas_call(
        kernel,
        name="add_residual",
        out_shape=jax.ShapeDtypeStruct((rows, columns), BF16),
        in_specs=[VMEM] * (1 + count + len(after)),
        out_specs=VMEM,
        compiler_params=limit(4),
    )(own, *terms, *after)


def norm_rows(halves, gain):
    count = len(halves[0])
    flat = [block for blocks in halves for block in blocks]
    size, columns = flat[0].shape
    rows, depth = size * count, columns * len(halves)
    att = lax.axis_size("att")
    chips = att // 2
    share = rows // att

    def kernel(*refs):
        blocks, (gain, normed, tail, residual) = refs[: len(flat)], refs[len(flat) :]
        for k, block in enumerate(blocks):
            part, r = k // count, k % count
            residual[r * size : (r + 1) * size, part * columns : (part + 1) * columns] = block[...]
        me = lax.axis_index("att")
        chip, core = me // 2, lax.rem(me, 2)
        for side in range(2):
            for d in range(chips):
                owner = lax.rem(chip + d, chips) * 2 + lax.rem(core + side, 2)
                part = residual[pl.ds(pl.multiple_of(owner * share, share), share), :].astype(F32)
                here = slice((side * chips + d) * share, (side * chips + d + 1) * share)
                normed[here, :] = (part * gain[...]).astype(BF16)
                squares = jnp.sum(part * part, axis=1, keepdims=True)
                high = squares.astype(BF16).astype(F32)
                lane = lax.broadcasted_iota(jnp.int32, (share, HD), 1)
                tail[here, :] = jnp.where(lane == 0, high, squares - high).astype(BF16)

    return pl.pallas_call(
        kernel,
        name="norm_rows",
        out_shape=[
            jax.ShapeDtypeStruct((rows, depth), BF16),
            jax.ShapeDtypeStruct((rows, HD), BF16),
        ],
        in_specs=[VMEM] * (len(flat) + 1),
        out_specs=[VMEM] * 2,
        scratch_shapes=[pltpu.VMEM((rows, depth), BF16)],
        compiler_params=limit(4),
    )(*flat, gain)


def widen(normed, tail, w_gate, w_up, first, count, after):
    rows, depth = normed.shape
    half = rows // 2
    width = count * 2 * BLOCK + HD

    def kernel(normed, tail, gate, up, *refs):
        keep, send = refs[-2:]
        keep[:, count * 2 * BLOCK :] = tail[:half, :]
        send[:, count * 2 * BLOCK :] = tail[half:, :]
        for j in range(count):
            for which, w in enumerate((gate, up)):
                at = (first + j) * BLOCK
                product = dot(normed[...], w[:, at : at + BLOCK])
                here = slice((2 * j + which) * BLOCK, (2 * j + which + 1) * BLOCK)
                keep[:, here] = product[:half].astype(BF16)
                send[:, here] = product[half:].astype(BF16)

    return pl.pallas_call(
        kernel,
        name="widen",
        out_shape=[jax.ShapeDtypeStruct((half, width), BF16)] * 2,
        in_specs=[VMEM] * (4 + len(after)),
        out_specs=[VMEM] * 2,
        compiler_params=limit(4),
        cost_estimate=matmul_cost(rows, depth, count * 2 * BLOCK),
    )(normed, tail, vmem(w_gate), vmem(w_up), *after)


def gate_rows(own, moved, model):
    share, width = own.shape
    count = width // (2 * BLOCK)
    others = len(moved)

    def kernel(*refs):
        own, moved, out = refs[0], refs[1 : 1 + others], refs[-1]

        def total(here):
            value = own[:, here]
            for part in moved:
                value = value + part[:, here].astype(F32)
            return value

        tail = total(slice(count * 2 * BLOCK, count * 2 * BLOCK + HD))
        factor = lax.rsqrt((tail[:, 0:1] + tail[:, 1:2]) / model + EPSILON)
        for j in range(count):
            gate = total(slice(2 * j * BLOCK, (2 * j + 1) * BLOCK)) * factor
            up = total(slice((2 * j + 1) * BLOCK, (2 * j + 2) * BLOCK)) * factor
            out[:, j * BLOCK : (j + 1) * BLOCK] = (gate / (1.0 + jnp.exp(-gate)) * up).astype(BF16)

    return pl.pallas_call(
        kernel,
        name="gate",
        out_shape=jax.ShapeDtypeStruct((share, count * BLOCK), BF16),
        in_specs=[VMEM] * (1 + others),
        out_specs=VMEM,
        compiler_params=limit(4),
        cost_estimate=pl.CostEstimate(flops=WAIT * own.size, bytes_accessed=0, transcendentals=0),
    )(own, *moved)


def place_rows(chunks):
    sizes = [same.shape[1] for same, _ in chunks]
    rows = 2 * chunks[0][0].shape[0]

    def kernel(*refs):
        out, at = refs[-1], 0
        for k, size in enumerate(sizes):
            place_gathered(refs[2 * k], refs[2 * k + 1], out, slice(at, at + size))
            at += size

    return pl.pallas_call(
        kernel,
        name="place_rows",
        out_shape=jax.ShapeDtypeStruct((rows, sum(sizes)), BF16),
        in_specs=[VMEM] * (2 * len(sizes)),
        out_specs=VMEM,
        compiler_params=limit(4),
    )(*[x for pair in chunks for x in pair])


def finish(residual, terms):
    count = len(terms[0])
    rows, columns = residual[0].shape

    def kernel(*refs):
        out = refs[-1]
        for part in range(PARTS):
            total = refs[PARTS + part * count][...]
            for term in refs[PARTS + part * count + 1 : PARTS + (part + 1) * count]:
                total = total + term[...].astype(F32)
            here = slice(part * columns, (part + 1) * columns)
            out[:, here] = (refs[part][...].astype(F32) + total).astype(BF16)

    return pl.pallas_call(
        kernel,
        name="finish",
        out_shape=jax.ShapeDtypeStruct((rows, PARTS * columns), BF16),
        in_specs=[VMEM] * (PARTS + PARTS * count),
        out_specs=VMEM,
        compiler_params=limit(4),
    )(*residual, *[term for group in terms for term in group])


def local(
    incoming, queries, new_kv, cache, lengths, slot_of, w_out, norm_gain, w_gate, w_up, w_down
):
    ffn = lax.axis_size("ffn")
    att = lax.axis_size("att")
    requests = slot_of.shape[0]
    slots = cache.shape[0]
    model = w_out.shape[1]
    width = w_gate.shape[1]
    owned = requests // ffn

    whole = lambda x: (x, x.shape[0])
    queries, new_kv, token = load([whole(queries), whole(new_kv)], "load_new")
    qkv = jnp.concatenate([queries.reshape(slots, -1), new_kv.reshape(slots, -1)], axis=1)
    small = [whole(slot_of.reshape(1, requests)), whole(lengths.reshape(1, slots))]
    cache, slot_row, lengths, own, token = load(
        [whole(cache)] + small + [(incoming, owned)], "load_cache", [corner(qkv)]
    )
    own = own.reshape(owned, STEPS * model)
    same, other = gather_att(qkv, [token])
    attended = attend(lengths, slot_row, same, other, cache)
    w_out, token = load([whole(w_out)], "load_out", [corner(attended)])
    rows = order_rows(slot_row, *gather_att(attended, [token]))
    products = [multiply(rows, w_out, part, "project") for part in range(PARTS)]
    halves = []
    for k in range(PARTS):
        after = [corner(halves[-1][1])] if halves else []
        halves.append(gather_ffn(add_residual(own, k, reduce_ffn(*products[k]), after)))
    residual = [blocks[0] for blocks in halves]
    normed, tail = norm_rows(halves, norm_gain.reshape(1, model))
    blocks, whole_of = width // BLOCK, sum(CHUNKS)
    edges = [blocks * sum(CHUNKS[:k]) // whole_of for k in range(len(CHUNKS) + 1)]
    pairs = []
    for k, (first, last) in enumerate(zip(edges[:-1], edges[1:])):
        after = [corner(keep)] if k == 1 else [corner(pairs[k - 2][1])] if k else []
        keep, send = widen(normed, tail, w_gate, w_up, first, last - first, after)
        pairs.append(add_parts(keep, exchange(send, "att", 1), att // 2, F32))
    moved = [
        [shift(part, "att", 2 * (d + 1)) for d, part in enumerate(away)] for _, *away in pairs
    ]
    chunks = [
        gather_att(gate_rows(pair[0], parts, model * att))
        for pair, parts in zip(pairs, moved)
    ]
    hidden = place_rows(chunks)
    sums = [reduce_ffn(*multiply(hidden, w_down, part, "narrow")) for part in range(PARTS)]
    out = finish(residual, sums)
    return jnp.swapaxes(out.reshape(STEPS, owned, model), 0, 1)


def solution(mesh):
    return jax.shard_map(
        local,
        mesh=mesh,
        in_specs=(
            P("parts", None, "att"),
            P(("parts", "att"), None, "ffn"),
            P(("parts", "att"), None, "ffn"),
            P(("parts", "att"), None, "ffn"),
            P(("parts", "att")),
            P("parts"),
            P("ffn", "att"),
            P("att"),
            P("att", "ffn"),
            P("att", "ffn"),
            P("ffn", "att"),
        ),
        out_specs=P(("parts", "ffn"), None, "att"),
        check_vma=False,
    )
```

```python
import functools

import jax
import jax.numpy as jnp
from jax import lax
from jax.experimental import pallas as pl
from jax.experimental.pallas import tpu as pltpu
from jax.sharding import PartitionSpec as P

H = 64
KVH = 8
HD = 128
STEPS = 2
GROUPS = H // KVH
EPSILON = 1e-05
BLOCK = 256
CHUNKS = (1, 2, 2, 2)
PARTS = 1
WAIT = 2 * 10**9
F32 = jnp.float32
BF16 = jnp.bfloat16
MIB = 1024 * 1024


def dot(a, b):
    return jnp.dot(a, b, preferred_element_type=F32)

VMEM = pl.BlockSpec(memory_space=pltpu.VMEM)
ANY = pl.BlockSpec(memory_space=pl.ANY)


def shift(x, axis, d):
    n = lax.axis_size(axis)
    return lax.ppermute(x, axis, [(i, (i + d) % n) for i in range(n)])


def exchange(x, axis, bit):
    return lax.ppermute(x, axis, [(i, i ^ bit) for i in range(lax.axis_size(axis))])


def corner(x):
    return x[:8, :HD]


def limit(mib):
    return pltpu.CompilerParams(vmem_limit_bytes=mib * MIB)


def join(blocks, after=()):
    count = len(blocks)
    rows = [block.shape[0] for block in blocks]

    def kernel(*refs):
        out, at = refs[-1], 0
        for ref, size in zip(refs[:count], rows):
            out[at : at + size, :] = ref[...]
            at += size

    return pl.pallas_call(
        kernel,
        name="join",
        out_shape=jax.ShapeDtypeStruct((sum(rows), blocks[0].shape[1]), blocks[0].dtype),
        in_specs=[VMEM] * (count + len(after)),
        out_specs=VMEM,
        compiler_params=limit(4),
    )(*blocks, *after)


def gather_att(x, token=()):
    chips = lax.axis_size("att") // 2
    same = join([x] + [shift(x, "att", 2 * d) for d in range(1, chips)], token)
    return same, exchange(same, "att", 1)


def place_gathered(same, other, whole, columns=slice(None)):
    me, chips = lax.axis_index("att"), lax.axis_size("att") // 2
    rows = same.shape[0] // chips
    for d in range(chips):
        chip = lax.rem(me // 2 + chips - d, chips)
        for side, ref in enumerate((same, other)):
            source = chip * 2 + lax.rem(me + side, 2)
            at = pl.multiple_of(source * rows, rows)
            whole[pl.ds(at, rows), columns] = ref[d * rows : (d + 1) * rows, :]


def reduce_ffn(own, *others):
    masks = list(range(2, len(others) + 1)) + [1]
    return [own] + [exchange(others[mask - 1], "ffn", mask) for mask in masks]


def gather_ffn(x):
    across = [exchange(x, "ffn", m) for m in range(2, lax.axis_size("ffn"), 2)]
    blocks = [x, exchange(x, "ffn", 1)]
    for block in across:
        blocks += [block, exchange(block, "ffn", 1)]
    return blocks


def vmem(x):
    return pltpu.with_memory_space_constraint(x, pltpu.VMEM)


def hbm(x):
    return pltpu.with_memory_space_constraint(x, pltpu.HBM)


class Copies:
    def __init__(self, entries):
        self.entries = entries
        self.sources = [hbm(x) for x, _ in entries]
        self.shapes = [pltpu.VMEM((n,) + x.shape[1:], x.dtype) for x, n in entries]
        self.scratch = pltpu.SemaphoreType.DMA((len(entries), 8))
        self.bytes = sum(2 * x.size // x.shape[0] * n * x.dtype.itemsize for x, n in entries)

    def started(self, sources, targets, sems):
        copies = []
        for k, (x, rows) in enumerate(self.entries):
            parts = 8 if rows % 8 == 0 and x.size >= MIB else 1
            size = rows // parts
            begin = 0 if rows == x.shape[0] else lax.axis_index("ffn") * rows
            for p in range(parts):
                copies.append(
                    pltpu.make_async_copy(
                        sources[k].at[pl.ds(begin + p * size, size)],
                        targets[k].at[pl.ds(p * size, size)],
                        sems.at[k, p],
                    )
                )
        for copy in copies:
            copy.start()
        return copies


def load(entries, name, after=()):
    work = Copies(entries)
    count = len(entries)

    def kernel(*refs):
        targets, token, sems = refs[-2 - count : -2], refs[-2], refs[-1]
        copies = work.started(refs[:count], targets, sems)
        token[...] = jnp.zeros_like(token)
        for copy in copies:
            copy.wait()

    return pl.pallas_call(
        kernel,
        name=name,
        out_shape=work.shapes + [jax.ShapeDtypeStruct((8, HD), F32)],
        in_specs=[ANY] * count + [VMEM] * len(after),
        out_specs=[VMEM] * (count + 1),
        scratch_shapes=[work.scratch],
        compiler_params=limit(1),
        cost_estimate=pl.CostEstimate(flops=0, bytes_accessed=work.bytes, transcendentals=0),
    )(*work.sources, *after)


def attend(lengths, slot_row, same, other, cache):
    slots, cap, width = cache.shape
    kv_local = width // (2 * HD)
    heads = kv_local * GROUPS
    rows = STEPS * heads
    requests = slot_row.shape[1]
    fresh_at = STEPS * heads * HD
    columns = fresh_at + STEPS * width
    factor = HD ** (-0.5) * 1.4426950408889634

    def kernel(lengths, slot_row, same, other, cache, out, *scratch):
        qkv, qs, fresh, wide, scores, fresh_scores, mixed = scratch
        place_gathered(same, other, qkv)
        base = lax.axis_index("att") * slots
        wanted = lax.broadcasted_iota(jnp.int32, (slots, requests), 0) + base
        pick = jnp.where(slot_row[...] == wanted, 1.0, 0.0).astype(BF16)
        mine = dot(pick, qkv[...])
        for s in range(STEPS):
            for h in range(heads):
                at = (s * heads + h) * HD
                qs[pl.ds(s * heads + h, slots, stride=rows), :] = mine[:, at : at + HD]
            fresh[s * slots : (s + 1) * slots, :] = mine[
                :, fresh_at + s * width : fresh_at + (s + 1) * width
            ].astype(BF16)
        group_of = lax.broadcasted_iota(jnp.int32, (slots * rows, HD), 0) % heads // GROUPS
        for g in range(kv_local):
            own = jnp.where(group_of == g, qs[...], 0.0)
            wide[:, g * HD : (g + 1) * HD] = own.astype(BF16)

        def of_groups(rows_kept, which):
            at = [g * 2 * HD + which * HD for g in range(kv_local)]
            return jnp.concatenate([rows_kept[:, first : first + HD] for first in at], axis=1)

        across = (((1,), (1,)), ((), ()))
        fresh_scores[...] = lax.dot_general(
            wide[...], of_groups(fresh, 0), across, preferred_element_type=F32
        )
        for i in range(slots):
            here = slice(i * rows, (i + 1) * rows)
            scores[here, :] = lax.dot_general(
                wide[here, :], of_groups(cache.at[i], 0), across, preferred_element_type=F32
            )
        key_at = lax.broadcasted_iota(jnp.int32, (rows, cap), 1)
        fresh_step = lax.broadcasted_iota(jnp.int32, (rows, STEPS * slots), 1)
        row_step = lax.broadcasted_iota(jnp.int32, (rows, STEPS * slots), 0) // heads
        for i in range(slots):
            here = slice(i * rows, (i + 1) * rows)
            kept = jnp.where(key_at < lengths[:, i : i + 1], scores[here, :], -jnp.inf)
            own = (fresh_step % slots == i) & (fresh_step // slots <= row_step)
            new = jnp.where(own, fresh_scores[here, :], -jnp.inf)
            top = jnp.maximum(
                jnp.max(kept, axis=1, keepdims=True), jnp.max(new, axis=1, keepdims=True)
            )
            kept = jnp.exp2((kept - top) * factor)
            new = jnp.exp2((new - top) * factor)
            total = jnp.sum(kept, axis=1, keepdims=True) + jnp.sum(new, axis=1, keepdims=True)
            values = dot(kept.astype(BF16), of_groups(cache.at[i], 1))
            values = values + dot(new.astype(BF16), of_groups(fresh, 1))
            values = values / total
            for s in range(STEPS):
                for g in range(kv_local):
                    at = s * heads + g * GROUPS
                    mixed[i * rows + at : i * rows + at + GROUPS, :] = values[
                        at : at + GROUPS, g * HD : (g + 1) * HD
                    ]
        for s in range(STEPS):
            for h in range(heads):
                out[s * slots : (s + 1) * slots, h * HD : (h + 1) * HD] = mixed[
                    pl.ds(s * heads + h, slots, stride=rows), :
                ].astype(BF16)
    return pl.pallas_call(
        kernel,
        name="attend",
        out_shape=jax.ShapeDtypeStruct((STEPS * slots, heads * HD), BF16),
        in_specs=[VMEM] * 5,
        out_specs=VMEM,
        scratch_shapes=[
            pltpu.VMEM((requests, columns), BF16),
            pltpu.VMEM((slots * rows, HD), F32),
            pltpu.VMEM((STEPS * slots, width), BF16),
            pltpu.VMEM((slots * rows, kv_local * HD), BF16),
            pltpu.VMEM((slots * rows, cap), F32),
            pltpu.VMEM((slots * rows, STEPS * slots), F32),
            pltpu.VMEM((slots * rows, HD), F32),
        ],
        compiler_params=limit(6),
        cost_estimate=pl.CostEstimate(
            flops=4 * slots * rows * cap * width,
            bytes_accessed=slots * cap * width * 2,
            transcendentals=slots * rows * cap,
        ),
    )(lengths, slot_row, same, other, cache)


def matmul_cost(rows, depth, columns):
    return pl.CostEstimate(
        flops=2 * rows * depth * columns,
        bytes_accessed=2 * (rows * depth + depth * columns + rows * columns),
        transcendentals=0,
    )


def order_rows(slot_row, same, other):
    requests = slot_row.shape[1]
    rows = STEPS * requests
    depth = same.shape[1]
    slots = requests // lax.axis_size("att")
    ffn = lax.axis_size("ffn")
    owned = requests // ffn

    def kernel(slot_row, same, other, out, gathered, natural):
        place_gathered(same, other, gathered)
        slot = slot_row[...]
        first = lax.div(slot, slots) * (STEPS * slots) + lax.rem(slot, slots)
        at = lax.broadcasted_iota(jnp.int32, (rows, requests), 0)
        me = lax.axis_index("ffn")
        for step in range(STEPS):
            pick = jnp.where(at == first + step * slots, 1.0, 0.0).astype(BF16)
            picked = lax.dot_general(
                pick, gathered[...], (((0,), (0,)), ((), ())), preferred_element_type=F32
            )
            natural[...] = picked.astype(BF16)
            for r in range(ffn):
                owner = jnp.bitwise_xor(me, r)
                here = slice((r * STEPS + step) * owned, (r * STEPS + step + 1) * owned)
                out[here, :] = natural[pl.ds(pl.multiple_of(owner * owned, owned), owned), :]

    return pl.pallas_call(
        kernel,
        name="order_rows",
        out_shape=jax.ShapeDtypeStruct((rows, depth), BF16),
        in_specs=[VMEM] * 3,
        out_specs=VMEM,
        scratch_shapes=[pltpu.VMEM((rows, depth), BF16), pltpu.VMEM((requests, depth), BF16)],
        compiler_params=limit(4),
    )(slot_row, same, other)


def multiply(rows, w, part, name):
    columns = w.shape[1] // PARTS
    first = part * columns
    count, depth = rows.shape
    ffn = lax.axis_size("ffn")
    share = count // ffn
    block = min(512, columns)

    def kernel(rows, w, *outs):
        for j in range(columns // block):
            here = slice(j * block, (j + 1) * block)
            at = first + j * block
            product = dot(rows[...], w[:, at : at + block])
            for r, out in enumerate(outs):
                out[:, here] = product[r * share : (r + 1) * share].astype(out.dtype)

    return pl.pallas_call(
        kernel,
        name=name,
        out_shape=[
            jax.ShapeDtypeStruct((share, columns), BF16 if r else F32) for r in range(ffn)
        ],
        in_specs=[VMEM] * 2,
        out_specs=[VMEM] * ffn,
        compiler_params=limit(4),
        cost_estimate=matmul_cost(count, depth, columns),
    )(rows, vmem(w))


def add_parts(keep, arrived, parts, first=BF16):
    rows, width = keep.shape
    share = rows // parts
    types = [first] + [BF16] * (parts - 1)

    def kernel(keep, arrived, *outs):
        for d, out in enumerate(outs):
            here = slice(d * share, (d + 1) * share)
            out[...] = (keep[here, :].astype(F32) + arrived[here, :].astype(F32)).astype(out.dtype)

    return pl.pallas_call(
        kernel,
        name="add_parts",
        out_shape=[jax.ShapeDtypeStruct((share, width), kind) for kind in types],
        in_specs=[VMEM] * 2,
        out_specs=[VMEM] * parts,
        compiler_params=limit(4),
    )(keep, arrived)


def add_residual(own, part, terms, after):
    rows, columns = terms[0].shape
    model = columns * PARTS
    owned = rows // STEPS
    count = len(terms)

    def kernel(own, *refs):
        terms, out = refs[:count], refs[-1]
        total = terms[0][...]
        for term in terms[1:]:
            total = total + term[...].astype(F32)
        for step in range(STEPS):
            here = slice(step * owned, (step + 1) * owned)
            at = step * model + part * columns
            out[here, :] = (own[:, at : at + columns].astype(F32) + total[here]).astype(BF16)

    return pl.pallas_call(
        kernel,
        name="add_residual",
        out_shape=jax.ShapeDtypeStruct((rows, columns), BF16),
        in_specs=[VMEM] * (1 + count + len(after)),
        out_specs=VMEM,
        compiler_params=limit(4),
    )(own, *terms, *after)


def norm_rows(halves, gain):
    count = len(halves[0])
    flat = [block for blocks in halves for block in blocks]
    size, columns = flat[0].shape
    rows, depth = size * count, columns * len(halves)
    att = lax.axis_size("att")
    chips = att // 2
    share = rows // att

    def kernel(*refs):
        blocks, (gain, normed, tail, residual) = refs[: len(flat)], refs[len(flat) :]
        for k, block in enumerate(blocks):
            part, r = k // count, k % count
            residual[r * size : (r + 1) * size, part * columns : (part + 1) * columns] = block[...]
        me = lax.axis_index("att")
        chip, core = me // 2, lax.rem(me, 2)
        for side in range(2):
            for d in range(chips):
                owner = lax.rem(chip + d, chips) * 2 + lax.rem(core + side, 2)
                part = residual[pl.ds(pl.multiple_of(owner * share, share), share), :].astype(F32)
                here = slice((side * chips + d) * share, (side * chips + d + 1) * share)
                normed[here, :] = (part * gain[...]).astype(BF16)
                squares = jnp.sum(part * part, axis=1, keepdims=True)
                high = squares.astype(BF16).astype(F32)
                lane = lax.broadcasted_iota(jnp.int32, (share, HD), 1)
                tail[here, :] = jnp.where(lane == 0, high, squares - high).astype(BF16)

    return pl.pallas_call(
        kernel,
        name="norm_rows",
        out_shape=[
            jax.ShapeDtypeStruct((rows, depth), BF16),
            jax.ShapeDtypeStruct((rows, HD), BF16),
        ],
        in_specs=[VMEM] * (len(flat) + 1),
        out_specs=[VMEM] * 2,
        scratch_shapes=[pltpu.VMEM((rows, depth), BF16)],
        compiler_params=limit(4),
    )(*flat, gain)


def widen(normed, tail, w_gate, w_up, first, count, after):
    rows, depth = normed.shape
    half = rows // 2
    extra = [] if tail is None else [tail]
    width = count * 2 * BLOCK + HD * len(extra)

    def kernel(normed, gate, up, *refs):
        keep, send = refs[-2:]
        for tail in refs[: len(extra)]:
            keep[:, count * 2 * BLOCK :] = tail[:half, :]
            send[:, count * 2 * BLOCK :] = tail[half:, :]
        for j in range(count):
            for which, w in enumerate((gate, up)):
                at = (first + j) * BLOCK
                product = dot(normed[...], w[:, at : at + BLOCK])
                here = slice((2 * j + which) * BLOCK, (2 * j + which + 1) * BLOCK)
                keep[:, here] = product[:half].astype(BF16)
                send[:, here] = product[half:].astype(BF16)

    return pl.pallas_call(
        kernel,
        name="widen",
        out_shape=[jax.ShapeDtypeStruct((half, width), BF16)] * 2,
        in_specs=[VMEM] * (3 + len(extra) + len(after)),
        out_specs=[VMEM] * 2,
        compiler_params=limit(4),
        cost_estimate=matmul_cost(rows, depth, count * 2 * BLOCK),
    )(normed, vmem(w_gate), vmem(w_up), *extra, *after)


def gate_rows(own, moved, scale, ahead, model):
    share, width = own.shape
    count = width // (2 * BLOCK)
    first = scale is None
    others = len(moved)
    held = ahead[0].shape[1] if ahead else 0

    def kernel(*refs):
        own, moved, rest = refs[0], refs[1 : 1 + others], refs[1 + others :]

        def total(here):
            value = own[:, here]
            for part in moved:
                value = value + part[:, here].astype(F32)
            return value

        if first:
            out, scale = rest
            tail = total(slice(count * 2 * BLOCK, count * 2 * BLOCK + HD))
            factor = lax.rsqrt((tail[:, 0:1] + tail[:, 1:2]) / model + EPSILON)
            scale[...] = jnp.broadcast_to(factor, scale.shape)
        else:
            scale, out = rest[0], rest[-1]
            factor = scale[:, 0:1]
            for block in rest[1:-1]:
                out[:, :held] = block[...]
        for j in range(count):
            gate = total(slice(2 * j * BLOCK, (2 * j + 1) * BLOCK)) * factor
            up = total(slice((2 * j + 1) * BLOCK, (2 * j + 2) * BLOCK)) * factor
            here = slice(held + j * BLOCK, held + (j + 1) * BLOCK)
            out[:, here] = (gate / (1.0 + jnp.exp(-gate)) * up).astype(BF16)

    hidden = jax.ShapeDtypeStruct((share, held + count * BLOCK), BF16)
    kept = jax.ShapeDtypeStruct((share, HD), F32)
    return pl.pallas_call(
        kernel,
        name="gate",
        out_shape=[hidden, kept] if first else hidden,
        in_specs=[VMEM] * (1 + others + (0 if first else 1 + len(ahead))),
        out_specs=[VMEM] * 2 if first else VMEM,
        compiler_params=limit(4),
        cost_estimate=pl.CostEstimate(flops=WAIT, bytes_accessed=0, transcendentals=0),
    )(own, *moved, *([] if first else [scale, *ahead]))


def place_rows(chunks):
    sizes = [same.shape[1] for same, _ in chunks]
    rows = 2 * chunks[0][0].shape[0]

    def kernel(*refs):
        out, at = refs[-1], 0
        for k, size in enumerate(sizes):
            place_gathered(refs[2 * k], refs[2 * k + 1], out, slice(at, at + size))
            at += size

    return pl.pallas_call(
        kernel,
        name="place_rows",
        out_shape=jax.ShapeDtypeStruct((rows, sum(sizes)), BF16),
        in_specs=[VMEM] * (2 * len(sizes)),
        out_specs=VMEM,
        compiler_params=limit(4),
    )(*[x for pair in chunks for x in pair])


def finish(residual, terms):
    count = len(terms[0])
    rows, columns = residual[0].shape

    def kernel(*refs):
        out = refs[-1]
        for part in range(PARTS):
            total = refs[PARTS + part * count][...]
            for term in refs[PARTS + part * count + 1 : PARTS + (part + 1) * count]:
                total = total + term[...].astype(F32)
            here = slice(part * columns, (part + 1) * columns)
            out[:, here] = (refs[part][...].astype(F32) + total).astype(BF16)

    return pl.pallas_call(
        kernel,
        name="finish",
        out_shape=jax.ShapeDtypeStruct((rows, PARTS * columns), BF16),
        in_specs=[VMEM] * (PARTS + PARTS * count),
        out_specs=VMEM,
        compiler_params=limit(4),
    )(*residual, *[term for group in terms for term in group])


def local(
    incoming, queries, new_kv, cache, lengths, slot_of, w_out, norm_gain, w_gate, w_up, w_down
):
    ffn = lax.axis_size("ffn")
    att = lax.axis_size("att")
    requests = slot_of.shape[0]
    slots = cache.shape[0]
    model = w_out.shape[1]
    width = w_gate.shape[1]
    owned = requests // ffn

    whole = lambda x: (x, x.shape[0])
    queries, new_kv, token = load([whole(queries), whole(new_kv)], "load_new")
    qkv = jnp.concatenate([queries.reshape(slots, -1), new_kv.reshape(slots, -1)], axis=1)
    small = [whole(slot_of.reshape(1, requests)), whole(lengths.reshape(1, slots))]
    cache, slot_row, lengths, own, token = load(
        [whole(cache)] + small + [(incoming, owned)], "load_cache", [corner(qkv)]
    )
    own = own.reshape(owned, STEPS * model)
    same, other = gather_att(qkv, [token])
    attended = attend(lengths, slot_row, same, other, cache)
    w_out, token = load([whole(w_out)], "load_out", [corner(attended)])
    rows = order_rows(slot_row, *gather_att(attended, [token]))
    products = [multiply(rows, w_out, part, "project") for part in range(PARTS)]
    halves = []
    for k in range(PARTS):
        after = [corner(halves[-1][1])] if halves else []
        halves.append(gather_ffn(add_residual(own, k, reduce_ffn(*products[k]), after)))
    residual = [blocks[0] for blocks in halves]
    normed, tail = norm_rows(halves, norm_gain.reshape(1, model))
    blocks, whole_of = width // BLOCK, sum(CHUNKS)
    edges = [blocks * sum(CHUNKS[:k]) // whole_of for k in range(len(CHUNKS) + 1)]
    pairs, after = [], []
    for k, (first, last) in enumerate(zip(edges[:-1], edges[1:])):
        ends = None if k else tail
        keep, send = widen(normed, ends, w_gate, w_up, first, last - first, after)
        pairs.append(add_parts(keep, exchange(send, "att", 1), att // 2, F32))
        after = [corner(pairs[max(k - 1, 0)][1])]
    chunks = []
    scale = None
    for total, *away in pairs:
        moved = [shift(part, "att", 2 * (d + 1)) for d, part in enumerate(away)]
        if scale is None:
            hidden, scale = gate_rows(total, moved, None, [], model * att)
            ahead = [hidden]
        else:
            hidden = gate_rows(total, moved, scale, ahead, model * att)
            chunks.append(gather_att(hidden))
            ahead = []
    hidden = place_rows(chunks)
    sums = [reduce_ffn(*multiply(hidden, w_down, part, "narrow")) for part in range(PARTS)]
    out = finish(residual, sums)
    return jnp.swapaxes(out.reshape(STEPS, owned, model), 0, 1)


def solution(mesh):
    return jax.shard_map(
        local,
        mesh=mesh,
        in_specs=(
            P("parts", None, "att"),
            P(("parts", "att"), None, "ffn"),
            P(("parts", "att"), None, "ffn"),
            P(("parts", "att"), None, "ffn"),
            P(("parts", "att")),
            P("parts"),
            P("ffn", "att"),
            P("att"),
            P("att", "ffn"),
            P("att", "ffn"),
            P("ffn", "att"),
        ),
        out_specs=P(("parts", "ffn"), None, "att"),
        check_vma=False,
    )
```

```python
import functools

import jax
import jax.numpy as jnp
from jax import lax
from jax.experimental import pallas as pl
from jax.experimental.pallas import tpu as pltpu
from jax.sharding import PartitionSpec as P

H = 64
KVH = 8
HD = 128
STEPS = 2
GROUPS = H // KVH
EPSILON = 1e-05
BLOCK = 256
CHUNKS = (2, 3, 2)
PARTS = 1
WAIT = 2 * 10**9
F32 = jnp.float32
BF16 = jnp.bfloat16
MIB = 1024 * 1024


def dot(a, b):
    return jnp.dot(a, b, preferred_element_type=F32)

VMEM = pl.BlockSpec(memory_space=pltpu.VMEM)
ANY = pl.BlockSpec(memory_space=pl.ANY)


def shift(x, axis, d):
    n = lax.axis_size(axis)
    return lax.ppermute(x, axis, [(i, (i + d) % n) for i in range(n)])


def exchange(x, axis, bit):
    return lax.ppermute(x, axis, [(i, i ^ bit) for i in range(lax.axis_size(axis))])


def corner(x):
    return x[:8, :HD]


def limit(mib):
    return pltpu.CompilerParams(vmem_limit_bytes=mib * MIB)


def join(blocks, after=()):
    count = len(blocks)
    rows = [block.shape[0] for block in blocks]

    def kernel(*refs):
        out, at = refs[-1], 0
        for ref, size in zip(refs[:count], rows):
            out[at : at + size, :] = ref[...]
            at += size

    return pl.pallas_call(
        kernel,
        name="join",
        out_shape=jax.ShapeDtypeStruct((sum(rows), blocks[0].shape[1]), blocks[0].dtype),
        in_specs=[VMEM] * (count + len(after)),
        out_specs=VMEM,
        compiler_params=limit(4),
    )(*blocks, *after)


def gather_att(x, token=()):
    chips = lax.axis_size("att") // 2
    same = join([x] + [shift(x, "att", 2 * d) for d in range(1, chips)], token)
    return same, exchange(same, "att", 1)


def place_gathered(same, other, whole, columns=slice(None)):
    me, chips = lax.axis_index("att"), lax.axis_size("att") // 2
    rows = same.shape[0] // chips
    for d in range(chips):
        chip = lax.rem(me // 2 + chips - d, chips)
        for side, ref in enumerate((same, other)):
            source = chip * 2 + lax.rem(me + side, 2)
            at = pl.multiple_of(source * rows, rows)
            whole[pl.ds(at, rows), columns] = ref[d * rows : (d + 1) * rows, :]


def reduce_ffn(own, *others):
    return [own] + [exchange(others[mask - 1], "ffn", mask) for mask in ffn_masks()[1:]]


def ffn_masks():
    return [0] + list(range(2, lax.axis_size("ffn"))) + [1]


def gather_ffn(x):
    return [exchange(x, "ffn", mask) for mask in ffn_masks()[:0:-1]] + [x]


def vmem(x):
    return pltpu.with_memory_space_constraint(x, pltpu.VMEM)


def hbm(x):
    return pltpu.with_memory_space_constraint(x, pltpu.HBM)


class Copies:
    def __init__(self, entries):
        self.entries = entries
        self.sources = [hbm(x) for x, _ in entries]
        self.shapes = [pltpu.VMEM((n,) + x.shape[1:], x.dtype) for x, n in entries]
        self.scratch = pltpu.SemaphoreType.DMA((len(entries), 8))
        self.bytes = sum(2 * x.size // x.shape[0] * n * x.dtype.itemsize for x, n in entries)

    def started(self, sources, targets, sems):
        copies = []
        for k, (x, rows) in enumerate(self.entries):
            parts = 8 if rows % 8 == 0 and x.size >= MIB else 1
            size = rows // parts
            begin = 0 if rows == x.shape[0] else lax.axis_index("ffn") * rows
            for p in range(parts):
                copies.append(
                    pltpu.make_async_copy(
                        sources[k].at[pl.ds(begin + p * size, size)],
                        targets[k].at[pl.ds(p * size, size)],
                        sems.at[k, p],
                    )
                )
        for copy in copies:
            copy.start()
        return copies


def load(entries, name, after=()):
    work = Copies(entries)
    count = len(entries)

    def kernel(*refs):
        targets, token, sems = refs[-2 - count : -2], refs[-2], refs[-1]
        copies = work.started(refs[:count], targets, sems)
        token[...] = jnp.zeros_like(token)
        for copy in copies:
            copy.wait()

    return pl.pallas_call(
        kernel,
        name=name,
        out_shape=work.shapes + [jax.ShapeDtypeStruct((8, HD), F32)],
        in_specs=[ANY] * count + [VMEM] * len(after),
        out_specs=[VMEM] * (count + 1),
        scratch_shapes=[work.scratch],
        compiler_params=limit(1),
        cost_estimate=pl.CostEstimate(flops=0, bytes_accessed=work.bytes, transcendentals=0),
    )(*work.sources, *after)


def attend(lengths, slot_row, same, other, cache):
    slots, cap, width = cache.shape
    kv_local = width // (2 * HD)
    heads = kv_local * GROUPS
    rows = STEPS * heads
    requests = slot_row.shape[1]
    fresh_at = STEPS * heads * HD
    columns = fresh_at + STEPS * width
    factor = HD ** (-0.5) * 1.4426950408889634

    def kernel(lengths, slot_row, same, other, cache, out, *scratch):
        qkv, qs, fresh, wide, scores, fresh_scores, mixed = scratch
        place_gathered(same, other, qkv)
        base = lax.axis_index("att") * slots
        wanted = lax.broadcasted_iota(jnp.int32, (slots, requests), 0) + base
        pick = jnp.where(slot_row[...] == wanted, 1.0, 0.0).astype(BF16)
        mine = dot(pick, qkv[...])
        for s in range(STEPS):
            for h in range(heads):
                at = (s * heads + h) * HD
                qs[pl.ds(s * heads + h, slots, stride=rows), :] = mine[:, at : at + HD]
            fresh[s * slots : (s + 1) * slots, :] = mine[
                :, fresh_at + s * width : fresh_at + (s + 1) * width
            ].astype(BF16)
        group_of = lax.broadcasted_iota(jnp.int32, (slots * rows, HD), 0) % heads // GROUPS
        for g in range(kv_local):
            own = jnp.where(group_of == g, qs[...], 0.0)
            wide[:, g * HD : (g + 1) * HD] = own.astype(BF16)

        def of_groups(rows_kept, which):
            at = [g * 2 * HD + which * HD for g in range(kv_local)]
            return jnp.concatenate([rows_kept[:, first : first + HD] for first in at], axis=1)

        across = (((1,), (1,)), ((), ()))
        fresh_scores[...] = lax.dot_general(
            wide[...], of_groups(fresh, 0), across, preferred_element_type=F32
        )
        for i in range(slots):
            here = slice(i * rows, (i + 1) * rows)
            scores[here, :] = lax.dot_general(
                wide[here, :], of_groups(cache.at[i], 0), across, preferred_element_type=F32
            )
        key_at = lax.broadcasted_iota(jnp.int32, (rows, cap), 1)
        fresh_step = lax.broadcasted_iota(jnp.int32, (rows, STEPS * slots), 1)
        row_step = lax.broadcasted_iota(jnp.int32, (rows, STEPS * slots), 0) // heads
        for i in range(slots):
            here = slice(i * rows, (i + 1) * rows)
            kept = jnp.where(key_at < lengths[:, i : i + 1], scores[here, :], -jnp.inf)
            own = (fresh_step % slots == i) & (fresh_step // slots <= row_step)
            new = jnp.where(own, fresh_scores[here, :], -jnp.inf)
            top = jnp.maximum(
                jnp.max(kept, axis=1, keepdims=True), jnp.max(new, axis=1, keepdims=True)
            )
            kept = jnp.exp2((kept - top) * factor)
            new = jnp.exp2((new - top) * factor)
            total = jnp.sum(kept, axis=1, keepdims=True) + jnp.sum(new, axis=1, keepdims=True)
            values = dot(kept.astype(BF16), of_groups(cache.at[i], 1))
            values = values + dot(new.astype(BF16), of_groups(fresh, 1))
            values = values / total
            for s in range(STEPS):
                for g in range(kv_local):
                    at = s * heads + g * GROUPS
                    mixed[i * rows + at : i * rows + at + GROUPS, :] = values[
                        at : at + GROUPS, g * HD : (g + 1) * HD
                    ]
        for s in range(STEPS):
            for h in range(heads):
                out[s * slots : (s + 1) * slots, h * HD : (h + 1) * HD] = mixed[
                    pl.ds(s * heads + h, slots, stride=rows), :
                ].astype(BF16)
    return pl.pallas_call(
        kernel,
        name="attend",
        out_shape=jax.ShapeDtypeStruct((STEPS * slots, heads * HD), BF16),
        in_specs=[VMEM] * 5,
        out_specs=VMEM,
        scratch_shapes=[
            pltpu.VMEM((requests, columns), BF16),
            pltpu.VMEM((slots * rows, HD), F32),
            pltpu.VMEM((STEPS * slots, width), BF16),
            pltpu.VMEM((slots * rows, kv_local * HD), BF16),
            pltpu.VMEM((slots * rows, cap), F32),
            pltpu.VMEM((slots * rows, STEPS * slots), F32),
            pltpu.VMEM((slots * rows, HD), F32),
        ],
        compiler_params=limit(6),
        cost_estimate=pl.CostEstimate(
            flops=4 * slots * rows * cap * width,
            bytes_accessed=slots * cap * width * 2,
            transcendentals=slots * rows * cap,
        ),
    )(lengths, slot_row, same, other, cache)


def matmul_cost(rows, depth, columns):
    return pl.CostEstimate(
        flops=2 * rows * depth * columns,
        bytes_accessed=2 * (rows * depth + depth * columns + rows * columns),
        transcendentals=0,
    )


def order_rows(slot_row, same, other):
    requests = slot_row.shape[1]
    rows = STEPS * requests
    depth = same.shape[1]
    slots = requests // lax.axis_size("att")
    ffn = lax.axis_size("ffn")
    owned = requests // ffn

    def kernel(slot_row, same, other, out, gathered, natural):
        place_gathered(same, other, gathered)
        slot = slot_row[...]
        first = lax.div(slot, slots) * (STEPS * slots) + lax.rem(slot, slots)
        at = lax.broadcasted_iota(jnp.int32, (rows, requests), 0)
        me = lax.axis_index("ffn")
        for step in range(STEPS):
            pick = jnp.where(at == first + step * slots, 1.0, 0.0).astype(BF16)
            picked = lax.dot_general(
                pick, gathered[...], (((0,), (0,)), ((), ())), preferred_element_type=F32
            )
            natural[...] = picked.astype(BF16)
            for r in range(ffn):
                owner = jnp.bitwise_xor(me, r)
                here = slice((r * STEPS + step) * owned, (r * STEPS + step + 1) * owned)
                out[here, :] = natural[pl.ds(pl.multiple_of(owner * owned, owned), owned), :]

    return pl.pallas_call(
        kernel,
        name="order_rows",
        out_shape=jax.ShapeDtypeStruct((rows, depth), BF16),
        in_specs=[VMEM] * 3,
        out_specs=VMEM,
        scratch_shapes=[pltpu.VMEM((rows, depth), BF16), pltpu.VMEM((requests, depth), BF16)],
        compiler_params=limit(4),
    )(slot_row, same, other)


def multiply(rows, w, part, name):
    columns = w.shape[1] // PARTS
    first = part * columns
    count, depth = rows.shape
    ffn = lax.axis_size("ffn")
    share = count // ffn
    block = min(512, columns)

    def kernel(rows, w, *outs):
        for j in range(columns // block):
            here = slice(j * block, (j + 1) * block)
            at = first + j * block
            product = dot(rows[...], w[:, at : at + block])
            for r, out in enumerate(outs):
                out[:, here] = product[r * share : (r + 1) * share].astype(out.dtype)

    return pl.pallas_call(
        kernel,
        name=name,
        out_shape=[
            jax.ShapeDtypeStruct((share, columns), BF16 if r else F32) for r in range(ffn)
        ],
        in_specs=[VMEM] * 2,
        out_specs=[VMEM] * ffn,
        compiler_params=limit(4),
        cost_estimate=matmul_cost(count, depth, columns),
    )(rows, vmem(w))


def add_parts(keep, arrived, parts, first=BF16):
    rows, width = keep.shape
    share = rows // parts
    types = [first] + [BF16] * (parts - 1)

    def kernel(keep, arrived, *outs):
        for d, out in enumerate(outs):
            here = slice(d * share, (d + 1) * share)
            out[...] = (keep[here, :].astype(F32) + arrived[here, :].astype(F32)).astype(out.dtype)

    return pl.pallas_call(
        kernel,
        name="add_parts",
        out_shape=[jax.ShapeDtypeStruct((share, width), kind) for kind in types],
        in_specs=[VMEM] * 2,
        out_specs=[VMEM] * parts,
        compiler_params=limit(4),
    )(keep, arrived)


def add_residual(own, part, terms, after):
    rows, columns = terms[0].shape
    model = columns * PARTS
    owned = rows // STEPS
    count = len(terms)

    def kernel(own, *refs):
        terms, out = refs[:count], refs[-1]
        total = terms[0][...]
        for term in terms[1:]:
            total = total + term[...].astype(F32)
        for step in range(STEPS):
            here = slice(step * owned, (step + 1) * owned)
            at = step * model + part * columns
            out[here, :] = (own[:, at : at + columns].astype(F32) + total[here]).astype(BF16)

    return pl.pallas_call(
        kernel,
        name="add_residual",
        out_shape=jax.ShapeDtypeStruct((rows, columns), BF16),
        in_specs=[VMEM] * (1 + count + len(after)),
        out_specs=VMEM,
        compiler_params=limit(4),
    )(own, *terms, *after)


def norm_rows(halves, gain):
    masks = ffn_masks()[::-1]
    count = len(halves[0])
    flat = [block for blocks in halves for block in blocks]
    size, columns = flat[0].shape
    rows, depth = size * count, columns * len(halves)
    att = lax.axis_size("att")
    chips = att // 2
    share = rows // att

    def kernel(*refs):
        blocks, (gain, normed, tail, residual) = refs[: len(flat)], refs[len(flat) :]
        for k, block in enumerate(blocks):
            part, r = k // count, masks[k % count]
            residual[r * size : (r + 1) * size, part * columns : (part + 1) * columns] = block[...]
        me = lax.axis_index("att")
        chip, core = me // 2, lax.rem(me, 2)
        for side in range(2):
            for d in range(chips):
                owner = lax.rem(chip + d, chips) * 2 + lax.rem(core + side, 2)
                part = residual[pl.ds(pl.multiple_of(owner * share, share), share), :].astype(F32)
                here = slice((side * chips + d) * share, (side * chips + d + 1) * share)
                normed[here, :] = (part * gain[...]).astype(BF16)
                squares = jnp.sum(part * part, axis=1, keepdims=True)
                high = squares.astype(BF16).astype(F32)
                lane = lax.broadcasted_iota(jnp.int32, (share, HD), 1)
                tail[here, :] = jnp.where(lane == 0, high, squares - high).astype(BF16)

    return pl.pallas_call(
        kernel,
        name="norm_rows",
        out_shape=[
            jax.ShapeDtypeStruct((rows, depth), BF16),
            jax.ShapeDtypeStruct((rows, HD), BF16),
        ],
        in_specs=[VMEM] * (len(flat) + 1),
        out_specs=[VMEM] * 2,
        scratch_shapes=[pltpu.VMEM((rows, depth), BF16)],
        compiler_params=limit(4),
    )(*flat, gain)


def widen(normed, tail, w_gate, w_up, first, count, after):
    rows, depth = normed.shape
    half = rows // 2
    width = count * 2 * BLOCK + HD

    def kernel(normed, tail, gate, up, *refs):
        keep, send = refs[-2:]
        keep[:, count * 2 * BLOCK :] = tail[:half, :]
        send[:, count * 2 * BLOCK :] = tail[half:, :]
        for j in range(count):
            for which, w in enumerate((gate, up)):
                at = (first + j) * BLOCK
                product = dot(normed[...], w[:, at : at + BLOCK])
                here = slice((2 * j + which) * BLOCK, (2 * j + which + 1) * BLOCK)
                keep[:, here] = product[:half].astype(BF16)
                send[:, here] = product[half:].astype(BF16)

    return pl.pallas_call(
        kernel,
        name="widen",
        out_shape=[jax.ShapeDtypeStruct((half, width), BF16)] * 2,
        in_specs=[VMEM] * (4 + len(after)),
        out_specs=[VMEM] * 2,
        compiler_params=limit(4),
        cost_estimate=matmul_cost(rows, depth, count * 2 * BLOCK),
    )(normed, tail, vmem(w_gate), vmem(w_up), *after)


def gate_rows(own, moved, model):
    share, width = own.shape
    count = width // (2 * BLOCK)
    others = len(moved)

    def kernel(*refs):
        own, moved, out = refs[0], refs[1 : 1 + others], refs[-1]

        def total(here):
            value = own[:, here]
            for part in moved:
                value = value + part[:, here].astype(F32)
            return value

        tail = total(slice(count * 2 * BLOCK, count * 2 * BLOCK + HD))
        factor = lax.rsqrt((tail[:, 0:1] + tail[:, 1:2]) / model + EPSILON)
        for j in range(count):
            gate = total(slice(2 * j * BLOCK, (2 * j + 1) * BLOCK)) * factor
            up = total(slice((2 * j + 1) * BLOCK, (2 * j + 2) * BLOCK)) * factor
            out[:, j * BLOCK : (j + 1) * BLOCK] = (gate / (1.0 + jnp.exp(-gate)) * up).astype(BF16)

    return pl.pallas_call(
        kernel,
        name="gate",
        out_shape=jax.ShapeDtypeStruct((share, count * BLOCK), BF16),
        in_specs=[VMEM] * (1 + others),
        out_specs=VMEM,
        compiler_params=limit(4),
        cost_estimate=pl.CostEstimate(flops=WAIT, bytes_accessed=0, transcendentals=0),
    )(own, *moved)


def place_rows(chunks):
    sizes = [same.shape[1] for same, _ in chunks]
    rows = 2 * chunks[0][0].shape[0]

    def kernel(*refs):
        out, at = refs[-1], 0
        for k, size in enumerate(sizes):
            place_gathered(refs[2 * k], refs[2 * k + 1], out, slice(at, at + size))
            at += size

    return pl.pallas_call(
        kernel,
        name="place_rows",
        out_shape=jax.ShapeDtypeStruct((rows, sum(sizes)), BF16),
        in_specs=[VMEM] * (2 * len(sizes)),
        out_specs=VMEM,
        compiler_params=limit(4),
    )(*[x for pair in chunks for x in pair])


def finish(residual, terms):
    count = len(terms[0])
    rows, columns = residual[0].shape

    def kernel(*refs):
        out = refs[-1]
        for part in range(PARTS):
            total = refs[PARTS + part * count][...]
            for term in refs[PARTS + part * count + 1 : PARTS + (part + 1) * count]:
                total = total + term[...].astype(F32)
            here = slice(part * columns, (part + 1) * columns)
            out[:, here] = (refs[part][...].astype(F32) + total).astype(BF16)

    return pl.pallas_call(
        kernel,
        name="finish",
        out_shape=jax.ShapeDtypeStruct((rows, PARTS * columns), BF16),
        in_specs=[VMEM] * (PARTS + PARTS * count),
        out_specs=VMEM,
        compiler_params=limit(4),
    )(*residual, *[term for group in terms for term in group])


def local(
    incoming, queries, new_kv, cache, lengths, slot_of, w_out, norm_gain, w_gate, w_up, w_down
):
    ffn = lax.axis_size("ffn")
    att = lax.axis_size("att")
    requests = slot_of.shape[0]
    slots = cache.shape[0]
    model = w_out.shape[1]
    width = w_gate.shape[1]
    owned = requests // ffn

    whole = lambda x: (x, x.shape[0])
    queries, new_kv, token = load([whole(queries), whole(new_kv)], "load_new")
    qkv = jnp.concatenate([queries.reshape(slots, -1), new_kv.reshape(slots, -1)], axis=1)
    small = [whole(slot_of.reshape(1, requests)), whole(lengths.reshape(1, slots))]
    cache, slot_row, lengths, own, token = load(
        [whole(cache)] + small + [(incoming, owned)], "load_cache", [corner(qkv)]
    )
    own = own.reshape(owned, STEPS * model)
    same, other = gather_att(qkv, [token])
    attended = attend(lengths, slot_row, same, other, cache)
    w_out, token = load([whole(w_out)], "load_out", [corner(attended)])
    rows = order_rows(slot_row, *gather_att(attended, [token]))
    products = [multiply(rows, w_out, part, "project") for part in range(PARTS)]
    halves = []
    for k in range(PARTS):
        after = [corner(halves[-1][0])] if halves else []
        halves.append(gather_ffn(add_residual(own, k, reduce_ffn(*products[k]), after)))
    residual = [blocks[-1] for blocks in halves]
    normed, tail = norm_rows(halves, norm_gain.reshape(1, model))
    blocks, whole_of = width // BLOCK, sum(CHUNKS)
    edges = [blocks * sum(CHUNKS[:k]) // whole_of for k in range(len(CHUNKS) + 1)]
    pairs = []
    for k, (first, last) in enumerate(zip(edges[:-1], edges[1:])):
        after = [corner(keep)] if k == 1 else [corner(pairs[k - 2][1])] if k else []
        keep, send = widen(normed, tail, w_gate, w_up, first, last - first, after)
        pairs.append(add_parts(keep, exchange(send, "att", 1), att // 2, F32))
    moved = [
        [shift(part, "att", 2 * (d + 1)) for d, part in enumerate(away)] for _, *away in pairs
    ]
    chunks = [
        gather_att(gate_rows(pair[0], parts, model * att))
        for pair, parts in zip(pairs, moved)
    ]
    hidden = place_rows(chunks)
    sums = [reduce_ffn(*multiply(hidden, w_down, part, "narrow")) for part in range(PARTS)]
    out = finish(residual, sums)
    return jnp.swapaxes(out.reshape(STEPS, owned, model), 0, 1)


def solution(mesh):
    return jax.shard_map(
        local,
        mesh=mesh,
        in_specs=(
            P("parts", None, "att"),
            P(("parts", "att"), None, "ffn"),
            P(("parts", "att"), None, "ffn"),
            P(("parts", "att"), None, "ffn"),
            P(("parts", "att")),
            P("parts"),
            P("ffn", "att"),
            P("att"),
            P("att", "ffn"),
            P("att", "ffn"),
            P("ffn", "att"),
        ),
        out_specs=P(("parts", "ffn"), None, "att"),
        check_vma=False,
    )
```

```python
import functools

import jax
import jax.numpy as jnp
from jax import lax
from jax.experimental import pallas as pl
from jax.experimental.pallas import tpu as pltpu
from jax.sharding import PartitionSpec as P

H = 64
KVH = 8
HD = 128
STEPS = 2
GROUPS = H // KVH
EPSILON = 1e-05
BLOCK = 256
CHUNKS = (3, 3, 1)
WAIT = 2 * 10**9
F32 = jnp.float32
BF16 = jnp.bfloat16
MIB = 1024 * 1024


def dot(a, b):
    return jnp.dot(a, b, preferred_element_type=F32)

VMEM = pl.BlockSpec(memory_space=pltpu.VMEM)
ANY = pl.BlockSpec(memory_space=pl.ANY)


def shift(x, axis, d):
    n = lax.axis_size(axis)
    return lax.ppermute(x, axis, [(i, (i + d) % n) for i in range(n)])


def exchange(x, axis, bit):
    return lax.ppermute(x, axis, [(i, i ^ bit) for i in range(lax.axis_size(axis))])


def corner(x):
    return x[:8, :HD]


def limit(mib):
    return pltpu.CompilerParams(vmem_limit_bytes=mib * MIB)


def join(blocks, after=()):
    count = len(blocks)
    rows = [block.shape[0] for block in blocks]

    def kernel(*refs):
        out, at = refs[-1], 0
        for ref, size in zip(refs[:count], rows):
            out[at : at + size, :] = ref[...]
            at += size

    return pl.pallas_call(
        kernel,
        name="join",
        out_shape=jax.ShapeDtypeStruct((sum(rows), blocks[0].shape[1]), blocks[0].dtype),
        in_specs=[VMEM] * (count + len(after)),
        out_specs=VMEM,
        compiler_params=limit(4),
    )(*blocks, *after)


def gather_att(x, token=()):
    chips = lax.axis_size("att") // 2
    same = join([x] + [shift(x, "att", 2 * d) for d in range(1, chips)], token)
    return same, exchange(same, "att", 1)


def place_gathered(same, other, whole, columns=slice(None)):
    me, chips = lax.axis_index("att"), lax.axis_size("att") // 2
    rows = same.shape[0] // chips
    for d in range(chips):
        chip = lax.rem(me // 2 + chips - d, chips)
        for side, ref in enumerate((same, other)):
            source = chip * 2 + lax.rem(me + side, 2)
            at = pl.multiple_of(source * rows, rows)
            whole[pl.ds(at, rows), columns] = ref[d * rows : (d + 1) * rows, :]


def reduce_ffn(own, near, keep, far, *ahead):
    direct = [exchange(rows, "ffn", k + 2) for k, rows in enumerate(ahead)]
    sums = add_parts(keep, exchange(far, "ffn", 1), len(ahead) // 2)
    across = [exchange(part, "ffn", 2 * (k + 1)) for k, part in enumerate(sums)]
    near = join([near], [corner(sums[0])])
    return [own, *direct, *across, exchange(near, "ffn", 1)]


def add_terms(refs, columns):
    own, rest, near = refs[0], refs[1:-1], refs[-1]
    half = own.shape[1] // 2
    direct = 2 * len(rest) // 3
    left = columns.stop <= half
    total = own[:, columns] + near[:, columns].astype(F32)
    here = columns if left else slice(columns.start - half, columns.stop - half)
    for term in rest[:direct] if left else rest[direct:]:
        total = total + term[:, here].astype(F32)
    return total


def gather_ffn(x, left, right):
    ffn, half = lax.axis_size("ffn"), left.shape[1]
    blocks = [(1, 0, exchange(x, "ffn", 1))]
    for mask in range(2, ffn, 2):
        moved = exchange(right, "ffn", mask)
        blocks += [(mask + 1, half, exchange(moved, "ffn", 1)), (mask, half, moved)]
    blocks += [(mask, 0, exchange(left, "ffn", mask)) for mask in range(ffn - 1, 1, -1)]
    return blocks + [(0, 0, x)]


def vmem(x):
    return pltpu.with_memory_space_constraint(x, pltpu.VMEM)


def hbm(x):
    return pltpu.with_memory_space_constraint(x, pltpu.HBM)


class Copies:
    def __init__(self, entries):
        self.entries = entries
        self.sources = [hbm(x) for x, _ in entries]
        self.shapes = [pltpu.VMEM((n,) + x.shape[1:], x.dtype) for x, n in entries]
        self.scratch = pltpu.SemaphoreType.DMA((len(entries), 8))
        self.bytes = sum(2 * x.size // x.shape[0] * n * x.dtype.itemsize for x, n in entries)

    def started(self, sources, targets, sems):
        copies = []
        for k, (x, rows) in enumerate(self.entries):
            parts = 8 if rows % 8 == 0 and x.size >= MIB else 1
            size = rows // parts
            begin = 0 if rows == x.shape[0] else lax.axis_index("ffn") * rows
            for p in range(parts):
                copies.append(
                    pltpu.make_async_copy(
                        sources[k].at[pl.ds(begin + p * size, size)],
                        targets[k].at[pl.ds(p * size, size)],
                        sems.at[k, p],
                    )
                )
        for copy in copies:
            copy.start()
        return copies


def load(entries, name, after=()):
    work = Copies(entries)
    count = len(entries)

    def kernel(*refs):
        targets, token, sems = refs[-2 - count : -2], refs[-2], refs[-1]
        copies = work.started(refs[:count], targets, sems)
        token[...] = jnp.zeros_like(token)
        for copy in copies:
            copy.wait()

    return pl.pallas_call(
        kernel,
        name=name,
        out_shape=work.shapes + [jax.ShapeDtypeStruct((8, HD), F32)],
        in_specs=[ANY] * count + [VMEM] * len(after),
        out_specs=[VMEM] * (count + 1),
        scratch_shapes=[work.scratch],
        compiler_params=limit(1),
        cost_estimate=pl.CostEstimate(flops=0, bytes_accessed=work.bytes, transcendentals=0),
    )(*work.sources, *after)


def attend(lengths, slot_row, same, other, cache):
    slots, cap, width = cache.shape
    kv_local = width // (2 * HD)
    heads = kv_local * GROUPS
    rows = STEPS * heads
    requests = slot_row.shape[1]
    fresh_at = STEPS * heads * HD
    columns = fresh_at + STEPS * width
    factor = HD ** (-0.5) * 1.4426950408889634

    def kernel(lengths, slot_row, same, other, cache, out, *scratch):
        qkv, qs, fresh, wide, scores, fresh_scores, mixed = scratch
        place_gathered(same, other, qkv)
        base = lax.axis_index("att") * slots
        wanted = lax.broadcasted_iota(jnp.int32, (slots, requests), 0) + base
        pick = jnp.where(slot_row[...] == wanted, 1.0, 0.0).astype(BF16)
        mine = dot(pick, qkv[...])
        for s in range(STEPS):
            for h in range(heads):
                at = (s * heads + h) * HD
                qs[pl.ds(s * heads + h, slots, stride=rows), :] = mine[:, at : at + HD]
            fresh[s * slots : (s + 1) * slots, :] = mine[
                :, fresh_at + s * width : fresh_at + (s + 1) * width
            ].astype(BF16)
        group_of = lax.broadcasted_iota(jnp.int32, (slots * rows, HD), 0) % heads // GROUPS
        for g in range(kv_local):
            own = jnp.where(group_of == g, qs[...], 0.0)
            wide[:, g * HD : (g + 1) * HD] = own.astype(BF16)

        def of_groups(rows_kept, which):
            at = [g * 2 * HD + which * HD for g in range(kv_local)]
            return jnp.concatenate([rows_kept[:, first : first + HD] for first in at], axis=1)

        across = (((1,), (1,)), ((), ()))
        fresh_scores[...] = lax.dot_general(
            wide[...], of_groups(fresh, 0), across, preferred_element_type=F32
        )
        for i in range(slots):
            here = slice(i * rows, (i + 1) * rows)
            scores[here, :] = lax.dot_general(
                wide[here, :], of_groups(cache.at[i], 0), across, preferred_element_type=F32
            )
        key_at = lax.broadcasted_iota(jnp.int32, (rows, cap), 1)
        fresh_step = lax.broadcasted_iota(jnp.int32, (rows, STEPS * slots), 1)
        row_step = lax.broadcasted_iota(jnp.int32, (rows, STEPS * slots), 0) // heads
        for i in range(slots):
            here = slice(i * rows, (i + 1) * rows)
            kept = jnp.where(key_at < lengths[:, i : i + 1], scores[here, :], -jnp.inf)
            own = (fresh_step % slots == i) & (fresh_step // slots <= row_step)
            new = jnp.where(own, fresh_scores[here, :], -jnp.inf)
            top = jnp.maximum(
                jnp.max(kept, axis=1, keepdims=True), jnp.max(new, axis=1, keepdims=True)
            )
            kept = jnp.exp2((kept - top) * factor)
            new = jnp.exp2((new - top) * factor)
            total = jnp.sum(kept, axis=1, keepdims=True) + jnp.sum(new, axis=1, keepdims=True)
            values = dot(kept.astype(BF16), of_groups(cache.at[i], 1))
            values = values + dot(new.astype(BF16), of_groups(fresh, 1))
            values = values / total
            for s in range(STEPS):
                for g in range(kv_local):
                    at = s * heads + g * GROUPS
                    mixed[i * rows + at : i * rows + at + GROUPS, :] = values[
                        at : at + GROUPS, g * HD : (g + 1) * HD
                    ]
        for s in range(STEPS):
            for h in range(heads):
                out[s * slots : (s + 1) * slots, h * HD : (h + 1) * HD] = mixed[
                    pl.ds(s * heads + h, slots, stride=rows), :
                ].astype(BF16)
    return pl.pallas_call(
        kernel,
        name="attend",
        out_shape=jax.ShapeDtypeStruct((STEPS * slots, heads * HD), BF16),
        in_specs=[VMEM] * 5,
        out_specs=VMEM,
        scratch_shapes=[
            pltpu.VMEM((requests, columns), BF16),
            pltpu.VMEM((slots * rows, HD), F32),
            pltpu.VMEM((STEPS * slots, width), BF16),
            pltpu.VMEM((slots * rows, kv_local * HD), BF16),
            pltpu.VMEM((slots * rows, cap), F32),
            pltpu.VMEM((slots * rows, STEPS * slots), F32),
            pltpu.VMEM((slots * rows, HD), F32),
        ],
        compiler_params=limit(6),
        cost_estimate=pl.CostEstimate(
            flops=4 * slots * rows * cap * width,
            bytes_accessed=slots * cap * width * 2,
            transcendentals=slots * rows * cap,
        ),
    )(lengths, slot_row, same, other, cache)


def matmul_cost(rows, depth, columns):
    return pl.CostEstimate(
        flops=2 * rows * depth * columns,
        bytes_accessed=2 * (rows * depth + depth * columns + rows * columns),
        transcendentals=0,
    )


def order_rows(slot_row, same, other):
    requests = slot_row.shape[1]
    rows = STEPS * requests
    depth = same.shape[1]
    slots = requests // lax.axis_size("att")
    ffn = lax.axis_size("ffn")
    owned = requests // ffn

    def kernel(slot_row, same, other, out, gathered, natural):
        place_gathered(same, other, gathered)
        slot = slot_row[...]
        first = lax.div(slot, slots) * (STEPS * slots) + lax.rem(slot, slots)
        at = lax.broadcasted_iota(jnp.int32, (rows, requests), 0)
        me = lax.axis_index("ffn")
        for step in range(STEPS):
            pick = jnp.where(at == first + step * slots, 1.0, 0.0).astype(BF16)
            picked = lax.dot_general(
                pick, gathered[...], (((0,), (0,)), ((), ())), preferred_element_type=F32
            )
            natural[...] = picked.astype(BF16)
            for r in range(ffn):
                owner = jnp.bitwise_xor(me, r)
                here = slice((r * STEPS + step) * owned, (r * STEPS + step + 1) * owned)
                out[here, :] = natural[pl.ds(pl.multiple_of(owner * owned, owned), owned), :]

    return pl.pallas_call(
        kernel,
        name="order_rows",
        out_shape=jax.ShapeDtypeStruct((rows, depth), BF16),
        in_specs=[VMEM] * 3,
        out_specs=VMEM,
        scratch_shapes=[pltpu.VMEM((rows, depth), BF16), pltpu.VMEM((requests, depth), BF16)],
        compiler_params=limit(4),
    )(slot_row, same, other)


def multiply(rows, w, name):
    columns = w.shape[1]
    half = columns // 2
    count, depth = rows.shape
    ffn = lax.axis_size("ffn")
    share = count // ffn
    rest = (ffn // 2 - 1) * share
    block = min(512, half)

    def kernel(rows, w, own, near, keep, far, *ahead):
        for at in range(0, columns, block):
            here = slice(at, at + block)
            product = dot(rows[...], w[:, here])
            own[:, here] = product[:share]
            near[:, here] = product[share : 2 * share].astype(BF16)
            for r in range(2, ffn):
                part = product[r * share : (r + 1) * share]
                if at < half:
                    ahead[r - 2][:, here] = part.astype(BF16)
                else:
                    out = far if r % 2 else keep
                    place = slice((r // 2 - 1) * share, r // 2 * share)
                    out[place, at - half : at - half + block] = part.astype(out.dtype)

    return pl.pallas_call(
        kernel,
        name=name,
        out_shape=[
            jax.ShapeDtypeStruct((share, columns), F32),
            jax.ShapeDtypeStruct((share, columns), BF16),
            jax.ShapeDtypeStruct((rest, half), F32),
            jax.ShapeDtypeStruct((rest, half), BF16),
        ]
        + [jax.ShapeDtypeStruct((share, half), BF16)] * (ffn - 2),
        in_specs=[VMEM] * 2,
        out_specs=[VMEM] * (ffn + 2),
        compiler_params=limit(4),
        cost_estimate=matmul_cost(count, depth, columns),
    )(rows, vmem(w))


def add_parts(keep, arrived, parts, first=BF16):
    rows, width = keep.shape
    share = rows // parts
    types = [first] + [BF16] * (parts - 1)

    def kernel(keep, arrived, *outs):
        for d, out in enumerate(outs):
            here = slice(d * share, (d + 1) * share)
            out[...] = (keep[here, :].astype(F32) + arrived[here, :].astype(F32)).astype(out.dtype)

    return pl.pallas_call(
        kernel,
        name="add_parts",
        out_shape=[jax.ShapeDtypeStruct((share, width), kind) for kind in types],
        in_specs=[VMEM] * 2,
        out_specs=[VMEM] * parts,
        compiler_params=limit(4),
    )(keep, arrived)


def add_residual(own, terms):
    rows, columns = terms[0].shape
    owned, half = rows // STEPS, columns // 2

    def kernel(own, *refs):
        terms, (whole, left, right) = refs[:-3], refs[-3:]
        for out, first in ((left, 0), (right, half)):
            total = add_terms(terms, slice(first, first + half))
            for step in range(STEPS):
                here = slice(step * owned, (step + 1) * owned)
                at = step * columns + first
                value = (own[:, at : at + half].astype(F32) + total[here]).astype(BF16)
                out[here, :] = value
                whole[here, first : first + half] = value

    return pl.pallas_call(
        kernel,
        name="add_residual",
        out_shape=[jax.ShapeDtypeStruct((rows, n), BF16) for n in (columns, half, half)],
        in_specs=[VMEM] * (1 + len(terms)),
        out_specs=[VMEM] * 3,
        compiler_params=limit(4),
    )(own, *terms)


def norm_rows(blocks, gain):
    places = [(mask, first) for mask, first, _ in blocks]
    flat = [block for _, _, block in blocks]
    size, depth = flat[-1].shape
    rows = size * lax.axis_size("ffn")
    att = lax.axis_size("att")
    chips = att // 2
    share = rows // att

    def kernel(*refs):
        blocks, (gain, normed, tail, residual) = refs[: len(flat)], refs[len(flat) :]
        for (mask, first), block in zip(places, blocks):
            here = slice(first, first + block.shape[1])
            residual[mask * size : (mask + 1) * size, here] = block[...]
        me = lax.axis_index("att")
        chip, core = me // 2, lax.rem(me, 2)
        for side in range(2):
            for d in range(chips):
                owner = lax.rem(chip + d, chips) * 2 + lax.rem(core + side, 2)
                part = residual[pl.ds(pl.multiple_of(owner * share, share), share), :].astype(F32)
                here = slice((side * chips + d) * share, (side * chips + d + 1) * share)
                normed[here, :] = (part * gain[...]).astype(BF16)
                squares = jnp.sum(part * part, axis=1, keepdims=True)
                high = squares.astype(BF16).astype(F32)
                lane = lax.broadcasted_iota(jnp.int32, (share, HD), 1)
                tail[here, :] = jnp.where(lane == 0, high, squares - high).astype(BF16)

    return pl.pallas_call(
        kernel,
        name="norm_rows",
        out_shape=[
            jax.ShapeDtypeStruct((rows, depth), BF16),
            jax.ShapeDtypeStruct((rows, HD), BF16),
        ],
        in_specs=[VMEM] * (len(flat) + 1),
        out_specs=[VMEM] * 2,
        scratch_shapes=[pltpu.VMEM((rows, depth), BF16)],
        compiler_params=limit(4),
    )(*flat, gain)


def widen(normed, tail, w_gate, w_up, first, count, after):
    rows, depth = normed.shape
    half = rows // 2
    width = count * 2 * BLOCK + HD

    def kernel(normed, tail, gate, up, *refs):
        keep, send = refs[-2:]
        keep[:, count * 2 * BLOCK :] = tail[:half, :]
        send[:, count * 2 * BLOCK :] = tail[half:, :]
        for j in range(count):
            for which, w in enumerate((gate, up)):
                at = (first + j) * BLOCK
                product = dot(normed[...], w[:, at : at + BLOCK])
                here = slice((2 * j + which) * BLOCK, (2 * j + which + 1) * BLOCK)
                keep[:, here] = product[:half].astype(BF16)
                send[:, here] = product[half:].astype(BF16)

    return pl.pallas_call(
        kernel,
        name="widen",
        out_shape=[jax.ShapeDtypeStruct((half, width), BF16)] * 2,
        in_specs=[VMEM] * (4 + len(after)),
        out_specs=[VMEM] * 2,
        compiler_params=limit(4),
        cost_estimate=matmul_cost(rows, depth, count * 2 * BLOCK),
    )(normed, tail, vmem(w_gate), vmem(w_up), *after)


def gate_rows(own, moved, model):
    share, width = own.shape
    count = width // (2 * BLOCK)
    others = len(moved)

    def kernel(*refs):
        own, moved, out = refs[0], refs[1 : 1 + others], refs[-1]

        def total(here):
            value = own[:, here]
            for part in moved:
                value = value + part[:, here].astype(F32)
            return value

        tail = total(slice(count * 2 * BLOCK, count * 2 * BLOCK + HD))
        factor = lax.rsqrt((tail[:, 0:1] + tail[:, 1:2]) / model + EPSILON)
        for j in range(count):
            gate = total(slice(2 * j * BLOCK, (2 * j + 1) * BLOCK)) * factor
            up = total(slice((2 * j + 1) * BLOCK, (2 * j + 2) * BLOCK)) * factor
            out[:, j * BLOCK : (j + 1) * BLOCK] = (gate / (1.0 + jnp.exp(-gate)) * up).astype(BF16)

    return pl.pallas_call(
        kernel,
        name="gate",
        out_shape=jax.ShapeDtypeStruct((share, count * BLOCK), BF16),
        in_specs=[VMEM] * (1 + others),
        out_specs=VMEM,
        compiler_params=limit(4),
        cost_estimate=pl.CostEstimate(flops=WAIT, bytes_accessed=0, transcendentals=0),
    )(own, *moved)


def place_rows(chunks):
    sizes = [same.shape[1] for same, _ in chunks]
    rows = 2 * chunks[0][0].shape[0]

    def kernel(*refs):
        out, at = refs[-1], 0
        for k, size in enumerate(sizes):
            place_gathered(refs[2 * k], refs[2 * k + 1], out, slice(at, at + size))
            at += size

    return pl.pallas_call(
        kernel,
        name="place_rows",
        out_shape=jax.ShapeDtypeStruct((rows, sum(sizes)), BF16),
        in_specs=[VMEM] * (2 * len(sizes)),
        out_specs=VMEM,
        compiler_params=limit(4),
    )(*[x for pair in chunks for x in pair])


def finish(residual, terms):
    rows, columns = residual.shape
    half = columns // 2

    def kernel(residual, *refs):
        for first in (0, half):
            here = slice(first, first + half)
            total = add_terms(refs[:-1], here)
            refs[-1][:, here] = (residual[:, here].astype(F32) + total).astype(BF16)

    return pl.pallas_call(
        kernel,
        name="finish",
        out_shape=jax.ShapeDtypeStruct((rows, columns), BF16),
        in_specs=[VMEM] * (1 + len(terms)),
        out_specs=VMEM,
        compiler_params=limit(4),
    )(residual, *terms)


def local(
    incoming, queries, new_kv, cache, lengths, slot_of, w_out, norm_gain, w_gate, w_up, w_down
):
    ffn = lax.axis_size("ffn")
    att = lax.axis_size("att")
    requests = slot_of.shape[0]
    slots = cache.shape[0]
    model = w_out.shape[1]
    width = w_gate.shape[1]
    owned = requests // ffn

    whole = lambda x: (x, x.shape[0])
    queries, new_kv, token = load([whole(queries), whole(new_kv)], "load_new")
    qkv = jnp.concatenate([queries.reshape(slots, -1), new_kv.reshape(slots, -1)], axis=1)
    small = [whole(slot_of.reshape(1, requests)), whole(lengths.reshape(1, slots))]
    cache, slot_row, lengths, own, token = load(
        [whole(cache)] + small + [(incoming, owned)], "load_cache", [corner(qkv)]
    )
    own = own.reshape(owned, STEPS * model)
    same, other = gather_att(qkv, [token])
    attended = attend(lengths, slot_row, same, other, cache)
    w_out, token = load([whole(w_out)], "load_out", [corner(attended)])
    rows = order_rows(slot_row, *gather_att(attended, [token]))
    sums = reduce_ffn(*multiply(rows, w_out, "project"))

    residual, left, right = add_residual(own, sums)
    normed, tail = norm_rows(gather_ffn(residual, left, right), norm_gain.reshape(1, model))
    blocks, whole_of = width // BLOCK, sum(CHUNKS)
    edges = [blocks * sum(CHUNKS[:k]) // whole_of for k in range(len(CHUNKS) + 1)]
    pairs = []
    for k, (first, last) in enumerate(zip(edges[:-1], edges[1:])):
        after = [corner(keep)] if k == 1 else [corner(pairs[k - 2][1])] if k else []
        keep, send = widen(normed, tail, w_gate, w_up, first, last - first, after)
        pairs.append(add_parts(keep, exchange(send, "att", 1), att // 2, F32))
    moved = [
        [shift(part, "att", 2 * (d + 1)) for d, part in enumerate(away)] for _, *away in pairs
    ]
    chunks = [
        gather_att(gate_rows(pair[0], parts, model * att))
        for pair, parts in zip(pairs, moved)
    ]
    hidden = place_rows(chunks)
    out = finish(residual, reduce_ffn(*multiply(hidden, w_down, "narrow")))
    return jnp.swapaxes(out.reshape(STEPS, owned, model), 0, 1)


def solution(mesh):
    return jax.shard_map(
        local,
        mesh=mesh,
        in_specs=(
            P("parts", None, "att"),
            P(("parts", "att"), None, "ffn"),
            P(("parts", "att"), None, "ffn"),
            P(("parts", "att"), None, "ffn"),
            P(("parts", "att")),
            P("parts"),
            P("ffn", "att"),
            P("att"),
            P("att", "ffn"),
            P("att", "ffn"),
            P("ffn", "att"),
        ),
        out_specs=P(("parts", "ffn"), None, "att"),
        check_vma=False,
    )
```

```python
import functools

import jax
import jax.numpy as jnp
from jax import lax
from jax.experimental import pallas as pl
from jax.experimental.pallas import tpu as pltpu
from jax.sharding import PartitionSpec as P

H = 64
KVH = 8
HD = 128
STEPS = 2
GROUPS = H // KVH
EPSILON = 1e-05
BLOCK = 256
CHUNKS = (2, 3, 2)
WAIT = 2 * 10**9
F32 = jnp.float32
BF16 = jnp.bfloat16
MIB = 1024 * 1024


def dot(a, b):
    return jnp.dot(a, b, preferred_element_type=F32)

VMEM = pl.BlockSpec(memory_space=pltpu.VMEM)
ANY = pl.BlockSpec(memory_space=pl.ANY)


def shift(x, axis, d):
    n = lax.axis_size(axis)
    return lax.ppermute(x, axis, [(i, (i + d) % n) for i in range(n)])


def exchange(x, axis, bit):
    return lax.ppermute(x, axis, [(i, i ^ bit) for i in range(lax.axis_size(axis))])


def corner(x):
    return x[:8, :HD]


def limit(mib):
    return pltpu.CompilerParams(vmem_limit_bytes=mib * MIB)


def join(blocks, after=()):
    count = len(blocks)
    rows = [block.shape[0] for block in blocks]

    def kernel(*refs):
        out, at = refs[-1], 0
        for ref, size in zip(refs[:count], rows):
            out[at : at + size, :] = ref[...]
            at += size

    return pl.pallas_call(
        kernel,
        name="join",
        out_shape=jax.ShapeDtypeStruct((sum(rows), blocks[0].shape[1]), blocks[0].dtype),
        in_specs=[VMEM] * (count + len(after)),
        out_specs=VMEM,
        compiler_params=limit(4),
    )(*blocks, *after)


def gather_att(x, token=()):
    chips = lax.axis_size("att") // 2
    same = join([x] + [shift(x, "att", 2 * d) for d in range(1, chips)], token)
    return same, exchange(same, "att", 1)


def place_gathered(same, other, whole, columns=slice(None)):
    me, chips = lax.axis_index("att"), lax.axis_size("att") // 2
    rows = same.shape[0] // chips
    for d in range(chips):
        chip = lax.rem(me // 2 + chips - d, chips)
        for side, ref in enumerate((same, other)):
            source = chip * 2 + lax.rem(me + side, 2)
            at = pl.multiple_of(source * rows, rows)
            whole[pl.ds(at, rows), columns] = ref[d * rows : (d + 1) * rows, :]


def reduce_ffn(own, near, keep, far, *ahead):
    direct = [exchange(rows, "ffn", k + 2) for k, rows in enumerate(ahead)]
    sums = add_parts(keep, exchange(far, "ffn", 1), len(ahead) // 2)
    across = [exchange(part, "ffn", 2 * (k + 1)) for k, part in enumerate(sums)]
    return [own, *direct, *across, exchange(near, "ffn", 1)]


def add_terms(refs, columns):
    own, rest, near = refs[0], refs[1:-1], refs[-1]
    half = own.shape[1] // 2
    direct = 2 * len(rest) // 3
    left = columns.stop <= half
    total = own[:, columns] + near[:, columns].astype(F32)
    here = columns if left else slice(columns.start - half, columns.stop - half)
    for term in rest[:direct] if left else rest[direct:]:
        total = total + term[:, here].astype(F32)
    return total


def gather_ffn(x, left, right):
    ffn, half = lax.axis_size("ffn"), left.shape[1]
    blocks = [(1, 0, exchange(x, "ffn", 1))]
    for mask in range(2, ffn, 2):
        moved = exchange(right, "ffn", mask)
        blocks += [(mask + 1, half, exchange(moved, "ffn", 1)), (mask, half, moved)]
    blocks += [(mask, 0, exchange(left, "ffn", mask)) for mask in range(ffn - 1, 1, -1)]
    return blocks + [(0, 0, x)]


def vmem(x):
    return pltpu.with_memory_space_constraint(x, pltpu.VMEM)


def hbm(x):
    return pltpu.with_memory_space_constraint(x, pltpu.HBM)


class Copies:
    def __init__(self, entries):
        self.entries = entries
        self.sources = [hbm(x) for x, _ in entries]
        self.shapes = [pltpu.VMEM((n,) + x.shape[1:], x.dtype) for x, n in entries]
        self.scratch = pltpu.SemaphoreType.DMA((len(entries), 8))
        self.bytes = sum(2 * x.size // x.shape[0] * n * x.dtype.itemsize for x, n in entries)

    def started(self, sources, targets, sems):
        copies = []
        for k, (x, rows) in enumerate(self.entries):
            parts = 8 if rows % 8 == 0 and x.size >= MIB else 1
            size = rows // parts
            begin = 0 if rows == x.shape[0] else lax.axis_index("ffn") * rows
            for p in range(parts):
                copies.append(
                    pltpu.make_async_copy(
                        sources[k].at[pl.ds(begin + p * size, size)],
                        targets[k].at[pl.ds(p * size, size)],
                        sems.at[k, p],
                    )
                )
        for copy in copies:
            copy.start()
        return copies


def load(entries, name, after=()):
    work = Copies(entries)
    count = len(entries)

    def kernel(*refs):
        targets, token, sems = refs[-2 - count : -2], refs[-2], refs[-1]
        copies = work.started(refs[:count], targets, sems)
        token[...] = jnp.zeros_like(token)
        for copy in copies:
            copy.wait()

    return pl.pallas_call(
        kernel,
        name=name,
        out_shape=work.shapes + [jax.ShapeDtypeStruct((8, HD), F32)],
        in_specs=[ANY] * count + [VMEM] * len(after),
        out_specs=[VMEM] * (count + 1),
        scratch_shapes=[work.scratch],
        compiler_params=limit(1),
        cost_estimate=pl.CostEstimate(flops=0, bytes_accessed=work.bytes, transcendentals=0),
    )(*work.sources, *after)


def attend(lengths, slot_row, same, other, cache):
    slots, cap, width = cache.shape
    kv_local = width // (2 * HD)
    heads = kv_local * GROUPS
    rows = STEPS * heads
    requests = slot_row.shape[1]
    fresh_at = STEPS * heads * HD
    columns = fresh_at + STEPS * width
    factor = HD ** (-0.5) * 1.4426950408889634

    def kernel(lengths, slot_row, same, other, cache, out, *scratch):
        qkv, qs, fresh, wide, scores, fresh_scores, mixed = scratch
        place_gathered(same, other, qkv)
        base = lax.axis_index("att") * slots
        wanted = lax.broadcasted_iota(jnp.int32, (slots, requests), 0) + base
        pick = jnp.where(slot_row[...] == wanted, 1.0, 0.0).astype(BF16)
        mine = dot(pick, qkv[...])
        for s in range(STEPS):
            for h in range(heads):
                at = (s * heads + h) * HD
                qs[pl.ds(s * heads + h, slots, stride=rows), :] = mine[:, at : at + HD]
            fresh[s * slots : (s + 1) * slots, :] = mine[
                :, fresh_at + s * width : fresh_at + (s + 1) * width
            ].astype(BF16)
        group_of = lax.broadcasted_iota(jnp.int32, (slots * rows, HD), 0) % heads // GROUPS
        for g in range(kv_local):
            own = jnp.where(group_of == g, qs[...], 0.0)
            wide[:, g * HD : (g + 1) * HD] = own.astype(BF16)

        def of_groups(rows_kept, which):
            at = [g * 2 * HD + which * HD for g in range(kv_local)]
            return jnp.concatenate([rows_kept[:, first : first + HD] for first in at], axis=1)

        across = (((1,), (1,)), ((), ()))
        fresh_scores[...] = lax.dot_general(
            wide[...], of_groups(fresh, 0), across, preferred_element_type=F32
        )
        for i in range(slots):
            here = slice(i * rows, (i + 1) * rows)
            scores[here, :] = lax.dot_general(
                wide[here, :], of_groups(cache.at[i], 0), across, preferred_element_type=F32
            )
        key_at = lax.broadcasted_iota(jnp.int32, (rows, cap), 1)
        fresh_step = lax.broadcasted_iota(jnp.int32, (rows, STEPS * slots), 1)
        row_step = lax.broadcasted_iota(jnp.int32, (rows, STEPS * slots), 0) // heads
        for i in range(slots):
            here = slice(i * rows, (i + 1) * rows)
            kept = jnp.where(key_at < lengths[:, i : i + 1], scores[here, :], -jnp.inf)
            own = (fresh_step % slots == i) & (fresh_step // slots <= row_step)
            new = jnp.where(own, fresh_scores[here, :], -jnp.inf)
            top = jnp.maximum(
                jnp.max(kept, axis=1, keepdims=True), jnp.max(new, axis=1, keepdims=True)
            )
            kept = jnp.exp2((kept - top) * factor)
            new = jnp.exp2((new - top) * factor)
            total = jnp.sum(kept, axis=1, keepdims=True) + jnp.sum(new, axis=1, keepdims=True)
            values = dot(kept.astype(BF16), of_groups(cache.at[i], 1))
            values = values + dot(new.astype(BF16), of_groups(fresh, 1))
            values = values / total
            for s in range(STEPS):
                for g in range(kv_local):
                    at = s * heads + g * GROUPS
                    mixed[i * rows + at : i * rows + at + GROUPS, :] = values[
                        at : at + GROUPS, g * HD : (g + 1) * HD
                    ]
        for s in range(STEPS):
            for h in range(heads):
                out[s * slots : (s + 1) * slots, h * HD : (h + 1) * HD] = mixed[
                    pl.ds(s * heads + h, slots, stride=rows), :
                ].astype(BF16)
    return pl.pallas_call(
        kernel,
        name="attend",
        out_shape=jax.ShapeDtypeStruct((STEPS * slots, heads * HD), BF16),
        in_specs=[VMEM] * 5,
        out_specs=VMEM,
        scratch_shapes=[
            pltpu.VMEM((requests, columns), BF16),
            pltpu.VMEM((slots * rows, HD), F32),
            pltpu.VMEM((STEPS * slots, width), BF16),
            pltpu.VMEM((slots * rows, kv_local * HD), BF16),
            pltpu.VMEM((slots * rows, cap), F32),
            pltpu.VMEM((slots * rows, STEPS * slots), F32),
            pltpu.VMEM((slots * rows, HD), F32),
        ],
        compiler_params=limit(6),
        cost_estimate=pl.CostEstimate(
            flops=4 * slots * rows * cap * width,
            bytes_accessed=slots * cap * width * 2,
            transcendentals=slots * rows * cap,
        ),
    )(lengths, slot_row, same, other, cache)


def matmul_cost(rows, depth, columns):
    return pl.CostEstimate(
        flops=2 * rows * depth * columns,
        bytes_accessed=2 * (rows * depth + depth * columns + rows * columns),
        transcendentals=0,
    )


def order_rows(slot_row, same, other):
    requests = slot_row.shape[1]
    rows = STEPS * requests
    depth = same.shape[1]
    slots = requests // lax.axis_size("att")
    ffn = lax.axis_size("ffn")
    owned = requests // ffn

    def kernel(slot_row, same, other, out, gathered, natural):
        place_gathered(same, other, gathered)
        slot = slot_row[...]
        first = lax.div(slot, slots) * (STEPS * slots) + lax.rem(slot, slots)
        at = lax.broadcasted_iota(jnp.int32, (rows, requests), 0)
        me = lax.axis_index("ffn")
        for step in range(STEPS):
            pick = jnp.where(at == first + step * slots, 1.0, 0.0).astype(BF16)
            picked = lax.dot_general(
                pick, gathered[...], (((0,), (0,)), ((), ())), preferred_element_type=F32
            )
            natural[...] = picked.astype(BF16)
            for r in range(ffn):
                owner = jnp.bitwise_xor(me, r)
                here = slice((r * STEPS + step) * owned, (r * STEPS + step + 1) * owned)
                out[here, :] = natural[pl.ds(pl.multiple_of(owner * owned, owned), owned), :]

    return pl.pallas_call(
        kernel,
        name="order_rows",
        out_shape=jax.ShapeDtypeStruct((rows, depth), BF16),
        in_specs=[VMEM] * 3,
        out_specs=VMEM,
        scratch_shapes=[pltpu.VMEM((rows, depth), BF16), pltpu.VMEM((requests, depth), BF16)],
        compiler_params=limit(4),
    )(slot_row, same, other)


def multiply(rows, w, name):
    columns = w.shape[1]
    half = columns // 2
    count, depth = rows.shape
    ffn = lax.axis_size("ffn")
    share = count // ffn
    rest = (ffn // 2 - 1) * share
    block = min(512, half)

    def kernel(rows, w, own, near, keep, far, *ahead):
        for at in range(0, columns, block):
            here = slice(at, at + block)
            product = dot(rows[...], w[:, here])
            own[:, here] = product[:share]
            near[:, here] = product[share : 2 * share].astype(BF16)
            for r in range(2, ffn):
                part = product[r * share : (r + 1) * share]
                if at < half:
                    ahead[r - 2][:, here] = part.astype(BF16)
                else:
                    out = far if r % 2 else keep
                    place = slice((r // 2 - 1) * share, r // 2 * share)
                    out[place, at - half : at - half + block] = part.astype(out.dtype)

    return pl.pallas_call(
        kernel,
        name=name,
        out_shape=[
            jax.ShapeDtypeStruct((share, columns), F32),
            jax.ShapeDtypeStruct((share, columns), BF16),
            jax.ShapeDtypeStruct((rest, half), F32),
            jax.ShapeDtypeStruct((rest, half), BF16),
        ]
        + [jax.ShapeDtypeStruct((share, half), BF16)] * (ffn - 2),
        in_specs=[VMEM] * 2,
        out_specs=[VMEM] * (ffn + 2),
        compiler_params=limit(4),
        cost_estimate=matmul_cost(count, depth, columns),
    )(rows, vmem(w))


def add_parts(keep, arrived, parts, first=BF16):
    rows, width = keep.shape
    share = rows // parts
    types = [first] + [BF16] * (parts - 1)

    def kernel(keep, arrived, *outs):
        for d, out in enumerate(outs):
            here = slice(d * share, (d + 1) * share)
            out[...] = (keep[here, :].astype(F32) + arrived[here, :].astype(F32)).astype(out.dtype)

    return pl.pallas_call(
        kernel,
        name="add_parts",
        out_shape=[jax.ShapeDtypeStruct((share, width), kind) for kind in types],
        in_specs=[VMEM] * 2,
        out_specs=[VMEM] * parts,
        compiler_params=limit(4),
    )(keep, arrived)


def add_residual(own, terms):
    rows, columns = terms[0].shape
    owned, half = rows // STEPS, columns // 2

    def kernel(own, *refs):
        terms, (whole, left, right) = refs[:-3], refs[-3:]
        for out, first in ((left, 0), (right, half)):
            total = add_terms(terms, slice(first, first + half))
            for step in range(STEPS):
                here = slice(step * owned, (step + 1) * owned)
                at = step * columns + first
                value = (own[:, at : at + half].astype(F32) + total[here]).astype(BF16)
                out[here, :] = value
                whole[here, first : first + half] = value

    return pl.pallas_call(
        kernel,
        name="add_residual",
        out_shape=[jax.ShapeDtypeStruct((rows, n), BF16) for n in (columns, half, half)],
        in_specs=[VMEM] * (1 + len(terms)),
        out_specs=[VMEM] * 3,
        compiler_params=limit(4),
    )(own, *terms)


def norm_rows(blocks, gain):
    places = [(mask, first) for mask, first, _ in blocks]
    flat = [block for _, _, block in blocks]
    size, depth = flat[-1].shape
    rows = size * lax.axis_size("ffn")
    att = lax.axis_size("att")
    chips = att // 2
    share = rows // att

    def kernel(*refs):
        blocks, (gain, normed, tail, residual) = refs[: len(flat)], refs[len(flat) :]
        for (mask, first), block in zip(places, blocks):
            here = slice(first, first + block.shape[1])
            residual[mask * size : (mask + 1) * size, here] = block[...]
        me = lax.axis_index("att")
        chip, core = me // 2, lax.rem(me, 2)
        for side in range(2):
            for d in range(chips):
                owner = lax.rem(chip + d, chips) * 2 + lax.rem(core + side, 2)
                part = residual[pl.ds(pl.multiple_of(owner * share, share), share), :].astype(F32)
                here = slice((side * chips + d) * share, (side * chips + d + 1) * share)
                normed[here, :] = (part * gain[...]).astype(BF16)
                squares = jnp.sum(part * part, axis=1, keepdims=True)
                high = squares.astype(BF16).astype(F32)
                lane = lax.broadcasted_iota(jnp.int32, (share, HD), 1)
                tail[here, :] = jnp.where(lane == 0, high, squares - high).astype(BF16)

    return pl.pallas_call(
        kernel,
        name="norm_rows",
        out_shape=[
            jax.ShapeDtypeStruct((rows, depth), BF16),
            jax.ShapeDtypeStruct((rows, HD), BF16),
        ],
        in_specs=[VMEM] * (len(flat) + 1),
        out_specs=[VMEM] * 2,
        scratch_shapes=[pltpu.VMEM((rows, depth), BF16)],
        compiler_params=limit(4),
    )(*flat, gain)


def widen(normed, tail, w_gate, w_up, first, count, after):
    rows, depth = normed.shape
    half = rows // 2
    width = count * 2 * BLOCK + HD

    def kernel(normed, tail, gate, up, *refs):
        keep, send = refs[-2:]
        keep[:, count * 2 * BLOCK :] = tail[:half, :]
        send[:, count * 2 * BLOCK :] = tail[half:, :]
        for j in range(count):
            for which, w in enumerate((gate, up)):
                at = (first + j) * BLOCK
                product = dot(normed[...], w[:, at : at + BLOCK])
                here = slice((2 * j + which) * BLOCK, (2 * j + which + 1) * BLOCK)
                keep[:, here] = product[:half].astype(BF16)
                send[:, here] = product[half:].astype(BF16)

    return pl.pallas_call(
        kernel,
        name="widen",
        out_shape=[jax.ShapeDtypeStruct((half, width), BF16)] * 2,
        in_specs=[VMEM] * (4 + len(after)),
        out_specs=[VMEM] * 2,
        compiler_params=limit(4),
        cost_estimate=matmul_cost(rows, depth, count * 2 * BLOCK),
    )(normed, tail, vmem(w_gate), vmem(w_up), *after)


def gate_rows(own, moved, model):
    share, width = own.shape
    count = width // (2 * BLOCK)
    others = len(moved)

    def kernel(*refs):
        own, moved, out = refs[0], refs[1 : 1 + others], refs[-1]

        def total(here):
            value = own[:, here]
            for part in moved:
                value = value + part[:, here].astype(F32)
            return value

        tail = total(slice(count * 2 * BLOCK, count * 2 * BLOCK + HD))
        factor = lax.rsqrt((tail[:, 0:1] + tail[:, 1:2]) / model + EPSILON)
        for j in range(count):
            gate = total(slice(2 * j * BLOCK, (2 * j + 1) * BLOCK)) * factor
            up = total(slice((2 * j + 1) * BLOCK, (2 * j + 2) * BLOCK)) * factor
            out[:, j * BLOCK : (j + 1) * BLOCK] = (gate / (1.0 + jnp.exp(-gate)) * up).astype(BF16)

    return pl.pallas_call(
        kernel,
        name="gate",
        out_shape=jax.ShapeDtypeStruct((share, count * BLOCK), BF16),
        in_specs=[VMEM] * (1 + others),
        out_specs=VMEM,
        compiler_params=limit(4),
        cost_estimate=pl.CostEstimate(flops=WAIT, bytes_accessed=0, transcendentals=0),
    )(own, *moved)


def place_rows(chunks):
    sizes = [same.shape[1] for same, _ in chunks]
    rows = 2 * chunks[0][0].shape[0]

    def kernel(*refs):
        out, at = refs[-1], 0
        for k, size in enumerate(sizes):
            place_gathered(refs[2 * k], refs[2 * k + 1], out, slice(at, at + size))
            at += size

    return pl.pallas_call(
        kernel,
        name="place_rows",
        out_shape=jax.ShapeDtypeStruct((rows, sum(sizes)), BF16),
        in_specs=[VMEM] * (2 * len(sizes)),
        out_specs=VMEM,
        compiler_params=limit(4),
    )(*[x for pair in chunks for x in pair])


def finish(residual, terms):
    rows, columns = residual.shape
    half = columns // 2

    def kernel(residual, *refs):
        for first in (0, half):
            here = slice(first, first + half)
            total = add_terms(refs[:-1], here)
            refs[-1][:, here] = (residual[:, here].astype(F32) + total).astype(BF16)

    return pl.pallas_call(
        kernel,
        name="finish",
        out_shape=jax.ShapeDtypeStruct((rows, columns), BF16),
        in_specs=[VMEM] * (1 + len(terms)),
        out_specs=VMEM,
        compiler_params=limit(4),
    )(residual, *terms)


def local(
    incoming, queries, new_kv, cache, lengths, slot_of, w_out, norm_gain, w_gate, w_up, w_down
):
    ffn = lax.axis_size("ffn")
    att = lax.axis_size("att")
    requests = slot_of.shape[0]
    slots = cache.shape[0]
    model = w_out.shape[1]
    width = w_gate.shape[1]
    owned = requests // ffn

    whole = lambda x: (x, x.shape[0])
    queries, new_kv, token = load([whole(queries), whole(new_kv)], "load_new")
    qkv = jnp.concatenate([queries.reshape(slots, -1), new_kv.reshape(slots, -1)], axis=1)
    small = [whole(slot_of.reshape(1, requests)), whole(lengths.reshape(1, slots))]
    cache, slot_row, lengths, own, token = load(
        [whole(cache)] + small + [(incoming, owned)], "load_cache", [corner(qkv)]
    )
    own = own.reshape(owned, STEPS * model)
    same, other = gather_att(qkv, [token])
    attended = attend(lengths, slot_row, same, other, cache)
    w_out, token = load([whole(w_out)], "load_out", [corner(attended)])
    rows = order_rows(slot_row, *gather_att(attended, [token]))
    sums = reduce_ffn(*multiply(rows, w_out, "project"))

    residual, left, right = add_residual(own, sums)
    normed, tail = norm_rows(gather_ffn(residual, left, right), norm_gain.reshape(1, model))
    blocks, whole_of = width // BLOCK, sum(CHUNKS)
    edges = [blocks * sum(CHUNKS[:k]) // whole_of for k in range(len(CHUNKS) + 1)]
    pairs = []
    for k, (first, last) in enumerate(zip(edges[:-1], edges[1:])):
        after = [corner(keep)] if k == 1 else [corner(pairs[k - 2][1])] if k else []
        keep, send = widen(normed, tail, w_gate, w_up, first, last - first, after)
        pairs.append(add_parts(keep, exchange(send, "att", 1), att // 2, F32))
    moved = [
        [shift(part, "att", 2 * (d + 1)) for d, part in enumerate(away)] for _, *away in pairs
    ]
    chunks = [
        gather_att(gate_rows(pair[0], parts, model * att))
        for pair, parts in zip(pairs, moved)
    ]
    hidden = place_rows(chunks)
    out = finish(residual, reduce_ffn(*multiply(hidden, w_down, "narrow")))
    return jnp.swapaxes(out.reshape(STEPS, owned, model), 0, 1)


def solution(mesh):
    return jax.shard_map(
        local,
        mesh=mesh,
        in_specs=(
            P("parts", None, "att"),
            P(("parts", "att"), None, "ffn"),
            P(("parts", "att"), None, "ffn"),
            P(("parts", "att"), None, "ffn"),
            P(("parts", "att")),
            P("parts"),
            P("ffn", "att"),
            P("att"),
            P("att", "ffn"),
            P("att", "ffn"),
            P("ffn", "att"),
        ),
        out_specs=P(("parts", "ffn"), None, "att"),
        check_vma=False,
    )
```

```python
import functools

import jax
import jax.numpy as jnp
from jax import lax
from jax.experimental import pallas as pl
from jax.experimental.pallas import tpu as pltpu
from jax.sharding import PartitionSpec as P

H = 64
KVH = 8
HD = 128
STEPS = 2
GROUPS = H // KVH
EPSILON = 1e-05
BLOCK = 256
CHUNKS = (2, 3, 2)
WAIT = 2 * 10**9
F32 = jnp.float32
BF16 = jnp.bfloat16
MIB = 1024 * 1024


def dot(a, b):
    return jnp.dot(a, b, preferred_element_type=F32)

VMEM = pl.BlockSpec(memory_space=pltpu.VMEM)
ANY = pl.BlockSpec(memory_space=pl.ANY)


def shift(x, axis, d):
    n = lax.axis_size(axis)
    return lax.ppermute(x, axis, [(i, (i + d) % n) for i in range(n)])


def exchange(x, axis, bit):
    return lax.ppermute(x, axis, [(i, i ^ bit) for i in range(lax.axis_size(axis))])


def corner(x):
    return x[:8, :HD]


def limit(mib):
    return pltpu.CompilerParams(vmem_limit_bytes=mib * MIB)


def join(blocks, after=()):
    count = len(blocks)
    rows = [block.shape[0] for block in blocks]

    def kernel(*refs):
        out, at = refs[-1], 0
        for ref, size in zip(refs[:count], rows):
            out[at : at + size, :] = ref[...]
            at += size

    return pl.pallas_call(
        kernel,
        name="join",
        out_shape=jax.ShapeDtypeStruct((sum(rows), blocks[0].shape[1]), blocks[0].dtype),
        in_specs=[VMEM] * (count + len(after)),
        out_specs=VMEM,
        compiler_params=limit(4),
    )(*blocks, *after)


def gather_att(x, token=()):
    chips = lax.axis_size("att") // 2
    same = join([x] + [shift(x, "att", 2 * d) for d in range(1, chips)], token)
    return same, exchange(same, "att", 1)


def place_gathered(same, other, whole, columns=slice(None)):
    me, chips = lax.axis_index("att"), lax.axis_size("att") // 2
    rows = same.shape[0] // chips
    for d in range(chips):
        chip = lax.rem(me // 2 + chips - d, chips)
        for side, ref in enumerate((same, other)):
            source = chip * 2 + lax.rem(me + side, 2)
            at = pl.multiple_of(source * rows, rows)
            whole[pl.ds(at, rows), columns] = ref[d * rows : (d + 1) * rows, :]


def reduce_ffn(own, *others):
    masks = list(range(2, len(others) + 1)) + [1]
    return [own] + [exchange(others[mask - 1], "ffn", mask) for mask in masks]


def add_terms(refs, columns):
    total = refs[0][:, columns]
    for term in refs[1:]:
        total = total + term[:, columns].astype(F32)
    return total


def gather_ffn(x, left, right):
    ffn, half = lax.axis_size("ffn"), left.shape[1]
    blocks = [(1, 0, exchange(x, "ffn", 1))]
    for mask in range(2, ffn, 2):
        moved = exchange(right, "ffn", mask)
        blocks += [(mask + 1, half, exchange(moved, "ffn", 1)), (mask, half, moved)]
    blocks += [(mask, 0, exchange(left, "ffn", mask)) for mask in range(ffn - 1, 1, -1)]
    return blocks + [(0, 0, x)]


def vmem(x):
    return pltpu.with_memory_space_constraint(x, pltpu.VMEM)


def hbm(x):
    return pltpu.with_memory_space_constraint(x, pltpu.HBM)


class Copies:
    def __init__(self, entries):
        self.entries = entries
        self.sources = [hbm(x) for x, _ in entries]
        self.shapes = [pltpu.VMEM((n,) + x.shape[1:], x.dtype) for x, n in entries]
        self.scratch = pltpu.SemaphoreType.DMA((len(entries), 8))
        self.bytes = sum(2 * x.size // x.shape[0] * n * x.dtype.itemsize for x, n in entries)

    def started(self, sources, targets, sems):
        copies = []
        for k, (x, rows) in enumerate(self.entries):
            parts = 8 if rows % 8 == 0 and x.size >= MIB else 1
            size = rows // parts
            begin = 0 if rows == x.shape[0] else lax.axis_index("ffn") * rows
            for p in range(parts):
                copies.append(
                    pltpu.make_async_copy(
                        sources[k].at[pl.ds(begin + p * size, size)],
                        targets[k].at[pl.ds(p * size, size)],
                        sems.at[k, p],
                    )
                )
        for copy in copies:
            copy.start()
        return copies


def load(entries, name, after=()):
    work = Copies(entries)
    count = len(entries)

    def kernel(*refs):
        targets, token, sems = refs[-2 - count : -2], refs[-2], refs[-1]
        copies = work.started(refs[:count], targets, sems)
        token[...] = jnp.zeros_like(token)
        for copy in copies:
            copy.wait()

    return pl.pallas_call(
        kernel,
        name=name,
        out_shape=work.shapes + [jax.ShapeDtypeStruct((8, HD), F32)],
        in_specs=[ANY] * count + [VMEM] * len(after),
        out_specs=[VMEM] * (count + 1),
        scratch_shapes=[work.scratch],
        compiler_params=limit(1),
        cost_estimate=pl.CostEstimate(flops=0, bytes_accessed=work.bytes, transcendentals=0),
    )(*work.sources, *after)


def attend(lengths, slot_row, same, other, cache):
    slots, cap, width = cache.shape
    kv_local = width // (2 * HD)
    heads = kv_local * GROUPS
    rows = STEPS * heads
    requests = slot_row.shape[1]
    fresh_at = STEPS * heads * HD
    columns = fresh_at + STEPS * width
    factor = HD ** (-0.5) * 1.4426950408889634

    def kernel(lengths, slot_row, same, other, cache, out, *scratch):
        qkv, qs, fresh, wide, scores, fresh_scores, mixed = scratch
        place_gathered(same, other, qkv)
        base = lax.axis_index("att") * slots
        wanted = lax.broadcasted_iota(jnp.int32, (slots, requests), 0) + base
        pick = jnp.where(slot_row[...] == wanted, 1.0, 0.0).astype(BF16)
        mine = dot(pick, qkv[...])
        for s in range(STEPS):
            for h in range(heads):
                at = (s * heads + h) * HD
                qs[pl.ds(s * heads + h, slots, stride=rows), :] = mine[:, at : at + HD]
            fresh[s * slots : (s + 1) * slots, :] = mine[
                :, fresh_at + s * width : fresh_at + (s + 1) * width
            ].astype(BF16)
        group_of = lax.broadcasted_iota(jnp.int32, (slots * rows, HD), 0) % heads // GROUPS
        for g in range(kv_local):
            own = jnp.where(group_of == g, qs[...], 0.0)
            wide[:, g * HD : (g + 1) * HD] = own.astype(BF16)

        def of_groups(rows_kept, which):
            at = [g * 2 * HD + which * HD for g in range(kv_local)]
            return jnp.concatenate([rows_kept[:, first : first + HD] for first in at], axis=1)

        across = (((1,), (1,)), ((), ()))
        fresh_scores[...] = lax.dot_general(
            wide[...], of_groups(fresh, 0), across, preferred_element_type=F32
        )
        for i in range(slots):
            here = slice(i * rows, (i + 1) * rows)
            scores[here, :] = lax.dot_general(
                wide[here, :], of_groups(cache.at[i], 0), across, preferred_element_type=F32
            )
        key_at = lax.broadcasted_iota(jnp.int32, (rows, cap), 1)
        fresh_step = lax.broadcasted_iota(jnp.int32, (rows, STEPS * slots), 1)
        row_step = lax.broadcasted_iota(jnp.int32, (rows, STEPS * slots), 0) // heads
        for i in range(slots):
            here = slice(i * rows, (i + 1) * rows)
            kept = jnp.where(key_at < lengths[:, i : i + 1], scores[here, :], -jnp.inf)
            own = (fresh_step % slots == i) & (fresh_step // slots <= row_step)
            new = jnp.where(own, fresh_scores[here, :], -jnp.inf)
            top = jnp.maximum(
                jnp.max(kept, axis=1, keepdims=True), jnp.max(new, axis=1, keepdims=True)
            )
            kept = jnp.exp2((kept - top) * factor)
            new = jnp.exp2((new - top) * factor)
            total = jnp.sum(kept, axis=1, keepdims=True) + jnp.sum(new, axis=1, keepdims=True)
            values = dot(kept.astype(BF16), of_groups(cache.at[i], 1))
            values = values + dot(new.astype(BF16), of_groups(fresh, 1))
            values = values / total
            for s in range(STEPS):
                for g in range(kv_local):
                    at = s * heads + g * GROUPS
                    mixed[i * rows + at : i * rows + at + GROUPS, :] = values[
                        at : at + GROUPS, g * HD : (g + 1) * HD
                    ]
        for s in range(STEPS):
            for h in range(heads):
                out[s * slots : (s + 1) * slots, h * HD : (h + 1) * HD] = mixed[
                    pl.ds(s * heads + h, slots, stride=rows), :
                ].astype(BF16)
    return pl.pallas_call(
        kernel,
        name="attend",
        out_shape=jax.ShapeDtypeStruct((STEPS * slots, heads * HD), BF16),
        in_specs=[VMEM] * 5,
        out_specs=VMEM,
        scratch_shapes=[
            pltpu.VMEM((requests, columns), BF16),
            pltpu.VMEM((slots * rows, HD), F32),
            pltpu.VMEM((STEPS * slots, width), BF16),
            pltpu.VMEM((slots * rows, kv_local * HD), BF16),
            pltpu.VMEM((slots * rows, cap), F32),
            pltpu.VMEM((slots * rows, STEPS * slots), F32),
            pltpu.VMEM((slots * rows, HD), F32),
        ],
        compiler_params=limit(6),
        cost_estimate=pl.CostEstimate(
            flops=4 * slots * rows * cap * width,
            bytes_accessed=slots * cap * width * 2,
            transcendentals=slots * rows * cap,
        ),
    )(lengths, slot_row, same, other, cache)


def matmul_cost(rows, depth, columns):
    return pl.CostEstimate(
        flops=2 * rows * depth * columns,
        bytes_accessed=2 * (rows * depth + depth * columns + rows * columns),
        transcendentals=0,
    )


def order_rows(slot_row, same, other):
    requests = slot_row.shape[1]
    rows = STEPS * requests
    depth = same.shape[1]
    slots = requests // lax.axis_size("att")
    ffn = lax.axis_size("ffn")
    owned = requests // ffn

    def kernel(slot_row, same, other, out, gathered, natural):
        place_gathered(same, other, gathered)
        slot = slot_row[...]
        first = lax.div(slot, slots) * (STEPS * slots) + lax.rem(slot, slots)
        at = lax.broadcasted_iota(jnp.int32, (rows, requests), 0)
        me = lax.axis_index("ffn")
        for step in range(STEPS):
            pick = jnp.where(at == first + step * slots, 1.0, 0.0).astype(BF16)
            picked = lax.dot_general(
                pick, gathered[...], (((0,), (0,)), ((), ())), preferred_element_type=F32
            )
            natural[...] = picked.astype(BF16)
            for r in range(ffn):
                owner = jnp.bitwise_xor(me, r)
                here = slice((r * STEPS + step) * owned, (r * STEPS + step + 1) * owned)
                out[here, :] = natural[pl.ds(pl.multiple_of(owner * owned, owned), owned), :]

    return pl.pallas_call(
        kernel,
        name="order_rows",
        out_shape=jax.ShapeDtypeStruct((rows, depth), BF16),
        in_specs=[VMEM] * 3,
        out_specs=VMEM,
        scratch_shapes=[pltpu.VMEM((rows, depth), BF16), pltpu.VMEM((requests, depth), BF16)],
        compiler_params=limit(4),
    )(slot_row, same, other)


def multiply(rows, w, name):
    columns = w.shape[1]
    count, depth = rows.shape
    ffn = lax.axis_size("ffn")
    share = count // ffn
    block = min(512, columns)

    def kernel(rows, w, *outs):
        for j in range(columns // block):
            here = slice(j * block, (j + 1) * block)
            product = dot(rows[...], w[:, here])
            for r, out in enumerate(outs):
                out[:, here] = product[r * share : (r + 1) * share].astype(out.dtype)

    return pl.pallas_call(
        kernel,
        name=name,
        out_shape=[
            jax.ShapeDtypeStruct((share, columns), BF16 if r else F32) for r in range(ffn)
        ],
        in_specs=[VMEM] * 2,
        out_specs=[VMEM] * ffn,
        compiler_params=limit(4),
        cost_estimate=matmul_cost(count, depth, columns),
    )(rows, vmem(w))


def add_parts(keep, arrived, parts, first=BF16):
    rows, width = keep.shape
    share = rows // parts
    types = [first] + [BF16] * (parts - 1)

    def kernel(keep, arrived, *outs):
        for d, out in enumerate(outs):
            here = slice(d * share, (d + 1) * share)
            out[...] = (keep[here, :].astype(F32) + arrived[here, :].astype(F32)).astype(out.dtype)

    return pl.pallas_call(
        kernel,
        name="add_parts",
        out_shape=[jax.ShapeDtypeStruct((share, width), kind) for kind in types],
        in_specs=[VMEM] * 2,
        out_specs=[VMEM] * parts,
        compiler_params=limit(4),
    )(keep, arrived)


def add_residual(own, terms):
    rows, columns = terms[0].shape
    owned, half = rows // STEPS, columns // 2

    def kernel(own, *refs):
        terms, (whole, left, right) = refs[:-3], refs[-3:]
        for out, first in ((left, 0), (right, half)):
            total = add_terms(terms, slice(first, first + half))
            for step in range(STEPS):
                here = slice(step * owned, (step + 1) * owned)
                at = step * columns + first
                value = (own[:, at : at + half].astype(F32) + total[here]).astype(BF16)
                out[here, :] = value
                whole[here, first : first + half] = value

    return pl.pallas_call(
        kernel,
        name="add_residual",
        out_shape=[jax.ShapeDtypeStruct((rows, n), BF16) for n in (columns, half, half)],
        in_specs=[VMEM] * (1 + len(terms)),
        out_specs=[VMEM] * 3,
        compiler_params=limit(4),
    )(own, *terms)


def norm_rows(blocks, gain):
    places = [(mask, first) for mask, first, _ in blocks]
    flat = [block for _, _, block in blocks]
    size, depth = flat[-1].shape
    rows = size * lax.axis_size("ffn")
    att = lax.axis_size("att")
    chips = att // 2
    share = rows // att

    def kernel(*refs):
        blocks, (gain, normed, tail, residual) = refs[: len(flat)], refs[len(flat) :]
        for (mask, first), block in zip(places, blocks):
            here = slice(first, first + block.shape[1])
            residual[mask * size : (mask + 1) * size, here] = block[...]
        me = lax.axis_index("att")
        chip, core = me // 2, lax.rem(me, 2)
        for side in range(2):
            for d in range(chips):
                owner = lax.rem(chip + d, chips) * 2 + lax.rem(core + side, 2)
                part = residual[pl.ds(pl.multiple_of(owner * share, share), share), :].astype(F32)
                here = slice((side * chips + d) * share, (side * chips + d + 1) * share)
                normed[here, :] = (part * gain[...]).astype(BF16)
                squares = jnp.sum(part * part, axis=1, keepdims=True)
                high = squares.astype(BF16).astype(F32)
                lane = lax.broadcasted_iota(jnp.int32, (share, HD), 1)
                tail[here, :] = jnp.where(lane == 0, high, squares - high).astype(BF16)

    return pl.pallas_call(
        kernel,
        name="norm_rows",
        out_shape=[
            jax.ShapeDtypeStruct((rows, depth), BF16),
            jax.ShapeDtypeStruct((rows, HD), BF16),
        ],
        in_specs=[VMEM] * (len(flat) + 1),
        out_specs=[VMEM] * 2,
        scratch_shapes=[pltpu.VMEM((rows, depth), BF16)],
        compiler_params=limit(4),
    )(*flat, gain)


def widen(normed, tail, w_gate, w_up, first, count, after):
    rows, depth = normed.shape
    half = rows // 2
    width = count * 2 * BLOCK + HD

    def kernel(normed, tail, gate, up, *refs):
        keep, send = refs[-2:]
        keep[:, count * 2 * BLOCK :] = tail[:half, :]
        send[:, count * 2 * BLOCK :] = tail[half:, :]
        for j in range(count):
            for which, w in enumerate((gate, up)):
                at = (first + j) * BLOCK
                product = dot(normed[...], w[:, at : at + BLOCK])
                here = slice((2 * j + which) * BLOCK, (2 * j + which + 1) * BLOCK)
                keep[:, here] = product[:half].astype(BF16)
                send[:, here] = product[half:].astype(BF16)

    return pl.pallas_call(
        kernel,
        name="widen",
        out_shape=[jax.ShapeDtypeStruct((half, width), BF16)] * 2,
        in_specs=[VMEM] * (4 + len(after)),
        out_specs=[VMEM] * 2,
        compiler_params=limit(4),
        cost_estimate=matmul_cost(rows, depth, count * 2 * BLOCK),
    )(normed, tail, vmem(w_gate), vmem(w_up), *after)


def gate_rows(own, moved, model):
    share, width = own.shape
    count = width // (2 * BLOCK)
    others = len(moved)

    def kernel(*refs):
        own, moved, out = refs[0], refs[1 : 1 + others], refs[-1]

        def total(here):
            value = own[:, here]
            for part in moved:
                value = value + part[:, here].astype(F32)
            return value

        tail = total(slice(count * 2 * BLOCK, count * 2 * BLOCK + HD))
        factor = lax.rsqrt((tail[:, 0:1] + tail[:, 1:2]) / model + EPSILON)
        for j in range(count):
            gate = total(slice(2 * j * BLOCK, (2 * j + 1) * BLOCK)) * factor
            up = total(slice((2 * j + 1) * BLOCK, (2 * j + 2) * BLOCK)) * factor
            out[:, j * BLOCK : (j + 1) * BLOCK] = (gate / (1.0 + jnp.exp(-gate)) * up).astype(BF16)

    return pl.pallas_call(
        kernel,
        name="gate",
        out_shape=jax.ShapeDtypeStruct((share, count * BLOCK), BF16),
        in_specs=[VMEM] * (1 + others),
        out_specs=VMEM,
        compiler_params=limit(4),
        cost_estimate=pl.CostEstimate(flops=WAIT, bytes_accessed=0, transcendentals=0),
    )(own, *moved)


def place_rows(chunks):
    sizes = [same.shape[1] for same, _ in chunks]
    rows = 2 * chunks[0][0].shape[0]

    def kernel(*refs):
        out, at = refs[-1], 0
        for k, size in enumerate(sizes):
            place_gathered(refs[2 * k], refs[2 * k + 1], out, slice(at, at + size))
            at += size

    return pl.pallas_call(
        kernel,
        name="place_rows",
        out_shape=jax.ShapeDtypeStruct((rows, sum(sizes)), BF16),
        in_specs=[VMEM] * (2 * len(sizes)),
        out_specs=VMEM,
        compiler_params=limit(4),
    )(*[x for pair in chunks for x in pair])


def finish(residual, terms):
    rows, columns = residual.shape
    half = columns // 2

    def kernel(residual, *refs):
        for first in (0, half):
            here = slice(first, first + half)
            total = add_terms(refs[:-1], here)
            refs[-1][:, here] = (residual[:, here].astype(F32) + total).astype(BF16)

    return pl.pallas_call(
        kernel,
        name="finish",
        out_shape=jax.ShapeDtypeStruct((rows, columns), BF16),
        in_specs=[VMEM] * (1 + len(terms)),
        out_specs=VMEM,
        compiler_params=limit(4),
    )(residual, *terms)


def local(
    incoming, queries, new_kv, cache, lengths, slot_of, w_out, norm_gain, w_gate, w_up, w_down
):
    ffn = lax.axis_size("ffn")
    att = lax.axis_size("att")
    requests = slot_of.shape[0]
    slots = cache.shape[0]
    model = w_out.shape[1]
    width = w_gate.shape[1]
    owned = requests // ffn

    whole = lambda x: (x, x.shape[0])
    queries, new_kv, token = load([whole(queries), whole(new_kv)], "load_new")
    qkv = jnp.concatenate([queries.reshape(slots, -1), new_kv.reshape(slots, -1)], axis=1)
    small = [whole(slot_of.reshape(1, requests)), whole(lengths.reshape(1, slots))]
    cache, slot_row, lengths, own, token = load(
        [whole(cache)] + small + [(incoming, owned)], "load_cache", [corner(qkv)]
    )
    own = own.reshape(owned, STEPS * model)
    same, other = gather_att(qkv, [token])
    attended = attend(lengths, slot_row, same, other, cache)
    w_out, token = load([whole(w_out)], "load_out", [corner(attended)])
    rows = order_rows(slot_row, *gather_att(attended, [token]))
    sums = reduce_ffn(*multiply(rows, w_out, "project"))

    residual, left, right = add_residual(own, sums)
    normed, tail = norm_rows(gather_ffn(residual, left, right), norm_gain.reshape(1, model))
    blocks, whole_of = width // BLOCK, sum(CHUNKS)
    edges = [blocks * sum(CHUNKS[:k]) // whole_of for k in range(len(CHUNKS) + 1)]
    pairs = []
    for k, (first, last) in enumerate(zip(edges[:-1], edges[1:])):
        after = [corner(keep)] if k == 1 else [corner(pairs[k - 2][1])] if k else []
        keep, send = widen(normed, tail, w_gate, w_up, first, last - first, after)
        pairs.append(add_parts(keep, exchange(send, "att", 1), att // 2, F32))
    moved = [
        [shift(part, "att", 2 * (d + 1)) for d, part in enumerate(away)] for _, *away in pairs
    ]
    chunks = [
        gather_att(gate_rows(pair[0], parts, model * att))
        for pair, parts in zip(pairs, moved)
    ]
    hidden = place_rows(chunks)
    out = finish(residual, reduce_ffn(*multiply(hidden, w_down, "narrow")))
    return jnp.swapaxes(out.reshape(STEPS, owned, model), 0, 1)


def solution(mesh):
    return jax.shard_map(
        local,
        mesh=mesh,
        in_specs=(
            P("parts", None, "att"),
            P(("parts", "att"), None, "ffn"),
            P(("parts", "att"), None, "ffn"),
            P(("parts", "att"), None, "ffn"),
            P(("parts", "att")),
            P("parts"),
            P("ffn", "att"),
            P("att"),
            P("att", "ffn"),
            P("att", "ffn"),
            P("ffn", "att"),
        ),
        out_specs=P(("parts", "ffn"), None, "att"),
        check_vma=False,
    )
```

```python
import functools

import jax
import jax.numpy as jnp
from jax import lax
from jax.experimental import pallas as pl
from jax.experimental.pallas import tpu as pltpu
from jax.sharding import PartitionSpec as P

H = 64
KVH = 8
HD = 128
STEPS = 2
GROUPS = H // KVH
EPSILON = 1e-05
BLOCK = 256
CHUNKS = (2, 3, 2)
WAIT = 2 * 10**9
F32 = jnp.float32
BF16 = jnp.bfloat16
MIB = 1024 * 1024


def dot(a, b):
    return jnp.dot(a, b, preferred_element_type=F32)

VMEM = pl.BlockSpec(memory_space=pltpu.VMEM)
ANY = pl.BlockSpec(memory_space=pl.ANY)


def shift(x, axis, d):
    n = lax.axis_size(axis)
    return lax.ppermute(x, axis, [(i, (i + d) % n) for i in range(n)])


def exchange(x, axis, bit):
    return lax.ppermute(x, axis, [(i, i ^ bit) for i in range(lax.axis_size(axis))])


def corner(x):
    return x[:8, :HD]


def limit(mib):
    return pltpu.CompilerParams(vmem_limit_bytes=mib * MIB)


def join(blocks, after=()):
    count = len(blocks)
    rows = [block.shape[0] for block in blocks]

    def kernel(*refs):
        out, at = refs[-1], 0
        for ref, size in zip(refs[:count], rows):
            out[at : at + size, :] = ref[...]
            at += size

    return pl.pallas_call(
        kernel,
        name="join",
        out_shape=jax.ShapeDtypeStruct((sum(rows), blocks[0].shape[1]), blocks[0].dtype),
        in_specs=[VMEM] * (count + len(after)),
        out_specs=VMEM,
        compiler_params=limit(4),
    )(*blocks, *after)


def gather_att(x, token=()):
    chips = lax.axis_size("att") // 2
    same = join([x] + [shift(x, "att", 2 * d) for d in range(1, chips)], token)
    return same, exchange(same, "att", 1)


def place_gathered(same, other, whole, columns=slice(None)):
    me, chips = lax.axis_index("att"), lax.axis_size("att") // 2
    rows = same.shape[0] // chips
    for d in range(chips):
        chip = lax.rem(me // 2 + chips - d, chips)
        for side, ref in enumerate((same, other)):
            source = chip * 2 + lax.rem(me + side, 2)
            at = pl.multiple_of(source * rows, rows)
            whole[pl.ds(at, rows), columns] = ref[d * rows : (d + 1) * rows, :]


def reduce_ffn(own, near, keep, far, *ahead):
    direct = [exchange(rows, "ffn", k + 2) for k, rows in enumerate(ahead)]
    sums = add_parts(keep, exchange(far, "ffn", 1), len(ahead) // 2)
    across = [exchange(part, "ffn", 2 * (k + 1)) for k, part in enumerate(sums)]
    return [own, *direct, *across, exchange(near, "ffn", 1)]


def add_terms(refs, columns):
    own, rest, near = refs[0], refs[1:-1], refs[-1]
    half = own.shape[1] // 2
    direct = 2 * len(rest) // 3
    left = columns.stop <= half
    total = own[:, columns] + near[:, columns].astype(F32)
    here = columns if left else slice(columns.start - half, columns.stop - half)
    for term in rest[:direct] if left else rest[direct:]:
        total = total + term[:, here].astype(F32)
    return total


def reduce_direct(own, *others):
    masks = list(range(2, len(others) + 1)) + [1]
    return [own] + [exchange(others[mask - 1], "ffn", mask) for mask in masks]


def gather_ffn(x, left, right):
    ffn, half = lax.axis_size("ffn"), left.shape[1]
    blocks = [(1, 0, exchange(x, "ffn", 1))]
    for mask in range(2, ffn, 2):
        moved = exchange(right, "ffn", mask)
        blocks += [(mask + 1, half, exchange(moved, "ffn", 1)), (mask, half, moved)]
    blocks += [(mask, 0, exchange(left, "ffn", mask)) for mask in range(ffn - 1, 1, -1)]
    return blocks + [(0, 0, x)]


def vmem(x):
    return pltpu.with_memory_space_constraint(x, pltpu.VMEM)


def hbm(x):
    return pltpu.with_memory_space_constraint(x, pltpu.HBM)


class Copies:
    def __init__(self, entries):
        self.entries = entries
        self.sources = [hbm(x) for x, _ in entries]
        self.shapes = [pltpu.VMEM((n,) + x.shape[1:], x.dtype) for x, n in entries]
        self.scratch = pltpu.SemaphoreType.DMA((len(entries), 8))
        self.bytes = sum(2 * x.size // x.shape[0] * n * x.dtype.itemsize for x, n in entries)

    def started(self, sources, targets, sems):
        copies = []
        for k, (x, rows) in enumerate(self.entries):
            parts = 8 if rows % 8 == 0 and x.size >= MIB else 1
            size = rows // parts
            begin = 0 if rows == x.shape[0] else lax.axis_index("ffn") * rows
            for p in range(parts):
                copies.append(
                    pltpu.make_async_copy(
                        sources[k].at[pl.ds(begin + p * size, size)],
                        targets[k].at[pl.ds(p * size, size)],
                        sems.at[k, p],
                    )
                )
        for copy in copies:
            copy.start()
        return copies


def load(entries, name, after=()):
    work = Copies(entries)
    count = len(entries)

    def kernel(*refs):
        targets, token, sems = refs[-2 - count : -2], refs[-2], refs[-1]
        copies = work.started(refs[:count], targets, sems)
        token[...] = jnp.zeros_like(token)
        for copy in copies:
            copy.wait()

    return pl.pallas_call(
        kernel,
        name=name,
        out_shape=work.shapes + [jax.ShapeDtypeStruct((8, HD), F32)],
        in_specs=[ANY] * count + [VMEM] * len(after),
        out_specs=[VMEM] * (count + 1),
        scratch_shapes=[work.scratch],
        compiler_params=limit(1),
        cost_estimate=pl.CostEstimate(flops=0, bytes_accessed=work.bytes, transcendentals=0),
    )(*work.sources, *after)


def attend(lengths, slot_row, same, other, cache):
    slots, cap, width = cache.shape
    kv_local = width // (2 * HD)
    heads = kv_local * GROUPS
    rows = STEPS * heads
    requests = slot_row.shape[1]
    fresh_at = STEPS * heads * HD
    columns = fresh_at + STEPS * width
    factor = HD ** (-0.5) * 1.4426950408889634

    def kernel(lengths, slot_row, same, other, cache, out, *scratch):
        qkv, qs, fresh, wide, scores, fresh_scores, mixed = scratch
        place_gathered(same, other, qkv)
        base = lax.axis_index("att") * slots
        wanted = lax.broadcasted_iota(jnp.int32, (slots, requests), 0) + base
        pick = jnp.where(slot_row[...] == wanted, 1.0, 0.0).astype(BF16)
        mine = dot(pick, qkv[...])
        for s in range(STEPS):
            for h in range(heads):
                at = (s * heads + h) * HD
                qs[pl.ds(s * heads + h, slots, stride=rows), :] = mine[:, at : at + HD]
            fresh[s * slots : (s + 1) * slots, :] = mine[
                :, fresh_at + s * width : fresh_at + (s + 1) * width
            ].astype(BF16)
        group_of = lax.broadcasted_iota(jnp.int32, (slots * rows, HD), 0) % heads // GROUPS
        for g in range(kv_local):
            own = jnp.where(group_of == g, qs[...], 0.0)
            wide[:, g * HD : (g + 1) * HD] = own.astype(BF16)

        def of_groups(rows_kept, which):
            at = [g * 2 * HD + which * HD for g in range(kv_local)]
            return jnp.concatenate([rows_kept[:, first : first + HD] for first in at], axis=1)

        across = (((1,), (1,)), ((), ()))
        fresh_scores[...] = lax.dot_general(
            wide[...], of_groups(fresh, 0), across, preferred_element_type=F32
        )
        for i in range(slots):
            here = slice(i * rows, (i + 1) * rows)
            scores[here, :] = lax.dot_general(
                wide[here, :], of_groups(cache.at[i], 0), across, preferred_element_type=F32
            )
        key_at = lax.broadcasted_iota(jnp.int32, (rows, cap), 1)
        fresh_step = lax.broadcasted_iota(jnp.int32, (rows, STEPS * slots), 1)
        row_step = lax.broadcasted_iota(jnp.int32, (rows, STEPS * slots), 0) // heads
        for i in range(slots):
            here = slice(i * rows, (i + 1) * rows)
            kept = jnp.where(key_at < lengths[:, i : i + 1], scores[here, :], -jnp.inf)
            own = (fresh_step % slots == i) & (fresh_step // slots <= row_step)
            new = jnp.where(own, fresh_scores[here, :], -jnp.inf)
            top = jnp.maximum(
                jnp.max(kept, axis=1, keepdims=True), jnp.max(new, axis=1, keepdims=True)
            )
            kept = jnp.exp2((kept - top) * factor)
            new = jnp.exp2((new - top) * factor)
            total = jnp.sum(kept, axis=1, keepdims=True) + jnp.sum(new, axis=1, keepdims=True)
            values = dot(kept.astype(BF16), of_groups(cache.at[i], 1))
            values = values + dot(new.astype(BF16), of_groups(fresh, 1))
            values = values / total
            for s in range(STEPS):
                for g in range(kv_local):
                    at = s * heads + g * GROUPS
                    mixed[i * rows + at : i * rows + at + GROUPS, :] = values[
                        at : at + GROUPS, g * HD : (g + 1) * HD
                    ]
        for s in range(STEPS):
            for h in range(heads):
                out[s * slots : (s + 1) * slots, h * HD : (h + 1) * HD] = mixed[
                    pl.ds(s * heads + h, slots, stride=rows), :
                ].astype(BF16)
    return pl.pallas_call(
        kernel,
        name="attend",
        out_shape=jax.ShapeDtypeStruct((STEPS * slots, heads * HD), BF16),
        in_specs=[VMEM] * 5,
        out_specs=VMEM,
        scratch_shapes=[
            pltpu.VMEM((requests, columns), BF16),
            pltpu.VMEM((slots * rows, HD), F32),
            pltpu.VMEM((STEPS * slots, width), BF16),
            pltpu.VMEM((slots * rows, kv_local * HD), BF16),
            pltpu.VMEM((slots * rows, cap), F32),
            pltpu.VMEM((slots * rows, STEPS * slots), F32),
            pltpu.VMEM((slots * rows, HD), F32),
        ],
        compiler_params=limit(6),
        cost_estimate=pl.CostEstimate(
            flops=4 * slots * rows * cap * width,
            bytes_accessed=slots * cap * width * 2,
            transcendentals=slots * rows * cap,
        ),
    )(lengths, slot_row, same, other, cache)


def matmul_cost(rows, depth, columns):
    return pl.CostEstimate(
        flops=2 * rows * depth * columns,
        bytes_accessed=2 * (rows * depth + depth * columns + rows * columns),
        transcendentals=0,
    )


def order_rows(slot_row, same, other):
    requests = slot_row.shape[1]
    rows = STEPS * requests
    depth = same.shape[1]
    slots = requests // lax.axis_size("att")
    ffn = lax.axis_size("ffn")
    owned = requests // ffn

    def kernel(slot_row, same, other, out, gathered, natural):
        place_gathered(same, other, gathered)
        slot = slot_row[...]
        first = lax.div(slot, slots) * (STEPS * slots) + lax.rem(slot, slots)
        at = lax.broadcasted_iota(jnp.int32, (rows, requests), 0)
        me = lax.axis_index("ffn")
        for step in range(STEPS):
            pick = jnp.where(at == first + step * slots, 1.0, 0.0).astype(BF16)
            picked = lax.dot_general(
                pick, gathered[...], (((0,), (0,)), ((), ())), preferred_element_type=F32
            )
            natural[...] = picked.astype(BF16)
            for r in range(ffn):
                owner = jnp.bitwise_xor(me, r)
                here = slice((r * STEPS + step) * owned, (r * STEPS + step + 1) * owned)
                out[here, :] = natural[pl.ds(pl.multiple_of(owner * owned, owned), owned), :]

    return pl.pallas_call(
        kernel,
        name="order_rows",
        out_shape=jax.ShapeDtypeStruct((rows, depth), BF16),
        in_specs=[VMEM] * 3,
        out_specs=VMEM,
        scratch_shapes=[pltpu.VMEM((rows, depth), BF16), pltpu.VMEM((requests, depth), BF16)],
        compiler_params=limit(4),
    )(slot_row, same, other)


def multiply(rows, w, name):
    columns = w.shape[1]
    half = columns // 2
    count, depth = rows.shape
    ffn = lax.axis_size("ffn")
    share = count // ffn
    rest = (ffn // 2 - 1) * share
    block = min(512, half)

    def kernel(rows, w, own, near, keep, far, *ahead):
        for at in range(0, columns, block):
            here = slice(at, at + block)
            product = dot(rows[...], w[:, here])
            own[:, here] = product[:share]
            near[:, here] = product[share : 2 * share].astype(BF16)
            for r in range(2, ffn):
                part = product[r * share : (r + 1) * share]
                if at < half:
                    ahead[r - 2][:, here] = part.astype(BF16)
                else:
                    out = far if r % 2 else keep
                    place = slice((r // 2 - 1) * share, r // 2 * share)
                    out[place, at - half : at - half + block] = part.astype(out.dtype)

    return pl.pallas_call(
        kernel,
        name=name,
        out_shape=[
            jax.ShapeDtypeStruct((share, columns), F32),
            jax.ShapeDtypeStruct((share, columns), BF16),
            jax.ShapeDtypeStruct((rest, half), F32),
            jax.ShapeDtypeStruct((rest, half), BF16),
        ]
        + [jax.ShapeDtypeStruct((share, half), BF16)] * (ffn - 2),
        in_specs=[VMEM] * 2,
        out_specs=[VMEM] * (ffn + 2),
        compiler_params=limit(4),
        cost_estimate=matmul_cost(count, depth, columns),
    )(rows, vmem(w))


def multiply_direct(rows, w, name):
    columns = w.shape[1]
    count, depth = rows.shape
    ffn = lax.axis_size("ffn")
    share = count // ffn
    block = min(512, columns)

    def kernel(rows, w, *outs):
        for j in range(columns // block):
            here = slice(j * block, (j + 1) * block)
            product = dot(rows[...], w[:, here])
            for r, out in enumerate(outs):
                out[:, here] = product[r * share : (r + 1) * share].astype(out.dtype)

    return pl.pallas_call(
        kernel,
        name=name,
        out_shape=[
            jax.ShapeDtypeStruct((share, columns), BF16 if r else F32) for r in range(ffn)
        ],
        in_specs=[VMEM] * 2,
        out_specs=[VMEM] * ffn,
        compiler_params=limit(4),
        cost_estimate=matmul_cost(count, depth, columns),
    )(rows, vmem(w))


def add_parts(keep, arrived, parts, first=BF16):
    rows, width = keep.shape
    share = rows // parts
    types = [first] + [BF16] * (parts - 1)

    def kernel(keep, arrived, *outs):
        for d, out in enumerate(outs):
            here = slice(d * share, (d + 1) * share)
            out[...] = (keep[here, :].astype(F32) + arrived[here, :].astype(F32)).astype(out.dtype)

    return pl.pallas_call(
        kernel,
        name="add_parts",
        out_shape=[jax.ShapeDtypeStruct((share, width), kind) for kind in types],
        in_specs=[VMEM] * 2,
        out_specs=[VMEM] * parts,
        compiler_params=limit(4),
    )(keep, arrived)


def add_residual(own, terms):
    rows, columns = terms[0].shape
    owned, half = rows // STEPS, columns // 2

    def kernel(own, *refs):
        terms, (whole, left, right) = refs[:-3], refs[-3:]
        for out, first in ((left, 0), (right, half)):
            total = add_terms(terms, slice(first, first + half))
            for step in range(STEPS):
                here = slice(step * owned, (step + 1) * owned)
                at = step * columns + first
                value = (own[:, at : at + half].astype(F32) + total[here]).astype(BF16)
                out[here, :] = value
                whole[here, first : first + half] = value

    return pl.pallas_call(
        kernel,
        name="add_residual",
        out_shape=[jax.ShapeDtypeStruct((rows, n), BF16) for n in (columns, half, half)],
        in_specs=[VMEM] * (1 + len(terms)),
        out_specs=[VMEM] * 3,
        compiler_params=limit(4),
    )(own, *terms)


def norm_rows(blocks, gain):
    places = [(mask, first) for mask, first, _ in blocks]
    flat = [block for _, _, block in blocks]
    size, depth = flat[-1].shape
    rows = size * lax.axis_size("ffn")
    att = lax.axis_size("att")
    chips = att // 2
    share = rows // att

    def kernel(*refs):
        blocks, (gain, normed, tail, residual) = refs[: len(flat)], refs[len(flat) :]
        for (mask, first), block in zip(places, blocks):
            here = slice(first, first + block.shape[1])
            residual[mask * size : (mask + 1) * size, here] = block[...]
        me = lax.axis_index("att")
        chip, core = me // 2, lax.rem(me, 2)
        for side in range(2):
            for d in range(chips):
                owner = lax.rem(chip + d, chips) * 2 + lax.rem(core + side, 2)
                part = residual[pl.ds(pl.multiple_of(owner * share, share), share), :].astype(F32)
                here = slice((side * chips + d) * share, (side * chips + d + 1) * share)
                normed[here, :] = (part * gain[...]).astype(BF16)
                squares = jnp.sum(part * part, axis=1, keepdims=True)
                high = squares.astype(BF16).astype(F32)
                lane = lax.broadcasted_iota(jnp.int32, (share, HD), 1)
                tail[here, :] = jnp.where(lane == 0, high, squares - high).astype(BF16)

    return pl.pallas_call(
        kernel,
        name="norm_rows",
        out_shape=[
            jax.ShapeDtypeStruct((rows, depth), BF16),
            jax.ShapeDtypeStruct((rows, HD), BF16),
        ],
        in_specs=[VMEM] * (len(flat) + 1),
        out_specs=[VMEM] * 2,
        scratch_shapes=[pltpu.VMEM((rows, depth), BF16)],
        compiler_params=limit(4),
    )(*flat, gain)


def widen(normed, tail, w_gate, w_up, first, count, after):
    rows, depth = normed.shape
    half = rows // 2
    width = count * 2 * BLOCK + HD

    def kernel(normed, tail, gate, up, *refs):
        keep, send = refs[-2:]
        keep[:, count * 2 * BLOCK :] = tail[:half, :]
        send[:, count * 2 * BLOCK :] = tail[half:, :]
        for j in range(count):
            for which, w in enumerate((gate, up)):
                at = (first + j) * BLOCK
                product = dot(normed[...], w[:, at : at + BLOCK])
                here = slice((2 * j + which) * BLOCK, (2 * j + which + 1) * BLOCK)
                keep[:, here] = product[:half].astype(BF16)
                send[:, here] = product[half:].astype(BF16)

    return pl.pallas_call(
        kernel,
        name="widen",
        out_shape=[jax.ShapeDtypeStruct((half, width), BF16)] * 2,
        in_specs=[VMEM] * (4 + len(after)),
        out_specs=[VMEM] * 2,
        compiler_params=limit(4),
        cost_estimate=matmul_cost(rows, depth, count * 2 * BLOCK),
    )(normed, tail, vmem(w_gate), vmem(w_up), *after)


def gate_rows(own, moved, model):
    share, width = own.shape
    count = width // (2 * BLOCK)
    others = len(moved)

    def kernel(*refs):
        own, moved, out = refs[0], refs[1 : 1 + others], refs[-1]

        def total(here):
            value = own[:, here]
            for part in moved:
                value = value + part[:, here].astype(F32)
            return value

        tail = total(slice(count * 2 * BLOCK, count * 2 * BLOCK + HD))
        factor = lax.rsqrt((tail[:, 0:1] + tail[:, 1:2]) / model + EPSILON)
        for j in range(count):
            gate = total(slice(2 * j * BLOCK, (2 * j + 1) * BLOCK)) * factor
            up = total(slice((2 * j + 1) * BLOCK, (2 * j + 2) * BLOCK)) * factor
            out[:, j * BLOCK : (j + 1) * BLOCK] = (gate / (1.0 + jnp.exp(-gate)) * up).astype(BF16)

    return pl.pallas_call(
        kernel,
        name="gate",
        out_shape=jax.ShapeDtypeStruct((share, count * BLOCK), BF16),
        in_specs=[VMEM] * (1 + others),
        out_specs=VMEM,
        compiler_params=limit(4),
        cost_estimate=pl.CostEstimate(flops=WAIT, bytes_accessed=0, transcendentals=0),
    )(own, *moved)


def place_rows(chunks):
    sizes = [same.shape[1] for same, _ in chunks]
    rows = 2 * chunks[0][0].shape[0]

    def kernel(*refs):
        out, at = refs[-1], 0
        for k, size in enumerate(sizes):
            place_gathered(refs[2 * k], refs[2 * k + 1], out, slice(at, at + size))
            at += size

    return pl.pallas_call(
        kernel,
        name="place_rows",
        out_shape=jax.ShapeDtypeStruct((rows, sum(sizes)), BF16),
        in_specs=[VMEM] * (2 * len(sizes)),
        out_specs=VMEM,
        compiler_params=limit(4),
    )(*[x for pair in chunks for x in pair])


def finish(residual, terms):
    def kernel(residual, *refs):
        total = refs[0][...]
        for term in refs[1:-1]:
            total = total + term[...].astype(F32)
        refs[-1][...] = (residual[...].astype(F32) + total).astype(BF16)

    return pl.pallas_call(
        kernel,
        name="finish",
        out_shape=jax.ShapeDtypeStruct(residual.shape, BF16),
        in_specs=[VMEM] * (1 + len(terms)),
        out_specs=VMEM,
        compiler_params=limit(4),
    )(residual, *terms)


def local(
    incoming, queries, new_kv, cache, lengths, slot_of, w_out, norm_gain, w_gate, w_up, w_down
):
    ffn = lax.axis_size("ffn")
    att = lax.axis_size("att")
    requests = slot_of.shape[0]
    slots = cache.shape[0]
    model = w_out.shape[1]
    width = w_gate.shape[1]
    owned = requests // ffn

    whole = lambda x: (x, x.shape[0])
    queries, new_kv, token = load([whole(queries), whole(new_kv)], "load_new")
    qkv = jnp.concatenate([queries.reshape(slots, -1), new_kv.reshape(slots, -1)], axis=1)
    small = [whole(slot_of.reshape(1, requests)), whole(lengths.reshape(1, slots))]
    cache, slot_row, lengths, own, token = load(
        [whole(cache)] + small + [(incoming, owned)], "load_cache", [corner(qkv)]
    )
    own = own.reshape(owned, STEPS * model)
    same, other = gather_att(qkv, [token])
    attended = attend(lengths, slot_row, same, other, cache)
    w_out, token = load([whole(w_out)], "load_out", [corner(attended)])
    rows = order_rows(slot_row, *gather_att(attended, [token]))
    sums = reduce_ffn(*multiply(rows, w_out, "project"))

    residual, left, right = add_residual(own, sums)
    normed, tail = norm_rows(gather_ffn(residual, left, right), norm_gain.reshape(1, model))
    blocks, whole_of = width // BLOCK, sum(CHUNKS)
    edges = [blocks * sum(CHUNKS[:k]) // whole_of for k in range(len(CHUNKS) + 1)]
    pairs = []
    for k, (first, last) in enumerate(zip(edges[:-1], edges[1:])):
        after = [corner(keep)] if k == 1 else [corner(pairs[k - 2][1])] if k else []
        keep, send = widen(normed, tail, w_gate, w_up, first, last - first, after)
        pairs.append(add_parts(keep, exchange(send, "att", 1), att // 2, F32))
    moved = [
        [shift(part, "att", 2 * (d + 1)) for d, part in enumerate(away)] for _, *away in pairs
    ]
    chunks = [
        gather_att(gate_rows(pair[0], parts, model * att))
        for pair, parts in zip(pairs, moved)
    ]
    hidden = place_rows(chunks)
    out = finish(residual, reduce_direct(*multiply_direct(hidden, w_down, "narrow")))
    return jnp.swapaxes(out.reshape(STEPS, owned, model), 0, 1)


def solution(mesh):
    return jax.shard_map(
        local,
        mesh=mesh,
        in_specs=(
            P("parts", None, "att"),
            P(("parts", "att"), None, "ffn"),
            P(("parts", "att"), None, "ffn"),
            P(("parts", "att"), None, "ffn"),
            P(("parts", "att")),
            P("parts"),
            P("ffn", "att"),
            P("att"),
            P("att", "ffn"),
            P("att", "ffn"),
            P("ffn", "att"),
        ),
        out_specs=P(("parts", "ffn"), None, "att"),
        check_vma=False,
    )
```
